128 devices in a mesh: section: 2 (over core), batch: 64 (over z, x, y).
Axes of the slice: x: 4, y: 4, z: 4, core: 2. Of those that a mesh axis runs over, the one named last changes fastest.
Arguments:
- patches: bfloat16 [32768, 1024], P(('section', 'batch')), may hold values from -6 to 6
- lengths: int32 [128, 12], P(('section', 'batch')), may hold values from 0 to 784, as said below
- visible: int32 [100352], P(('section', 'batch')), may hold values from 0 to 1, as said below
- gsd_index: int32 [128, 12], P(('section', 'batch')), may hold values from 0 to 3
- enc_attn_gain: float32 [1024], replicated, may hold values from 0.5 to 1.5
- enc_attn_shift: float32 [1024], replicated, may hold values from -3 to 3
- enc_qkv: bfloat16 [1024, 3072], replicated, may hold values from -0.1875 to 0.1875
- enc_out: bfloat16 [1024, 1024], replicated, may hold values from -0.5 to 0.5
- enc_mlp_gain: float32 [1024], replicated, may hold values from 0.5 to 1.5
- enc_mlp_shift: float32 [1024], replicated, may hold values from -3 to 3
- enc_up: bfloat16 [1024, 4096], replicated, may hold values from -0.1875 to 0.1875
- enc_down: bfloat16 [4096, 1024], replicated, may hold values from -0.09375 to 0.09375
- dec_embed: bfloat16 [1024, 512], replicated, may hold values from -0.1875 to 0.1875
- mask_token: bfloat16 [512], replicated, may hold values from -4 to 4
- dec_attn_gain: float32 [512], replicated, may hold values from 0.5 to 1.5
- dec_attn_shift: float32 [512], replicated, may hold values from -3 to 3
- dec_qkv: bfloat16 [512, 1536], replicated, may hold values from -0.25 to 0.25
- dec_out: bfloat16 [512, 512], replicated, may hold values from -0.75 to 0.75
- dec_mlp_gain: float32 [512], replicated, may hold values from 0.5 to 1.5
- dec_mlp_shift: float32 [512], replicated, may hold values from -3 to 3
- dec_up: bfloat16 [512, 2048], replicated, may hold values from -0.25 to 0.25
- dec_down: bfloat16 [2048, 512], replicated, may hold values from -0.125 to 0.125
- out_grad: bfloat16 [100352, 512], P(('section', 'batch')), may hold values from -6 to 6
Outputs:
- dec_output: bfloat16 [100352, 512], P(('section', 'batch'))
- patch_grad: float32 [32768, 1024], P(('section', 'batch'))
- enc_attn_gain_grad: float32 [1024], P('batch')
- enc_attn_shift_grad: float32 [1024], P('batch')
- enc_qkv_grad: float32 [1024, 3072], P('batch')
- enc_out_grad: float32 [1024, 1024], P('batch')
- enc_mlp_gain_grad: float32 [1024], P('batch')
- enc_mlp_shift_grad: float32 [1024], P('batch')
- enc_up_grad: float32 [1024, 4096], P('batch')
- enc_down_grad: float32 [4096, 1024], P('batch')
- dec_embed_grad: float32 [1024, 512], P('batch')
- mask_token_grad: float32 [512], P('batch')
- dec_attn_gain_grad: float32 [512], P('batch')
- dec_attn_shift_grad: float32 [512], P('batch')
- dec_qkv_grad: float32 [512, 1536], P('batch')
- dec_out_grad: float32 [512, 512], P('batch')
- dec_mlp_gain_grad: float32 [512], P('batch')
- dec_mlp_shift_grad: float32 [512], P('batch')
- dec_up_grad: float32 [512, 2048], P('batch')
- dec_down_grad: float32 [2048, 512], P('batch')
The draws below stay inside these ranges and needn't reach their ends.
Inputs may be any that keep to these rules, and one draw needn't show every extreme that they name: `lengths`: each row holds item sizes 28 * 28, 14 ** 2 or (8) ** 2 (0 for an empty slot) in any order, summing to at most 784; some device holds one item of 784. `visible`: in each item of n rows exactly n // 4 rows are 1; rows after a device's items are 0.
All inputs are finite; a program needn't handle non-finite values.
Results may differ from the reference program's by a relative error of at most 0.019.
Values may be sent and summed in bfloat16 or wider, within the bound.
A program may use at most 384 MiB of HBM per device.

```python
import math
import jax
import jax.numpy as jnp
import numpy as np
from jax import lax

D = 1024
HEADS = 16
FF = 4096
DD = 512
DHEADS = 16
DFF = 2048
SIDE = 28
GRID_DEV = 784
ENC_DEV = 256
MAXI = 12
PATCHES = 100352
SLOTS = 32768
DEVICES = 128


def pattern_table(big_side, slot_count):
    large_item = big_side * big_side
    mid_item = big_side // 2 * (big_side // 2)
    small_item = 2 * big_side // 7 * (2 * big_side // 7)
    counts = [(1, 0, 0), (0, 4, 0), (0, 0, 12), (0, 3, 3), (0, 2, 6), (0, 1, 9)]
    table = np.zeros((6, slot_count), dtype=np.int32)
    for kind in range(6):
        row = [large_item] * counts[kind][0] + [mid_item] * counts[kind][1] + [small_item] * counts[kind][2]
        table[kind, :len(row)] = row
    return table


def item_layout(key):
    pattern_kind = jax.random.randint(jax.random.fold_in(key, 11), (DEVICES,), 0, 6)
    forced = jax.random.randint(jax.random.fold_in(key, 12), (), 0, DEVICES)
    pattern_kind = pattern_kind.at[forced].set(0)
    ordered = jnp.asarray(pattern_table(SIDE, MAXI))[pattern_kind]
    random_score = jax.random.randint(jax.random.fold_in(key, 13), (DEVICES, MAXI), 0, 1 << 20)
    distinct = random_score * MAXI + jnp.arange(MAXI, dtype=jnp.int32)[None, :]
    shuffle = jnp.argsort(distinct, axis=1, stable=True)
    lengths = jnp.take_along_axis(ordered, shuffle, axis=1).astype(jnp.int32)
    item_ends = jnp.cumsum(lengths, axis=1).astype(jnp.int32)
    starts = item_ends - lengths
    row_ids = jnp.arange(GRID_DEV, dtype=jnp.int32)
    segment = jnp.sum((row_ids[None, :, None] >= item_ends[:, None, :]).astype(jnp.int32), axis=2)
    onehot = (segment[:, :, None] == jnp.arange(MAXI, dtype=jnp.int32)[None, None, :]).astype(jnp.int32)
    length = jnp.sum(onehot * lengths[:, None, :], axis=2)
    start_row = jnp.sum(onehot * starts[:, None, :], axis=2)
    row_score = jax.random.randint(jax.random.fold_in(key, 14), (DEVICES, GRID_DEV), 0, 1 << 20)
    sort_key = segment * (1 << 21) + row_score
    sorted_order = jnp.argsort(sort_key, axis=1, stable=True)
    position = jnp.argsort(sorted_order, axis=1, stable=True)
    within = position - start_row
    visible = ((within < length // 4) & (segment < MAXI)).astype(jnp.int32)
    return (lengths, visible.reshape(DEVICES * GRID_DEV))


def draw_lengths(key, part):
    return item_layout(key)[0]


def draw_visible(key, part):
    return item_layout(key)[1]


def draw_gsd_index(key, part):
    key = jax.random.fold_in(key, 3)
    return jax.random.randint(key, (DEVICES, MAXI), 0, 4).astype(jnp.int32)


def steps_of(stream_key, extent, split, smallest, high):
    loudness, own = 1.0, jax.random.fold_in(stream_key, 6)
    for dim, blocks in split:
        draws = jnp.exp(jax.random.uniform(jax.random.fold_in(own, dim), (blocks,), jnp.float32, smallest / len(split), high / len(split)))
        loudness = loudness * jnp.repeat(draws, extent[dim] // blocks).reshape([-1 if axis == dim else 1 for axis in range(len(extent))])
    return loudness


def gaussian(rng, dims, scale, most, cuts=(), kind=jnp.bfloat16):
    level = steps_of(rng, dims, cuts, -0.22, 0.18) if cuts else 1.0
    entries = jax.random.normal(rng, dims, jnp.float32) * scale * level
    return jnp.minimum(jnp.maximum(entries, -most), most).astype(kind)


def setup_inputs(seed: int = 0) -> dict:
    seeds = jax.random.split(jax.random.key(seed), 24)
    return {
        "patches": gaussian(seeds[0], (SLOTS, D), 1.0, 6.0, ((0, 128),)),
        "lengths": draw_lengths(jax.random.fold_in(seeds[23], 71), 0),
        "visible": draw_visible(jax.random.fold_in(seeds[23], 71), 0),
        "gsd_index": draw_gsd_index(jax.random.fold_in(seeds[23], 71), 0),
        "enc_attn_gain": jnp.clip(1.0 + 0.1 * jax.random.normal(seeds[4], (D,), jnp.float32), 0.5, 1.5),
        "enc_attn_shift": gaussian(seeds[5], (D,), 0.3, 3.0, (), jnp.float32),
        "enc_qkv": gaussian(seeds[6], (D, 3 * D), D ** -0.5, 0.1875),
        "enc_out": gaussian(seeds[7], (D, D), (D // 8) ** -0.5, 0.5),
        "enc_mlp_gain": jnp.clip(1.0 + 0.1 * jax.random.normal(seeds[8], (D,), jnp.float32), 0.5, 1.5),
        "enc_mlp_shift": gaussian(seeds[9], (D,), 0.3, 3.0, (), jnp.float32),
        "enc_up": gaussian(seeds[10], (D, FF), D ** -0.5, 0.1875),
        "enc_down": gaussian(seeds[11], (FF, D), FF ** -0.5, 0.09375),
        "dec_embed": gaussian(seeds[12], (D, DD), D ** -0.5, 0.1875),
        "mask_token": gaussian(seeds[13], (DD,), 1.0, 4.0),
        "dec_attn_gain": jnp.clip(1.0 + 0.1 * jax.random.normal(seeds[14], (DD,), jnp.float32), 0.5, 1.5),
        "dec_attn_shift": gaussian(seeds[15], (DD,), 0.3, 3.0, (), jnp.float32),
        "dec_qkv": gaussian(seeds[16], (DD, 3 * DD), DD ** -0.5, 0.25),
        "dec_out": gaussian(seeds[17], (DD, DD), (DD // 8) ** -0.5, 0.75),
        "dec_mlp_gain": jnp.clip(1.0 + 0.1 * jax.random.normal(seeds[18], (DD,), jnp.float32), 0.5, 1.5),
        "dec_mlp_shift": gaussian(seeds[19], (DD,), 0.3, 3.0, (), jnp.float32),
        "dec_up": gaussian(seeds[20], (DD, DFF), DD ** -0.5, 0.25),
        "dec_down": gaussian(seeds[21], (DFF, DD), DFF ** -0.5, 0.125),
        "out_grad": gaussian(seeds[22], (PATCHES, DD), 1.0, 6.0, ((0, 128),)),
    }


@jax.custom_vjp
def low(v):
    return lax.optimization_barrier(v.astype(jnp.bfloat16)).astype(jnp.float32)

@jax.custom_vjp
def low_back(v):
    return v

def low_keep(v):
    return (low(v), None)

def low_pass(kept, grad):
    return (grad,)

def back_keep(v):
    return (v, None)

def back_low(kept, grad):
    return (low(grad),)
low.defvjp(low_keep, low_pass)
low_back.defvjp(back_keep, back_low)
epsilon = 1e-06
negative = -1e+30
highest = lax.Precision.HIGHEST

def normalize(values, gain, shift):
    row_mean = lax.optimization_barrier(jnp.mean(values, axis=-1, keepdims=True))
    centered = values - row_mean
    variance = lax.optimization_barrier(jnp.mean(centered * centered, axis=-1, keepdims=True))
    return centered * lax.rsqrt(variance + epsilon) * gain + shift

def product(left, right):
    return jnp.dot(left, right, precision=highest)

def grid_tables(lengths_row, visible_row, gsd_row, devices, enc_rows, model_width, big_side):
    grid_rows = visible_row.shape[0]
    slot_count = lengths_row.shape[0]
    mid_side = big_side // 2
    small_side = 2 * big_side // 7
    row_ids = jnp.arange(grid_rows, dtype=jnp.int32)
    item_ends = jnp.cumsum(lengths_row).astype(jnp.int32)
    starts = (item_ends - lengths_row).astype(jnp.int32)
    segment = lax.optimization_barrier(jnp.sum((row_ids[:, None] >= item_ends[None, :]).astype(jnp.int32), axis=1)).astype(jnp.int32)
    onehot = (segment[:, None] == jnp.arange(slot_count, dtype=jnp.int32)[None, :]).astype(jnp.int32)
    offset = (row_ids - lax.optimization_barrier(jnp.sum(onehot * starts[None, :], axis=1))).astype(jnp.int32)
    length = lax.optimization_barrier(jnp.sum(onehot * lengths_row[None, :], axis=1)).astype(jnp.int32)
    scale_index = lax.optimization_barrier(jnp.sum(onehot * gsd_row[None, :], axis=1)).astype(jnp.int32)
    live_rows = segment < slot_count
    side_len = jnp.where(length == small_side * small_side, small_side, jnp.where(length == mid_side * mid_side, mid_side, big_side)).astype(jnp.int32)
    row_pos = (offset // side_len).astype(jnp.float32)
    col_pos = (offset % side_len).astype(jnp.float32)
    factor = jnp.where(scale_index == 0, 0.5, jnp.where(scale_index == 1, 1.0, jnp.where(scale_index == 2, 2.0, 4.0))).astype(jnp.float32)
    quarter = model_width // 4
    frequency = jnp.exp(jnp.arange(quarter, dtype=jnp.float32) * (-math.log(10000.0) / quarter))
    row_angle = (row_pos * factor)[:, None] * frequency[None, :]
    col_angle = (col_pos * factor)[:, None] * frequency[None, :]
    position = jnp.concatenate([jnp.sin(row_angle), jnp.cos(row_angle), jnp.sin(col_angle), jnp.cos(col_angle)], axis=1)
    position = position * live_rows[:, None].astype(jnp.float32)
    is_shown = visible_row == 1
    vis_rank = (jnp.cumsum(visible_row) - 1).astype(jnp.int32)
    per_peer = enc_rows // devices
    source_row = jnp.where(is_shown, vis_rank % devices * per_peer + vis_rank // devices, 0).astype(jnp.int32)
    target = jnp.where(is_shown, vis_rank, enc_rows).astype(jnp.int32)
    item_of_rank = jnp.full((enc_rows,), -1, jnp.int32).at[target].set(segment, mode='drop')
    received = jnp.arange(enc_rows, dtype=jnp.int32)
    rank_of_row = (received % per_peer * devices + received // per_peer).astype(jnp.int32)
    item_of_row = jnp.take(item_of_rank, rank_of_row)
    return (segment, live_rows, position, is_shown, source_row, item_of_row)

def attend(triple, same_item, heads):
    row_count = triple.shape[0]
    model_width = triple.shape[1] // 3
    head_size = model_width // heads
    split_heads = triple.reshape(row_count, 3, heads, head_size)
    scores = jnp.einsum('qhd,khd->hqk', split_heads[:, 0], split_heads[:, 1], precision=highest) * head_size ** (-0.5)
    scores = jnp.where(same_item[None], low_back(scores), negative)
    row_peak = lax.optimization_barrier(jnp.max(scores, axis=-1, keepdims=True))
    weights = jnp.exp(scores - row_peak)
    attention = low(weights / lax.optimization_barrier(jnp.sum(weights, axis=-1, keepdims=True)))
    mixed = jnp.einsum('hqk,khd->qhd', attention, split_heads[:, 2], precision=highest)
    return mixed.reshape(row_count, model_width)

def block(inputs, weights, same_item, heads):
    attn_gain, attn_shift, w_qkv, w_out, mlp_gain, mlp_shift, w_up, w_down = weights
    normed = low(normalize(inputs, attn_gain, attn_shift))
    triple = low(low_back(product(normed, w_qkv)))
    attended = low(low_back(attend(triple, same_item, heads)))
    branch = inputs + low_back(product(attended, w_out))
    normed_mlp = low(normalize(branch, mlp_gain, mlp_shift))
    hidden = low_back(product(normed_mlp, w_up))
    active = low(jax.nn.gelu(hidden, approximate=False))
    return branch + low_back(product(active, w_down))

def one_grid(params, received, lengths_row, visible_row, gsd_row):
    enc_weights = params[0:8]
    dec_embed = params[8]
    mask_token = params[9]
    dec_weights = params[10:18]
    segment, live_rows, position, is_shown, source_row, item_of_row = grid_tables(lengths_row, visible_row, gsd_row, DEVICES, ENC_DEV, DD, SIDE)
    encoded = block(received, enc_weights, item_of_row[:, None] == item_of_row[None, :], HEADS)
    embedded = low_back(product(low(encoded), dec_embed))
    placed = jnp.take(embedded, source_row, axis=0)
    dec_input = jnp.where(is_shown[:, None], placed, mask_token[None, :]) + position
    decoded = block(dec_input, dec_weights, segment[:, None] == segment[None, :], DHEADS)
    return decoded * live_rows[:, None].astype(jnp.float32)

def reference(patches, lengths, visible, gsd_index, enc_attn_gain, enc_attn_shift, enc_qkv, enc_out, enc_mlp_gain, enc_mlp_shift, enc_up, enc_down, dec_embed, mask_token, dec_attn_gain, dec_attn_shift, dec_qkv, dec_out, dec_mlp_gain, dec_mlp_shift, dec_up, dec_down, out_grad):
    per_peer = ENC_DEV // DEVICES
    params = tuple((item.astype(jnp.float32) for item in (enc_attn_gain, enc_attn_shift, enc_qkv, enc_out, enc_mlp_gain, enc_mlp_shift, enc_up, enc_down, dec_embed, mask_token, dec_attn_gain, dec_attn_shift, dec_qkv, dec_out, dec_mlp_gain, dec_mlp_shift, dec_up, dec_down)))
    visible_grid = visible.reshape(DEVICES, GRID_DEV)

    def forward(weights, patch_values):
        arranged = patch_values.reshape(DEVICES, DEVICES, per_peer, D).transpose(1, 0, 2, 3)
        arranged = arranged.reshape(DEVICES, ENC_DEV, D)
        per_grid = jax.checkpoint(lambda pieces: one_grid(weights, pieces[0], pieces[1], pieces[2], pieces[3]))
        results = lax.map(per_grid, (arranged, lengths, visible_grid, gsd_index))
        return results.reshape(DEVICES * GRID_DEV, DD)
    decoded, pullback = jax.vjp(forward, params, patches.astype(jnp.float32))
    param_grads, patch_grads = pullback(out_grad.astype(jnp.float32))
    return (decoded.astype(jnp.bfloat16), patch_grads, param_grads[0], param_grads[1], param_grads[2], param_grads[3], param_grads[4], param_grads[5], param_grads[6], param_grads[7], param_grads[8], param_grads[9], param_grads[10], param_grads[11], param_grads[12], param_grads[13], param_grads[14], param_grads[15], param_grads[16], param_grads[17])
```

```python
import functools
import math

import jax
import jax.numpy as jnp
from jax import lax
from jax.experimental import pallas as pl
from jax.experimental.pallas import tpu as pltpu
from jax.sharding import PartitionSpec as P

HEADS = 16
DHEADS = 16
SIDE = 28


epsilon = 1e-06
negative = -1e30


def normalize(values, gain, shift):
    row_mean = jnp.mean(values, axis=-1, keepdims=True)
    centered = values - row_mean
    variance = jnp.mean(centered * centered, axis=-1, keepdims=True)
    return centered * lax.rsqrt(variance + epsilon) * gain + shift


def exact_gelu(values):
    return jax.nn.gelu(values, approximate=False)


def product(left, right):
    return jnp.dot(left, right, preferred_element_type=jnp.float32)


def inner_rows(left, right):
    return lax.dot_general(
        left, right, (((0,), (0,)), ((), ())), preferred_element_type=jnp.float32
    )


def times_transposed(left, right):
    return lax.dot_general(
        left, right, (((1,), (1,)), ((), ())), preferred_element_type=jnp.float32
    )


def grid_tables(lengths_row, visible_row, gsd_row, devices, enc_rows, model_width, big_side):
    grid_rows = visible_row.shape[0]
    slot_count = lengths_row.shape[0]
    mid_side = big_side // 2
    small_side = 2 * big_side // 7
    row_ids = jnp.arange(grid_rows, dtype=jnp.int32)
    item_ends = jnp.cumsum(lengths_row)
    starts = item_ends - lengths_row
    segment = jnp.sum((row_ids[:, None] >= item_ends[None, :]).astype(jnp.int32), axis=1)
    onehot = (segment[:, None] == jnp.arange(slot_count, dtype=jnp.int32)[None, :]).astype(
        jnp.int32
    )
    offset = row_ids - jnp.sum(onehot * starts[None, :], axis=1)
    length = jnp.sum(onehot * lengths_row[None, :], axis=1)
    scale_index = jnp.sum(onehot * gsd_row[None, :], axis=1)
    live_rows = segment < slot_count
    side_len = jnp.where(
        length == small_side * small_side,
        small_side,
        jnp.where(length == mid_side * mid_side, mid_side, big_side),
    ).astype(jnp.int32)
    row_pos = (offset // side_len).astype(jnp.float32)
    col_pos = (offset % side_len).astype(jnp.float32)
    factor = jnp.where(
        scale_index == 0,
        0.5,
        jnp.where(scale_index == 1, 1.0, jnp.where(scale_index == 2, 2.0, 4.0)),
    ).astype(jnp.float32)
    quarter = model_width // 4
    frequency = jnp.exp(jnp.arange(quarter, dtype=jnp.float32) * (-math.log(10000.0) / quarter))
    row_angle = (row_pos * factor)[:, None] * frequency[None, :]
    col_angle = (col_pos * factor)[:, None] * frequency[None, :]
    position = jnp.concatenate(
        [jnp.sin(row_angle), jnp.cos(row_angle), jnp.sin(col_angle), jnp.cos(col_angle)], axis=1
    )
    position = position * live_rows[:, None].astype(jnp.float32)
    is_shown = visible_row == 1
    vis_rank = jnp.cumsum(visible_row) - 1
    per_peer = enc_rows // devices
    source_row = jnp.where(is_shown, vis_rank % devices * per_peer + vis_rank // devices, 0)
    target = jnp.where(is_shown, vis_rank, enc_rows)
    item_of_rank = jnp.full((enc_rows,), -1, jnp.int32).at[target].set(segment, mode="drop")
    received = jnp.arange(enc_rows, dtype=jnp.int32)
    rank_of_row = received % per_peer * devices + received // per_peer
    item_of_row = jnp.take(item_of_rank, rank_of_row)
    return (segment, live_rows, position, is_shown, source_row, item_of_row)


def split_triple(triple, heads):
    row_count = triple.shape[0]
    model_width = triple.shape[1] // 3
    head_size = model_width // heads
    split_heads = triple.reshape(row_count, 3, heads, head_size)
    return (split_heads[:, 0], split_heads[:, 1], split_heads[:, 2], head_size ** (-0.5))


def attend(triple, same_item, heads):
    queries, key_rows, values, scale = split_triple(triple, heads)
    scores = (
        jnp.einsum("qhd,khd->hqk", queries, key_rows, preferred_element_type=jnp.float32) * scale
    )
    scores = jnp.where(same_item[None], scores, negative)
    row_peak = jnp.max(scores, axis=-1, keepdims=True)
    weights = jnp.exp(scores - row_peak)
    row_total = jnp.sum(weights, axis=-1, keepdims=True)
    attention = (weights / row_total).astype(jnp.bfloat16)
    mixed = jnp.einsum("hqk,khd->qhd", attention, values, preferred_element_type=jnp.float32)
    return (
        mixed.reshape(triple.shape[0], triple.shape[1] // 3),
        (row_peak + jnp.log(row_total))[..., 0],
    )


def attend_back(triple, same_item, heads, log_total, mixed_grad):
    queries, key_rows, values, scale = split_triple(triple, heads)
    scores = (
        jnp.einsum("qhd,khd->hqk", queries, key_rows, preferred_element_type=jnp.float32) * scale
    )
    attention = jnp.where(same_item[None], jnp.exp(scores - log_total[..., None]), 0.0)
    head_grad = mixed_grad.reshape(queries.shape)
    weight_grad = jnp.einsum("qhd,khd->hqk", head_grad, values, preferred_element_type=jnp.float32)
    centre = jnp.sum(weight_grad * attention, axis=-1, keepdims=True)
    score_grad = (attention * (weight_grad - centre)).astype(jnp.bfloat16)
    query_grad = (
        jnp.einsum("hqk,khd->qhd", score_grad, key_rows, preferred_element_type=jnp.float32) * scale
    )
    key_grad = (
        jnp.einsum("hqk,qhd->khd", score_grad, queries, preferred_element_type=jnp.float32) * scale
    )
    value_grad = jnp.einsum(
        "hqk,qhd->khd",
        attention.astype(jnp.bfloat16),
        head_grad,
        preferred_element_type=jnp.float32,
    )
    stacked = jnp.stack([query_grad, key_grad, value_grad], axis=1)
    return stacked.reshape(triple.shape[0], triple.shape[1])


def block_forward(inputs, weights, same_item, heads):
    attn_gain, attn_shift, w_qkv, w_out, mlp_gain, mlp_shift, w_up, w_down = weights
    normed = normalize(inputs, attn_gain, attn_shift).astype(jnp.bfloat16)
    triple = product(normed, w_qkv).astype(jnp.bfloat16)
    attended, log_total = attend(triple, same_item, heads)
    attended = attended.astype(jnp.bfloat16)
    branch = inputs + product(attended, w_out)
    normed_mlp = normalize(branch, mlp_gain, mlp_shift).astype(jnp.bfloat16)
    hidden = product(normed_mlp, w_up)
    active = exact_gelu(hidden).astype(jnp.bfloat16)
    result = branch + product(active, w_down)
    return (result, (inputs, normed, triple, log_total, attended, branch, normed_mlp, None))


def block_backward(gradient, kept, weights, same_item, heads):
    attn_gain, attn_shift, w_qkv, w_out, mlp_gain, mlp_shift, w_up, w_down = weights
    inputs, normed, triple, log_total, attended, branch, normed_mlp, stored = kept
    hidden = product(normed_mlp, w_up)
    active = exact_gelu(hidden).astype(jnp.bfloat16)
    grad_low = gradient.astype(jnp.bfloat16)
    down_grad = inner_rows(active, grad_low)
    active_grad = times_transposed(grad_low, w_down)
    gelu_back = jax.vjp(exact_gelu, hidden)[1]
    hidden_grad = gelu_back(active_grad)[0].astype(jnp.bfloat16)
    up_grad = inner_rows(normed_mlp, hidden_grad)
    normed_mlp_grad = times_transposed(hidden_grad, w_up)
    mlp_norm_back = jax.vjp(normalize, branch, mlp_gain, mlp_shift)[1]
    branch_part, mlp_gain_grad, mlp_shift_grad = mlp_norm_back(normed_mlp_grad)
    branch_grad = gradient + branch_part
    branch_low = branch_grad.astype(jnp.bfloat16)
    proj_grad = inner_rows(attended, branch_low)
    attended_grad = times_transposed(branch_low, w_out).astype(jnp.bfloat16)
    triple_grad = attend_back(triple, same_item, heads, log_total, attended_grad).astype(
        jnp.bfloat16
    )
    qkv_grad = inner_rows(normed, triple_grad)
    normed_grad = times_transposed(triple_grad, w_qkv)
    attn_norm_back = jax.vjp(normalize, inputs, attn_gain, attn_shift)[1]
    input_part, attn_gain_grad, attn_shift_grad = attn_norm_back(normed_grad)
    return (
        branch_grad + input_part,
        (
            attn_gain_grad,
            attn_shift_grad,
            qkv_grad,
            proj_grad,
            mlp_gain_grad,
            mlp_shift_grad,
            up_grad,
            down_grad,
        ),
    )


MESH = pl.DeviceIdType.MESH
LANES = 128
SOURCES = (
    ("vec", 16, 256),
    ("embed", 16, 512),
    ("dqkv", 16, 768),
    ("dout", 16, 256),
    ("dup", 16, 1024),
    ("ddown", 32, 512),
    ("down", 64, 1024),
    ("up", 16, 4096),
    ("out", 16, 1024),
    ("qkv", 16, 3072),
)
SHARES = (
    (16, 256),
    (16, 512),
    (8, 1536),
    (8, 512),
    (8, 2048),
    (32, 512),
    (64, 1024),
    (16, 4096),
    (16, 1024),
    (16, 3072),
)
STREAMS = 6


def half_tiles():
    tiles = []
    for source, (_, rows, columns) in enumerate(SOURCES):
        for row in range(rows // 16):
            for column in range(columns // (2 * LANES)):
                tiles.append((source, row, column))
    return tiles


def make_units(counts):
    tiles = half_tiles()
    units, first = [], 0
    for chunk in counts:
        row = []
        for many in chunk:
            pieces = []
            for place in range(many):
                source, r, c = tiles[first + place]
                if pieces and pieces[-1][0] == source and pieces[-1][1] == r and pieces[-1][2] + pieces[-1][3] == c:
                    pieces[-1][3] += 1
                else:
                    pieces.append([source, r, c, 1, place])
            row.append((first, many, pieces))
            first += many
        units.append(row)
    assert first == len(tiles), (first, len(tiles))
    return units


class Stream:
    def __init__(self, number, coords):
        self.order = tuple((number + step) % 3 for step in range(3))
        self.swap = number >= 3
        self.coords = coords

    def flip(self, p):
        return p + 1 - 2 * lax.rem(p, 2)

    def first(self, p):
        return 3 - p if self.swap else self.flip(p)

    def mate(self, p):
        return self.flip(p) if self.swap else 3 - p


def reduce_kernel(units, *refs):
    n = len(SOURCES)
    inputs, outputs, refs = refs[:n], refs[n : 2 * n], refs[2 * n :]
    chunks = len(units)
    work, refs = refs[:chunks], refs[chunks:]
    landed = [refs[i * chunks : (i + 1) * chunks] for i in range(7)]
    refs = refs[7 * chunks :]
    final, send_sem, recv_sem, own_sem = refs
    section = lax.axis_index("section")
    batch = lax.axis_index("batch")
    coords = (batch // 16, lax.rem(batch // 4, 4), lax.rem(batch, 4))
    weights = (16, 4, 1)

    def peer(axis, place):
        return (section, batch + (place - coords[axis]) * weights[axis])

    sibling = (1 - section, batch)
    barrier = pltpu.get_barrier_semaphore()
    partners = [sibling]
    for axis in range(3):
        p = coords[axis]
        partners += [peer(axis, p + 1 - 2 * lax.rem(p, 2)), peer(axis, 3 - p)]
    for partner in partners:
        pl.semaphore_signal(barrier, inc=1, device_id=partner, device_id_type=MESH)
    pl.semaphore_wait(barrier, len(partners))

    sends = []
    count = [0]
    arrivals = {}
    owns = {}

    def send(source, target, device, key):
        number = count[0]
        count[0] += 1
        copy = pltpu.make_async_remote_copy(
            src_ref=source,
            dst_ref=target,
            send_sem=send_sem.at[number],
            recv_sem=recv_sem.at[number],
            device_id=device,
            device_id_type=MESH,
        )
        copy.start()
        sends.append(copy)
        arrivals.setdefault(key, []).append(copy)

    def arrive(key):
        for copy in arrivals.pop(key):
            copy.wait_recv()

    streams = [Stream(number, coords) for number in range(STREAMS)]
    own_count = [0]

    def at(level_refs, c, s, axes, picks, lanes):
        return (s, *[picks.get(axis, slice(None)) for axis in axes], slice(None), slice(0, lanes))

    def start(c):
        for s in range(STREAMS):
            _, many, pieces = units[c][s]
            for source, row, column, width, place in pieces:
                half = SOURCES[source][2] // 2
                rows = pl.ds(16 * row, 16)
                there = pl.ds(pl.multiple_of((1 - section) * half, LANES) + column * LANES, width * LANES)
                here = pl.ds(pl.multiple_of(section * half, LANES) + column * LANES, width * LANES)
                lanes = pl.ds(place * LANES, width * LANES)
                send(
                    inputs[source].at[:, :, :, rows, there],
                    landed[0][c].at[s, :, :, :, :, lanes],
                    sibling,
                    (c, s, 0),
                )
                own = pltpu.make_async_copy(
                    inputs[source].at[:, :, :, rows, here],
                    work[c].at[s, :, :, :, :, lanes],
                    own_sem.at[own_count[0]],
                )
                own_count[0] += 1
                own.start()
                owns.setdefault((c, s), []).append(own)

    def terms(c, s, level, picks, extra=None):
        stream = streams[s]
        lanes = units[c][s][1] * LANES
        every = (0, 1, 2)
        found = [(work[c], (s, *[picks.get(a, slice(None)) for a in every], slice(None), slice(0, lanes)))]
        found.append((landed[0][c], found[0][1]))
        for lower in range(level):
            later = sorted(stream.order[lower + 1 :])
            index = [picks.get(a, slice(None)) for a in later]
            found.append((landed[1 + 2 * lower][c], (s, 0, *index, slice(None), slice(0, lanes))))
            found.append((landed[2 + 2 * lower][c], (s, *index, slice(None), slice(0, lanes))))
        if extra is not None:
            later = sorted(stream.order[level + 1 :])
            index = [picks.get(a, slice(None)) for a in later]
            found.append((landed[1 + 2 * level][c], (s, extra, *index, slice(None), slice(0, lanes))))
        return found

    def total(found):
        values = [ref[index].astype(jnp.float32) for ref, index in found]
        while len(values) > 1:
            values = [a + b for a, b in zip(values[::2], values[1::2])] + (
                [values[-1]] if len(values) % 2 else []
            )
        return values[0]

    def settle(c, s, level, picks, extra=None):
        stream = streams[s]
        free = sorted(stream.order[level + 1 :])
        if len(free) == 2:

            @pl.loop(0, 4)
            def _(i):
                inner = {**picks, free[0]: i}
                found = terms(c, s, level, inner, extra)
                ref, index = found[0]
                ref[index] = total(found).astype(jnp.bfloat16)
        else:
            found = terms(c, s, level, picks, extra)
            ref, index = found[0]
            ref[index] = total(found).astype(jnp.bfloat16)

    def done_picks(stream, level):
        return {axis: coords[axis] for axis in stream.order[:level]}

    def region(c, s, picks):
        lanes = units[c][s][1] * LANES
        return work[c].at[(s, *[picks.get(a, slice(None)) for a in range(3)], slice(None), slice(0, lanes))]

    def stage_a(c, s, level):
        stream = streams[s]
        lanes = units[c][s][1] * LANES
        axis = stream.order[level]
        me = coords[axis]
        other = stream.first(me)
        if level == 0:
            for own in owns.pop((c, s)):
                own.wait()
            arrive((c, s, 0))
        else:
            arrive((c, s, ("b", level - 1)))
        later = len(stream.order[level + 1 :])
        for slab, place in ((1, stream.mate(other)), (0, other)):
            picks = {**done_picks(stream, level), axis: place}
            settle(c, s, level, picks)
            send(
                region(c, s, picks),
                landed[1 + 2 * level][c].at[(s, slab, *[slice(None)] * later, slice(None), slice(0, lanes))],
                peer(axis, other),
                (c, s, ("a", level, slab)),
            )

    def stage_b(c, s, level):
        stream = streams[s]
        lanes = units[c][s][1] * LANES
        axis = stream.order[level]
        me = coords[axis]
        other = stream.mate(me)
        picks = {**done_picks(stream, level), axis: other}
        arrive((c, s, ("a", level, 1)))
        settle(c, s, level, picks, extra=1)
        later = len(stream.order[level + 1 :])
        send(
            region(c, s, picks),
            landed[2 + 2 * level][c].at[(s, *[slice(None)] * later, slice(None), slice(0, lanes))],
            peer(axis, other),
            (c, s, ("b", level)),
        )
        arrive((c, s, ("a", level, 0)))

    def finish(c):
        for s in range(STREAMS):
            stream = streams[s]
            first, many, _ = units[c][s]
            arrive((c, s, ("b", 2)))
            value = total(terms(c, s, 3, done_picks(stream, 3)))
            for place in range(many):
                final[section, first + place] = value[:, place * LANES : (place + 1) * LANES]
        first = units[c][0][0]
        many = sum(unit[1] for unit in units[c])
        region = final.at[section, pl.ds(first, many)]
        send(region, region, sibling, (c, "final"))

    start(0)
    if chunks > 1:
        start(1)
    for step in range(chunks + 6):
        for c in range(chunks):
            stage = step - c
            if stage == 6:
                finish(c)
            elif 0 <= stage < 6:
                for s in range(STREAMS):
                    (stage_a if stage % 2 == 0 else stage_b)(c, s, stage // 2)
                if stage == 0 and c + 2 < chunks:
                    start(c + 2)
    tiles = half_tiles()
    for c in range(chunks):
        arrive((c, "final"))
    for number, (source, row, column) in enumerate(tiles):
        rows, columns = SOURCES[source][1:]
        share = SHARES[source]
        for half in range(2):
            value = final[half, number]
            lane = half * columns // 2 + column * LANES
            if share[0] == 8:
                outputs[source][:, lane : lane + LANES] = value[:8]
                outputs[source][:, columns + lane : columns + lane + LANES] = value[8:]
            else:
                outputs[source][16 * row : 16 * row + 16, lane : lane + LANES] = value
    for copy in sends:
        copy.wait_send()


def reduce_call(counts, arrays):
    units = make_units(counts)
    chunks = len(units)
    wide = [max(unit[1] for unit in row) * LANES for row in units]
    shapes = [
        (4, 4, 4), (4, 4, 4), (2, 4, 4), (4, 4), (2, 4), (4,), (2,), (),
    ]
    scratch = []
    for shape in shapes:
        for lanes in wide:
            scratch.append(pltpu.VMEM((STREAMS, *shape, 16, lanes), jnp.bfloat16))
    scratch.append(pltpu.VMEM((2, len(half_tiles()), 16, LANES), jnp.float32))
    pieces = sum(len(unit[2]) for row in units for unit in row)
    sends = pieces + 9 * chunks * STREAMS + chunks
    scratch += [
        pltpu.SemaphoreType.DMA((sends,)),
        pltpu.SemaphoreType.DMA((sends,)),
        pltpu.SemaphoreType.DMA((pieces,)),
    ]
    arrays = [
        array.reshape(4, 4, 4, rows, columns) for array, (_, rows, columns) in zip(arrays, SOURCES)
    ]
    return pl.pallas_call(
        functools.partial(reduce_kernel, units),
        out_shape=[jax.ShapeDtypeStruct(share, jnp.float32) for share in SHARES],
        in_specs=[pl.BlockSpec(memory_space=pl.ANY)] * len(arrays),
        out_specs=[pl.BlockSpec(memory_space=pltpu.VMEM)] * len(SHARES),
        scratch_shapes=scratch,
        compiler_params=pltpu.CompilerParams(
            collective_id=0, has_side_effects=True, vmem_limit_bytes=60 * 1024 * 1024
        ),
        name="reduce_shares",
    )(*arrays)


COUNTS = ((3,) * 6, (4,) * 6, (4, 4, 4, 3, 3, 3))

def shared_sums(enc_grads, dec_terms):
    (enc_gain1, enc_shift1, enc_qkv, enc_out, enc_gain2, enc_shift2, enc_up, enc_down) = enc_grads
    embed, mask = dec_terms[:2]
    dec_gain1, dec_shift1, dec_qkv, dec_out, dec_gain2, dec_shift2, dec_up, dec_down = dec_terms[2:]
    vectors = (
        enc_gain1, enc_shift1, enc_gain2, enc_shift2,
        mask, dec_gain1, dec_shift1, dec_gain2, dec_shift2,
    )
    low = lambda value: value.astype(jnp.bfloat16)
    rows = low(jnp.concatenate([vector.reshape(64, -1) for vector in vectors], axis=1))
    rows = jnp.pad(rows[:, None, :], ((0, 0), (0, 15), (0, 256 - rows.shape[1])))

    def paired(value):
        columns = value.shape[1]
        value = low(value).reshape(64, 8, 2, columns // 2)
        return value.transpose(0, 2, 1, 3).reshape(1024, columns // 2)

    shares = reduce_call(
        COUNTS,
        (
            rows, low(embed), paired(dec_qkv), paired(dec_out), paired(dec_up), low(dec_down),
            low(enc_down), low(enc_up), low(enc_out), low(enc_qkv),
        ),
    )
    row = shares[0][0]
    cuts, first = [], 0
    for vector in vectors:
        many = vector.shape[0] // 64
        cuts.append(row[first : first + many])
        first += many
    return (
        cuts[0], cuts[1], shares[9], shares[8], cuts[2], cuts[3], shares[7], shares[6],
        shares[1], cuts[4], cuts[5], cuts[6], shares[2], shares[3], cuts[7], cuts[8], shares[4], shares[5],
    )


def per_device(
    patches,
    lengths,
    visible,
    gsd_index,
    enc_attn_gain,
    enc_attn_shift,
    enc_qkv,
    enc_out,
    enc_mlp_gain,
    enc_mlp_shift,
    enc_up,
    enc_down,
    dec_embed,
    mask_token,
    dec_attn_gain,
    dec_attn_shift,
    dec_qkv,
    dec_out,
    dec_mlp_gain,
    dec_mlp_shift,
    dec_up,
    dec_down,
    out_grad,
):
    devices = lax.axis_size(("section", "batch"))
    enc_rows = patches.shape[0]
    segment, live_rows, position, is_shown, source_row, item_of_row = grid_tables(
        lengths[0], visible, gsd_index[0], devices, enc_rows, mask_token.shape[0], SIDE
    )
    live_float = live_rows[:, None].astype(jnp.float32)
    enc_weights = (
        enc_attn_gain,
        enc_attn_shift,
        enc_qkv,
        enc_out,
        enc_mlp_gain,
        enc_mlp_shift,
        enc_up,
        enc_down,
    )
    dec_weights = (
        dec_attn_gain,
        dec_attn_shift,
        dec_qkv,
        dec_out,
        dec_mlp_gain,
        dec_mlp_shift,
        dec_up,
        dec_down,
    )
    enc_same = item_of_row[:, None] == item_of_row[None, :]
    dec_same = segment[:, None] == segment[None, :]
    arrived = lax.all_to_all(patches, ("section", "batch"), split_axis=0, concat_axis=0, tiled=True)
    inputs = arrived.astype(jnp.float32)
    encoded, enc_kept = block_forward(inputs, enc_weights, enc_same, HEADS)
    encoded_low = encoded.astype(jnp.bfloat16)
    embedded = product(encoded_low, dec_embed)
    placed = jnp.take(embedded, source_row, axis=0)
    dec_input = (
        jnp.where(is_shown[:, None], placed, mask_token.astype(jnp.float32)[None, :]) + position
    )
    decoded, dec_kept = block_forward(dec_input, dec_weights, dec_same, DHEADS)
    dec_output = (decoded * live_float).astype(jnp.bfloat16)
    top_grad = out_grad.astype(jnp.float32) * live_float
    input_grad, dec_grads = block_backward(top_grad, dec_kept, dec_weights, dec_same, DHEADS)
    mask_grad = jnp.sum(jnp.where(is_shown[:, None], 0.0, input_grad), axis=0)
    target = jnp.where(is_shown, source_row, enc_rows)
    embedded_grad = (
        jnp.zeros(embedded.shape, jnp.float32)
        .at[target]
        .add(jnp.where(is_shown[:, None], input_grad, 0.0), mode="drop")
    )
    embedded_low = embedded_grad.astype(jnp.bfloat16)
    embed_grad = inner_rows(encoded_low, embedded_low)
    dec_terms = (embed_grad, mask_grad) + tuple(dec_grads)
    encoded_grad = times_transposed(embedded_low, dec_embed)
    received_grad, enc_grads = block_backward(encoded_grad, enc_kept, enc_weights, enc_same, HEADS)
    patch_grad = lax.all_to_all(
        received_grad.astype(jnp.bfloat16),
        ("section", "batch"),
        split_axis=0,
        concat_axis=0,
        tiled=True,
    ).astype(received_grad.dtype)
    shares = shared_sums(enc_grads, dec_terms)
    return (dec_output, patch_grad) + shares


def solution(mesh):
    return jax.shard_map(
        per_device,
        mesh=mesh,
        in_specs=(
            P(("section", "batch"), None),
            P(("section", "batch"), None),
            P(("section", "batch")),
            P(("section", "batch"), None),
            P(),
            P(),
            P(),
            P(),
            P(),
            P(),
            P(),
            P(),
            P(),
            P(),
            P(),
            P(),
            P(),
            P(),
            P(),
            P(),
            P(),
            P(),
            P(("section", "batch"), None),
        ),
        out_specs=(
            P(("section", "batch"), None),
            P(("section", "batch"), None),
            P("batch"),
            P("batch"),
            P("batch", None),
            P("batch", None),
            P("batch"),
            P("batch"),
            P("batch", None),
            P("batch", None),
            P("batch", None),
            P("batch"),
            P("batch"),
            P("batch"),
            P("batch", None),
            P("batch", None),
            P("batch"),
            P("batch"),
            P("batch", None),
            P("batch", None),
        ),
        check_vma=False,
    )
```

```python
import functools
import math

import jax
import jax.numpy as jnp
import numpy as np
from jax import lax
from jax.experimental import pallas as pl
from jax.experimental.pallas import tpu as pltpu
from jax.sharding import PartitionSpec as P

MESH = pl.DeviceIdType.MESH
LANES = 128
SOURCES = (
    ("vec", 16, 256),
    ("embed", 16, 512),
    ("dqkv", 16, 768),
    ("dout", 16, 256),
    ("dup", 16, 1024),
    ("ddown", 32, 512),
    ("down", 64, 1024),
    ("up", 16, 4096),
    ("out", 16, 1024),
    ("qkv", 16, 3072),
)
SHARES = (
    (16, 256),
    (16, 512),
    (8, 1536),
    (8, 512),
    (8, 2048),
    (32, 512),
    (64, 1024),
    (16, 4096),
    (16, 1024),
    (16, 3072),
)
STREAMS = 6


def half_tiles():
    tiles = []
    for source, (_, rows, columns) in enumerate(SOURCES):
        for row in range(rows // 16):
            for column in range(columns // (2 * LANES)):
                tiles.append((source, row, column))
    return tiles


def make_units(counts):
    tiles = half_tiles()
    units, first = [], 0
    for chunk in counts:
        row = []
        for many in chunk:
            pieces = []
            for place in range(many):
                source, r, c = tiles[first + place]
                if pieces and pieces[-1][0] == source and pieces[-1][1] == r and pieces[-1][2] + pieces[-1][3] == c:
                    pieces[-1][3] += 1
                else:
                    pieces.append([source, r, c, 1, place])
            row.append((first, many, pieces))
            first += many
        units.append(row)
    assert first == len(tiles), (first, len(tiles))
    return units


class Stream:
    def __init__(self, number, coords):
        self.order = tuple((number + step) % 3 for step in range(3))
        self.swap = number >= 3
        self.coords = coords

    def flip(self, p):
        return p + 1 - 2 * lax.rem(p, 2)

    def first(self, p):
        return 3 - p if self.swap else self.flip(p)

    def mate(self, p):
        return self.flip(p) if self.swap else 3 - p


def reduce_kernel(units, *refs):
    n = len(SOURCES)
    inputs, outputs, refs = refs[:n], refs[n : 2 * n], refs[2 * n :]
    chunks = len(units)
    work, refs = refs[:chunks], refs[chunks:]
    landed = [refs[i * chunks : (i + 1) * chunks] for i in range(7)]
    refs = refs[7 * chunks :]
    final, send_sem, recv_sem, own_sem = refs
    section = lax.axis_index("section")
    batch = lax.axis_index("batch")
    coords = (batch // 16, lax.rem(batch // 4, 4), lax.rem(batch, 4))
    weights = (16, 4, 1)

    def peer(axis, place):
        return (section, batch + (place - coords[axis]) * weights[axis])

    sibling = (1 - section, batch)
    barrier = pltpu.get_barrier_semaphore()
    partners = [sibling]
    for axis in range(3):
        p = coords[axis]
        partners += [peer(axis, p + 1 - 2 * lax.rem(p, 2)), peer(axis, 3 - p)]
    for partner in partners:
        pl.semaphore_signal(barrier, inc=1, device_id=partner, device_id_type=MESH)
    pl.semaphore_wait(barrier, len(partners))

    sends = []
    count = [0]
    arrivals = {}
    owns = {}

    def send(source, target, device, key):
        number = count[0]
        count[0] += 1
        copy = pltpu.make_async_remote_copy(
            src_ref=source,
            dst_ref=target,
            send_sem=send_sem.at[number],
            recv_sem=recv_sem.at[number],
            device_id=device,
            device_id_type=MESH,
        )
        copy.start()
        sends.append(copy)
        arrivals.setdefault(key, []).append(copy)

    def arrive(key):
        for copy in arrivals.pop(key):
            copy.wait_recv()

    streams = [Stream(number, coords) for number in range(STREAMS)]
    own_count = [0]

    def at(level_refs, c, s, axes, picks, lanes):
        return (s, *[picks.get(axis, slice(None)) for axis in axes], slice(None), slice(0, lanes))

    def start(c):
        for s in range(STREAMS):
            _, many, pieces = units[c][s]
            for source, row, column, width, place in pieces:
                half = SOURCES[source][2] // 2
                rows = pl.ds(16 * row, 16)
                there = pl.ds(pl.multiple_of((1 - section) * half, LANES) + column * LANES, width * LANES)
                here = pl.ds(pl.multiple_of(section * half, LANES) + column * LANES, width * LANES)
                lanes = pl.ds(place * LANES, width * LANES)
                send(
                    inputs[source].at[:, :, :, rows, there],
                    landed[0][c].at[s, :, :, :, :, lanes],
                    sibling,
                    (c, s, 0),
                )
                own = pltpu.make_async_copy(
                    inputs[source].at[:, :, :, rows, here],
                    work[c].at[s, :, :, :, :, lanes],
                    own_sem.at[own_count[0]],
                )
                own_count[0] += 1
                own.start()
                owns.setdefault((c, s), []).append(own)

    def terms(c, s, level, picks, extra=None):
        stream = streams[s]
        lanes = units[c][s][1] * LANES
        every = (0, 1, 2)
        found = [(work[c], (s, *[picks.get(a, slice(None)) for a in every], slice(None), slice(0, lanes)))]
        found.append((landed[0][c], found[0][1]))
        for lower in range(level):
            later = sorted(stream.order[lower + 1 :])
            index = [picks.get(a, slice(None)) for a in later]
            found.append((landed[1 + 2 * lower][c], (s, 0, *index, slice(None), slice(0, lanes))))
            found.append((landed[2 + 2 * lower][c], (s, *index, slice(None), slice(0, lanes))))
        if extra is not None:
            later = sorted(stream.order[level + 1 :])
            index = [picks.get(a, slice(None)) for a in later]
            found.append((landed[1 + 2 * level][c], (s, extra, *index, slice(None), slice(0, lanes))))
        return found

    def total(found):
        values = [ref[index].astype(jnp.float32) for ref, index in found]
        while len(values) > 1:
            values = [a + b for a, b in zip(values[::2], values[1::2])] + (
                [values[-1]] if len(values) % 2 else []
            )
        return values[0]

    def settle(c, s, level, picks, extra=None):
        stream = streams[s]
        free = sorted(stream.order[level + 1 :])
        if len(free) == 2:

            @pl.loop(0, 4)
            def _(i):
                inner = {**picks, free[0]: i}
                found = terms(c, s, level, inner, extra)
                ref, index = found[0]
                ref[index] = total(found).astype(jnp.bfloat16)
        else:
            found = terms(c, s, level, picks, extra)
            ref, index = found[0]
            ref[index] = total(found).astype(jnp.bfloat16)

    def done_picks(stream, level):
        return {axis: coords[axis] for axis in stream.order[:level]}

    def region(c, s, picks):
        lanes = units[c][s][1] * LANES
        return work[c].at[(s, *[picks.get(a, slice(None)) for a in range(3)], slice(None), slice(0, lanes))]

    def stage_a(c, s, level):
        stream = streams[s]
        lanes = units[c][s][1] * LANES
        axis = stream.order[level]
        me = coords[axis]
        other = stream.first(me)
        if level == 0:
            for own in owns.pop((c, s)):
                own.wait()
            arrive((c, s, 0))
        else:
            arrive((c, s, ("b", level - 1)))
        later = len(stream.order[level + 1 :])
        for slab, place in ((1, stream.mate(other)), (0, other)):
            picks = {**done_picks(stream, level), axis: place}
            settle(c, s, level, picks)
            send(
                region(c, s, picks),
                landed[1 + 2 * level][c].at[(s, slab, *[slice(None)] * later, slice(None), slice(0, lanes))],
                peer(axis, other),
                (c, s, ("a", level, slab)),
            )

    def stage_b(c, s, level):
        stream = streams[s]
        lanes = units[c][s][1] * LANES
        axis = stream.order[level]
        me = coords[axis]
        other = stream.mate(me)
        picks = {**done_picks(stream, level), axis: other}
        arrive((c, s, ("a", level, 1)))
        settle(c, s, level, picks, extra=1)
        later = len(stream.order[level + 1 :])
        send(
            region(c, s, picks),
            landed[2 + 2 * level][c].at[(s, *[slice(None)] * later, slice(None), slice(0, lanes))],
            peer(axis, other),
            (c, s, ("b", level)),
        )
        arrive((c, s, ("a", level, 0)))

    def finish(c):
        for s in range(STREAMS):
            stream = streams[s]
            first, many, _ = units[c][s]
            arrive((c, s, ("b", 2)))
            value = total(terms(c, s, 3, done_picks(stream, 3)))
            for place in range(many):
                final[section, first + place] = value[:, place * LANES : (place + 1) * LANES]
        first = units[c][0][0]
        many = sum(unit[1] for unit in units[c])
        region = final.at[section, pl.ds(first, many)]
        send(region, region, sibling, (c, "final"))

    start(0)
    if chunks > 1:
        start(1)
    for step in range(chunks + 6):
        for c in range(chunks):
            stage = step - c
            if stage == 6:
                finish(c)
            elif 0 <= stage < 6:
                for s in range(STREAMS):
                    (stage_a if stage % 2 == 0 else stage_b)(c, s, stage // 2)
                if stage == 0 and c + 2 < chunks:
                    start(c + 2)
    tiles = half_tiles()
    for c in range(chunks):
        arrive((c, "final"))
    for number, (source, row, column) in enumerate(tiles):
        rows, columns = SOURCES[source][1:]
        share = SHARES[source]
        for half in range(2):
            value = final[half, number]
            lane = half * columns // 2 + column * LANES
            if share[0] == 8:
                outputs[source][:, lane : lane + LANES] = value[:8]
                outputs[source][:, columns + lane : columns + lane + LANES] = value[8:]
            else:
                outputs[source][16 * row : 16 * row + 16, lane : lane + LANES] = value
    for copy in sends:
        copy.wait_send()


def reduce_call(counts, arrays):
    units = make_units(counts)
    chunks = len(units)
    wide = [max(unit[1] for unit in row) * LANES for row in units]
    shapes = [
        (4, 4, 4), (4, 4, 4), (2, 4, 4), (4, 4), (2, 4), (4,), (2,), (),
    ]
    scratch = []
    for shape in shapes:
        for lanes in wide:
            scratch.append(pltpu.VMEM((STREAMS, *shape, 16, lanes), jnp.bfloat16))
    scratch.append(pltpu.VMEM((2, len(half_tiles()), 16, LANES), jnp.float32))
    pieces = sum(len(unit[2]) for row in units for unit in row)
    sends = pieces + 9 * chunks * STREAMS + chunks
    scratch += [
        pltpu.SemaphoreType.DMA((sends,)),
        pltpu.SemaphoreType.DMA((sends,)),
        pltpu.SemaphoreType.DMA((pieces,)),
    ]
    arrays = [
        array.reshape(4, 4, 4, rows, columns) for array, (_, rows, columns) in zip(arrays, SOURCES)
    ]
    return pl.pallas_call(
        functools.partial(reduce_kernel, units),
        out_shape=[jax.ShapeDtypeStruct(share, jnp.float32) for share in SHARES],
        in_specs=[pl.BlockSpec(memory_space=pl.ANY)] * len(arrays),
        out_specs=[pl.BlockSpec(memory_space=pltpu.VMEM)] * len(SHARES),
        scratch_shapes=scratch,
        compiler_params=pltpu.CompilerParams(
            collective_id=0, has_side_effects=True, vmem_limit_bytes=60 * 1024 * 1024
        ),
        name="reduce_shares",
    )(*arrays)


LOW = jnp.bfloat16
FULL = jnp.float32
LN2 = math.log(2.0)
FAR = -1e30


def dot(a, b):
    return jnp.dot(a, b, preferred_element_type=FULL)


def dot_nt(a, b):
    return lax.dot_general(a, b, (((1,), (1,)), ((), ())), preferred_element_type=FULL)


def norm_parts(v):
    centred = v - jnp.mean(v, axis=-1, keepdims=True)
    r = lax.rsqrt(jnp.mean(centred * centred, axis=-1, keepdims=True) + 1e-6)
    return centred * r, r


def norm_back(gn, v, gain):
    vh, r = norm_parts(v)
    gg = gn * gain
    gv = r * (gg - jnp.mean(gg, axis=-1, keepdims=True) - vh * jnp.mean(gg * vh, axis=-1, keepdims=True))
    return gv, jnp.sum(gn * vh, axis=0, keepdims=True), jnp.sum(gn, axis=0, keepdims=True)


def gelu_parts(u):
    z = jnp.abs(u) * (0.3275911 / math.sqrt(2.0))
    t = 1.0 / (1.0 + z)
    poly = 1.061405429
    for c in (-1.453152027, 1.421413741, -0.284496736, 0.254829592):
        poly = poly * t + c
    bell = jnp.exp2(u * u * (-0.5 / LN2))
    tail = (0.5 * t) * poly * bell
    phi = jnp.where(u >= 0, 1.0 - tail, tail)
    return u * phi, phi + u * (bell * (1.0 / math.sqrt(2.0 * math.pi)))


def paired(a, b):
    w = a.shape[1]
    return jnp.concatenate([a.reshape(64, 8, w), b.reshape(64, 8, w)], axis=1).astype(LOW)


def blocks_of(total, size):
    cuts = list(range(0, total - size + 1, size))
    return [(c, (size if i + 1 < len(cuts) else total - c)) for i, c in enumerate(cuts)]


def attention_forward(rows, heads, hs, k_ref, ones_ref, far_ref, qT, vT, mix, e_ref, oT, linv):
    group = 128 // hs
    mix[...] = jnp.zeros_like(mix)
    mix[128:256, :] = far_ref[...]
    for g in range(heads // group):
        lanes = slice(128 * g, 128 * g + 128)
        left = jnp.concatenate([k_ref[:, lanes], ones_ref[...]], axis=1)
        for i in range(group):
            h = g * group + i
            feat = slice(h * hs, h * hs + hs)
            if i:
                mix[(i - 1) * hs : i * hs, :] = jnp.zeros((hs, rows), LOW)
            else:
                mix[128 - hs : 128, :] = jnp.zeros((hs, rows), LOW)
            mix[i * hs : i * hs + hs, :] = qT[feat, :]
            head_forward(rows, h, feat, left, vT, mix, e_ref, oT, linv)


def head_forward(rows, h, feat, left, vT, mix, e_ref, oT, linv):
    for first, many in blocks_of(rows, 256):
        cols = slice(first, first + many)
        s = dot(left, mix[:, cols])
        peak = jnp.max(s, axis=0, keepdims=True)
        e_ref[h, :, cols] = jnp.exp2(s - peak).astype(LOW)
    lhs = jnp.concatenate([vT[feat, :], jnp.ones((16, rows), LOW)], axis=0)
    o = dot(lhs, e_ref[h])
    hs = feat.stop - feat.start
    inverse = 1.0 / o[hs : hs + 1]
    linv[h : h + 1, :] = inverse
    oT[feat, :] = (o[:hs] * inverse).astype(LOW)


def attention_backward(rows, heads, hs, v_ref, qT, kT, goT, oT, e_ref, linv, mix, gtT):
    group = 128 // hs
    width = heads * hs
    scale = hs**-0.5
    for g in range(heads // group):
        lanes = slice(128 * g, 128 * g + 128)
        for i in range(group):
            h = g * group + i
            feat = slice(h * hs, h * hs + hs)
            go = goT[feat, :] * linv[h : h + 1, :]
            low = go.astype(LOW)
            centre = jnp.sum(go * oT[feat, :].astype(FULL), axis=0, keepdims=True)
            if i:
                mix[(i - 1) * hs : i * hs, :] = jnp.zeros((hs, rows), LOW)
            else:
                mix[128 - hs : 128, :] = jnp.zeros((hs, rows), LOW)
            mix[i * hs : i * hs + hs, :] = low
            gtT[2 * width + h * hs : 2 * width + h * hs + hs, :] = dot_nt(low, e_ref[h]).astype(LOW)
            for first, many in blocks_of(rows, 256):
                cols = slice(first, first + many)
                gp = dot(v_ref[:, lanes], mix[0:128, cols])
                e_ref[h, :, cols] = (e_ref[h, :, cols].astype(FULL) * (gp - centre[:, cols])).astype(LOW)
            gs = e_ref[h]
            gtT[feat, :] = (dot(kT[feat, :], gs) * scale).astype(LOW)
            gtT[width + h * hs : width + h * hs + hs, :] = (dot_nt(qT[feat, :], gs) * LN2).astype(LOW)


ROWS, DD, DFF, HEADS = 784, 512, 2048, 16
STEP = 112


def decoder_kernel(
    embedded, tags, sines_high, sines_low, mask_token, gains, w_qkv, w_out, w_up, w_down, out_grad,
    dec_out, g_embedded, d_qkv, d_out, d_up, d_down, vectors,
    x_ref, low_a, low_aT, k_ref, v_ref, qT, kT, vT, e_ref, oT, linv, x1_ref, gz, ga_ref, y_ref, goT, gtT, mix, ones_ref, far_ref, sums,
):
    sums[...] = jnp.zeros_like(sums)
    tile = 256

    def each(body):
        @pl.loop(0, ROWS // STEP)
        def _(i):
            body(pl.ds(pl.multiple_of(i * STEP, STEP), STEP))

    wide = embedded[...]
    emb_high = wide.astype(LOW)
    emb_low = (wide - emb_high.astype(FULL)).astype(LOW)
    mask = mask_token[...].astype(FULL)

    def inputs(rows):
        tag = tags[rows, :]
        source, row_tag, column_tag, segment = (tag[:, i : i + 1] for i in range(4))
        lane = lax.broadcasted_iota(jnp.int32, (STEP, 256), 1)
        small = lax.broadcasted_iota(jnp.int32, (STEP, 128), 1)
        pick = (lane == source).astype(LOW)
        x = dot(pick, emb_high) + dot(pick, emb_low)
        x = jnp.where(source < 0, mask, x)
        row_pick = (small == row_tag).astype(LOW)
        column_pick = (small == column_tag).astype(LOW)
        row_wave = dot(row_pick, sines_high[...]) + dot(row_pick, sines_low[...])
        column_wave = dot(column_pick, sines_high[...]) + dot(column_pick, sines_low[...])
        x = x + jnp.concatenate([row_wave, column_wave], axis=1)
        x_ref[rows, :] = x
        low_a[rows, :] = (norm_parts(x)[0] * gains[0:1] + gains[1:2]).astype(LOW)
        same = small == segment
        ones_ref[rows, :] = same.astype(LOW)
        y_ref[rows, 0:128] = jnp.where(same | (small > 12), 0.0, FAR)
        live = (segment < 12).astype(FULL)
        gz[rows, :] = (out_grad[rows, :].astype(FULL) * live).astype(LOW)

    each(inputs)
    far_ref[...] = y_ref[:, 0:128].T.astype(LOW)
    low_aT[...] = low_a[...].T

    for j in range(2):
        t = dot(low_a[...], w_qkv[:, j * tile : (j + 1) * tile]) * (32**-0.5 / LN2)
        qT[j * tile : (j + 1) * tile, :] = t.astype(LOW).T
        t = dot(low_a[...], w_qkv[:, DD + j * tile : DD + (j + 1) * tile]).astype(LOW)
        k_ref[:, j * tile : (j + 1) * tile] = t
        kT[j * tile : (j + 1) * tile, :] = t.T
        t = dot(low_a[...], w_qkv[:, 2 * DD + j * tile : 2 * DD + (j + 1) * tile]).astype(LOW)
        v_ref[:, j * tile : (j + 1) * tile] = t
        vT[j * tile : (j + 1) * tile, :] = t.T

    attention_forward(ROWS, HEADS, 32, k_ref, ones_ref, far_ref, qT, vT, mix, e_ref, oT, linv)

    low_a[...] = oT[...].T
    for j in range(2):
        cols = slice(j * tile, (j + 1) * tile)
        x1_ref[:, cols] = x_ref[:, cols] + dot(low_a[...], w_out[:, cols])

    def second(rows):
        x1 = x1_ref[rows, :]
        low_a[rows, :] = (norm_parts(x1)[0] * gains[2:3] + gains[3:4]).astype(LOW)
        y_ref[rows, :] = x1
        ga_ref[rows, :] = jnp.zeros((STEP, DD), FULL)

    each(second)
    a2T = goT
    del a2T
    a2_t = low_a[...].T

    kT_keep = None
    del kT_keep
    gtT[0:DD, :] = a2_t

    @pl.loop(0, DFF // (2 * tile))
    def _(j):
        halves = []
        for half in range(2):
            cols = pl.ds(pl.multiple_of(j * tile + half * (DFF // 2), tile), tile)
            u = dot(low_a[...], w_up[:, cols])
            m, slope = gelu_parts(u)
            m = m.astype(LOW)
            y_ref[...] += dot(m, w_down[cols, :])
            gm = dot_nt(gz[...], w_down[cols, :])
            gu = (gm * slope).astype(LOW)
            ga_ref[...] += dot_nt(gu, w_up[:, cols])
            d_down[cols, :] = dot(m.T, gz[...]).astype(LOW)
            halves.append(dot(gtT[0:DD, :], gu))
        d_up[:, :, pl.ds(pl.multiple_of(j * tile, tile), tile)] = paired(*halves)

    def third(rows):
        live = (tags[rows, 3:4] < 12).astype(FULL)
        dec_out[rows, :] = (y_ref[rows, :] * live).astype(LOW)
        gv, dgain, dshift = norm_back(ga_ref[rows, :], x1_ref[rows, :], gains[2:3])
        gx1 = out_grad[rows, :].astype(FULL) * live + gv
        x1_ref[rows, :] = gx1
        low_a[rows, :] = gx1.astype(LOW)
        sums[2:3, :] += dgain
        sums[3:4, :] += dshift

    each(third)
    for j in range(2):
        goT[j * tile : (j + 1) * tile, :] = dot_nt(w_out[j * tile : (j + 1) * tile, :], low_a[...])
    for j in range(2):
        half = dot(oT[...], low_a[:, j * tile : (j + 1) * tile])
        if j == 0:
            first_half = half
        else:
            d_out[...] = paired(first_half, half)

    attention_backward(ROWS, HEADS, 32, v_ref, qT, kT, goT, oT, e_ref, linv, mix, gtT)

    for j in range(3):
        lo = dot_nt(low_aT[...], gtT[j * tile : (j + 1) * tile, :])
        hi = dot_nt(low_aT[...], gtT[768 + j * tile : 768 + (j + 1) * tile, :])
        d_qkv[:, :, j * tile : (j + 1) * tile] = paired(lo, hi)
    for j in range(2):
        cols = slice(j * tile, (j + 1) * tile)
        y_ref[:, cols] = dot(w_qkv[cols, :], gtT[...]).T

    def fourth(rows):
        gv, dgain, dshift = norm_back(y_ref[rows, :], x_ref[rows, :], gains[0:1])
        gx = x1_ref[rows, :] + gv
        sums[0:1, :] += dgain
        sums[1:2, :] += dshift
        source = tags[rows, 0:1]
        sums[4:5, :] += jnp.sum(jnp.where(source < 0, gx, 0.0), axis=0, keepdims=True)
        low_a[rows, :] = gx.astype(LOW)
        lane = lax.broadcasted_iota(jnp.int32, (STEP, 256), 1)
        y_ref[rows, 0:256] = (lane == source).astype(FULL)

    each(fourth)
    pick = y_ref[:, 0:256].astype(LOW).T
    g_embedded[...] = dot(pick, low_a[...]).astype(LOW)
    vectors[...] = sums[...]


def decoder_call(embedded, tags, sines_high, sines_low, mask_token, gains, w_qkv, w_out, w_up, w_down, out_grad):
    vmem = pl.BlockSpec(memory_space=pltpu.VMEM)
    low = lambda *shape: pltpu.VMEM(shape, LOW)
    full = lambda *shape: pltpu.VMEM(shape, FULL)
    return pl.pallas_call(
        decoder_kernel,
        out_shape=[
            jax.ShapeDtypeStruct((ROWS, DD), LOW),
            jax.ShapeDtypeStruct((256, DD), LOW),
            jax.ShapeDtypeStruct((64, 16, 768), LOW),
            jax.ShapeDtypeStruct((64, 16, 256), LOW),
            jax.ShapeDtypeStruct((64, 16, 1024), LOW),
            jax.ShapeDtypeStruct((DFF, DD), LOW),
            jax.ShapeDtypeStruct((8, DD), FULL),
        ],
        in_specs=[vmem] * 11,
        out_specs=[vmem] * 7,
        scratch_shapes=[
            full(ROWS, DD), low(ROWS, DD), low(DD, ROWS), low(ROWS, DD), low(ROWS, DD),
            low(DD, ROWS), low(DD, ROWS), low(DD, ROWS), low(HEADS, ROWS, ROWS), low(DD, ROWS),
            full(HEADS, ROWS), full(ROWS, DD), low(ROWS, DD), full(ROWS, DD), full(ROWS, DD),
            full(DD, ROWS), low(3 * DD, ROWS), low(256, ROWS), low(ROWS, 128), low(128, ROWS), full(8, DD),
        ],
        compiler_params=pltpu.CompilerParams(vmem_limit_bytes=63 * 1024 * 1024),
        name="decoder",
    )(embedded, tags, sines_high, sines_low, mask_token, gains, w_qkv, w_out, w_up, w_down, out_grad)


def wave_tables():
    quarter = DD // 4
    frequency = np.exp(np.arange(quarter, dtype=np.float32) * np.float32(-math.log(10000.0) / quarter)).astype(np.float32)
    places = np.zeros((128, 1), np.float32)
    for f, factor in enumerate((0.5, 1.0, 2.0, 4.0)):
        places[f * 28 : f * 28 + 28, 0] = np.arange(28, dtype=np.float32) * factor
    angle = (places * frequency[None, :]).astype(np.float32).astype(np.float64)
    waves = np.concatenate([np.sin(angle), np.cos(angle)], axis=1)
    waves[112:] = 0.0
    high = jnp.asarray(waves, FULL).astype(LOW)
    low = (jnp.asarray(waves, FULL) - high.astype(FULL)).astype(LOW)
    return high, low


ER, ED, EF = 256, 1024, 4096
EH = 64


def encoder_forward_kernel(
    arrived, tags, gains, w_qkv_h, w_out_h, w_up_h, w_down_h, w_embed_h,
    encoded_h, embedded_h, x1_h, m_h, slope_h, qT_h, kT_h, v_h, e_h, linv_h, oT_h,
    w_qkv, w_out, w_up, w_down, w_embed,
    encoded, embedded, x1, m_ref, slope_ref, qT, kT, v_ref, e_ref, linv, oT,
    x_ref, low_a, k_ref, vT, mix, ones_ref, far_ref, y_ref, in_sem, out_sem,
):
    loads = []
    for i, (source, target) in enumerate(
        ((w_qkv_h, w_qkv), (w_out_h, w_out), (w_up_h, w_up), (w_down_h, w_down), (w_embed_h, w_embed))
    ):
        copy = pltpu.make_async_copy(source, target, in_sem.at[i])
        copy.start()
        loads.append(copy)
    stores = []

    def keep(source, target):
        copy = pltpu.make_async_copy(source, target, out_sem.at[len(stores)])
        copy.start()
        stores.append(copy)

    tag = tags[...]
    lane = lax.broadcasted_iota(jnp.int32, (ROWS, 256), 1)
    small = lax.broadcasted_iota(jnp.int32, (ROWS, 128), 1)
    pick = (lane == tag[:, 0:1]).astype(FULL).T.astype(LOW)
    items = dot(pick, (small == tag[:, 3:4]).astype(LOW))
    slot = lax.broadcasted_iota(jnp.int32, (ER, 128), 1)
    empty = jnp.sum(items, axis=1, keepdims=True) < 0.5
    items = jnp.where((slot == 13) & empty, 1.0, items)
    ones_ref[...] = items.astype(LOW)
    far_ref[...] = jnp.where((items > 0.5) | (slot > 13), 0.0, FAR).T.astype(LOW)

    x = arrived[...].astype(FULL)
    x_ref[...] = x
    low_a[...] = (norm_parts(x)[0] * gains[0:1] + gains[1:2]).astype(LOW)
    loads[0].wait()

    tile = 256

    @pl.loop(0, ED // tile)
    def _(j):
        cols = pl.ds(pl.multiple_of(j * tile, tile), tile)
        t = dot(low_a[...], w_qkv[:, cols]) * (EH**-0.5 / LN2)
        qT[cols, :] = t.T.astype(LOW)
        t = dot(low_a[...], w_qkv[:, pl.ds(pl.multiple_of(ED + j * tile, tile), tile)])
        k_ref[:, cols] = t.astype(LOW)
        kT[cols, :] = t.T.astype(LOW)
        t = dot(low_a[...], w_qkv[:, pl.ds(pl.multiple_of(2 * ED + j * tile, tile), tile)])
        v_ref[:, cols] = t.astype(LOW)
        vT[cols, :] = t.T.astype(LOW)

    keep(qT, qT_h)
    keep(kT, kT_h)
    keep(v_ref, v_h)
    attention_forward(ER, HEADS, EH, k_ref, ones_ref, far_ref, qT, vT, mix, e_ref, oT, linv)
    keep(e_ref, e_h)
    keep(linv, linv_h)
    keep(oT, oT_h)
    low_a[...] = oT[...].T
    loads[1].wait()

    @pl.loop(0, ED // tile)
    def _(j):
        cols = pl.ds(pl.multiple_of(j * tile, tile), tile)
        x1[:, cols] = x_ref[:, cols] + dot(low_a[...], w_out[:, cols])

    keep(x1, x1_h)
    branch = x1[...]
    low_a[...] = (norm_parts(branch)[0] * gains[2:3] + gains[3:4]).astype(LOW)
    y_ref[...] = branch
    loads[2].wait()
    loads[3].wait()

    @pl.loop(0, EF // 512)
    def _(j):
        cols = pl.ds(pl.multiple_of(j * 512, 512), 512)
        m, slope = gelu_parts(dot(low_a[...], w_up[:, cols]))
        m = m.astype(LOW)
        m_ref[:, cols] = m
        slope_ref[:, cols] = slope.astype(LOW)
        y_ref[...] += dot(m, w_down[cols, :])

    keep(m_ref, m_h)
    keep(slope_ref, slope_h)
    encoded[...] = y_ref[...].astype(LOW)
    keep(encoded, encoded_h)
    loads[4].wait()
    embedded[...] = dot(encoded[...], w_embed[...])
    keep(embedded, embedded_h)
    for copy in stores:
        copy.wait()


ANY = pl.BlockSpec(memory_space=pl.ANY)
VMEM = pl.BlockSpec(memory_space=pltpu.VMEM)
WEIGHTS = [((ED, 3 * ED), LOW), ((ED, ED), LOW), ((ED, EF), LOW), ((EF, ED), LOW), ((ED, DD), LOW)]
KEPT = [
    ((ER, ED), LOW), ((ER, DD), FULL), ((ER, ED), FULL), ((ER, EF), LOW), ((ER, EF), LOW),
    ((ED, ER), LOW), ((ED, ER), LOW), ((ER, ED), LOW), ((HEADS, ER, ER), LOW), ((HEADS, ER), FULL), ((ED, ER), LOW),
]


def encoder_forward_call(arrived, tags, gains, w_qkv, w_out, w_up, w_down, w_embed):
    scratch = [pltpu.VMEM(*s) for s in WEIGHTS + KEPT]
    scratch += [
        pltpu.VMEM((ER, ED), FULL), pltpu.VMEM((ER, ED), LOW), pltpu.VMEM((ER, ED), LOW), pltpu.VMEM((ED, ER), LOW),
        pltpu.VMEM((256, ER), LOW), pltpu.VMEM((ER, 128), LOW), pltpu.VMEM((128, ER), LOW), pltpu.VMEM((ER, ED), FULL),
        pltpu.SemaphoreType.DMA((5,)), pltpu.SemaphoreType.DMA((len(KEPT),)),
    ]
    return pl.pallas_call(
        encoder_forward_kernel,
        out_shape=[jax.ShapeDtypeStruct(*s) for s in KEPT],
        in_specs=[VMEM] * 3 + [ANY] * 5,
        out_specs=[ANY] * len(KEPT),
        scratch_shapes=scratch,
        compiler_params=pltpu.CompilerParams(vmem_limit_bytes=60 * 1024 * 1024),
        name="encoder_forward",
    )(arrived, tags, gains, w_qkv, w_out, w_up, w_down, w_embed)


def encoder_backward_kernel(
    g_embedded, arrived, gains, w_qkv_h, w_out_h, w_up_h, w_down_h, w_embed_h,
    encoded_h, x1_h, m_h, slope_h, qT_h, kT_h, v_h, e_h, linv_h, oT_h,
    received, vectors, d_embed_h, d_qkv_h, d_out_h, d_up_h, d_down_h,
    w_qkv, w_out, w_up, w_down, w_embed,
    encoded, x1, m_ref, slope_ref, qT, kT, v_ref, e_ref, linv, oT,
    d_embed, d_up, d_down, gy, gz, ga_ref, low_a, a1T, a2T, goT, gtT, mix, in_sem, out_sem,
):
    pairs = [
        (w_embed_h, w_embed), (encoded_h, encoded), (w_down_h, w_down), (slope_h, slope_ref), (m_h, m_ref), (x1_h, x1), (w_up_h, w_up),
        (w_out_h, w_out), (oT_h, oT), (e_h, e_ref), (linv_h, linv), (v_h, v_ref), (kT_h, kT), (qT_h, qT), (w_qkv_h, w_qkv),
    ]
    loads = []
    for i, (source, target) in enumerate(pairs):
        copy = pltpu.make_async_copy(source, target, in_sem.at[i])
        copy.start()
        loads.append(copy)
    stores = []

    def keep(source, target):
        copy = pltpu.make_async_copy(source, target, out_sem.at[len(stores)])
        copy.start()
        stores.append(copy)

    def ready(count):
        while len(pairs) - len(loads) < count:
            loads.pop(0).wait()

    tile = 256
    x = arrived[...].astype(FULL)
    a1T[...] = (norm_parts(x)[0] * gains[0:1] + gains[1:2]).T.astype(LOW)
    ready(2)
    gy[...] = dot_nt(g_embedded[...], w_embed[...])
    gz[...] = gy[...].astype(LOW)
    d_embed[...] = dot(encoded[...].T, g_embedded[...]).astype(LOW)
    keep(d_embed, d_embed_h)
    ready(6)
    a2T[...] = (norm_parts(x1[...])[0] * gains[2:3] + gains[3:4]).T.astype(LOW)
    ga_ref[...] = jnp.zeros_like(ga_ref)
    ready(7)

    @pl.loop(0, EF // 512)
    def _(j):
        cols = pl.ds(pl.multiple_of(j * 512, 512), 512)
        gm = dot_nt(gz[...], w_down[cols, :])
        gu = (gm * slope_ref[:, cols].astype(FULL)).astype(LOW)
        ga_ref[...] += dot_nt(gu, w_up[:, cols])
        d_up[:, cols] = dot(a2T[...], gu).astype(LOW)
        d_down[cols, :] = dot(m_ref[:, cols].T, gz[...]).astype(LOW)

    keep(d_up, d_up_h)
    keep(d_down, d_down_h)
    gv, dgain, dshift = norm_back(ga_ref[...], x1[...], gains[2:3])
    vectors[2:3, :] = dgain
    vectors[3:4, :] = dshift
    gx1 = gy[...] + gv
    gy[...] = gx1
    low_a[...] = gx1.astype(LOW)
    ready(9)

    @pl.loop(0, ED // tile)
    def _(j):
        cols = pl.ds(pl.multiple_of(j * tile, tile), tile)
        goT[cols, :] = dot_nt(w_out[cols, :], low_a[...])
        w_up[:, cols] = dot(oT[...], low_a[:, cols]).astype(LOW)

    keep(w_up.at[:, 0:ED], d_out_h)
    ready(14)
    mix[...] = jnp.zeros_like(mix)
    attention_backward(ER, HEADS, EH, v_ref, qT, kT, goT, oT, e_ref, linv, mix, gtT)
    ready(15)

    @pl.loop(0, 3 * ED // tile)
    def _(j):
        cols = pl.ds(pl.multiple_of(j * tile, tile), tile)
        w_up[:, pl.ds(pl.multiple_of(ED + j * tile, tile), tile)] = dot_nt(a1T[...], gtT[cols, :]).astype(LOW)

    keep(w_up.at[:, ED:EF], d_qkv_h)

    @pl.loop(0, ED // tile)
    def _(j):
        cols = pl.ds(pl.multiple_of(j * tile, tile), tile)
        ga_ref[:, cols] = dot(w_qkv[cols, :], gtT[...]).T

    gv, dgain, dshift = norm_back(ga_ref[...], arrived[...].astype(FULL), gains[0:1])
    vectors[0:1, :] = dgain
    vectors[1:2, :] = dshift
    vectors[4:8, :] = jnp.zeros((4, ED), FULL)
    received[...] = (gy[...] + gv).astype(LOW)
    for copy in stores:
        copy.wait()


def encoder_backward_call(g_embedded, arrived, gains, weights, kept):
    encoded, _, x1, m, slope, qT, kT, v, e, linv, oT = kept
    kept_shapes = KEPT[:1] + KEPT[2:]
    shapes = [
        ((ER, ED), LOW), ((8, ED), FULL), ((ED, DD), LOW), ((ED, 3 * ED), LOW), ((ED, ED), LOW), ((ED, EF), LOW), ((EF, ED), LOW),
    ]
    scratch = [pltpu.VMEM(*s) for s in WEIGHTS + kept_shapes]
    scratch += [
        pltpu.VMEM((ED, DD), LOW), pltpu.VMEM((ED, EF), LOW), pltpu.VMEM((EF, ED), LOW),
        pltpu.VMEM((ER, ED), FULL), pltpu.VMEM((ER, ED), LOW), pltpu.VMEM((ER, ED), FULL), pltpu.VMEM((ER, ED), LOW),
        pltpu.VMEM((ED, ER), LOW), pltpu.VMEM((ED, ER), LOW), pltpu.VMEM((ED, ER), FULL), pltpu.VMEM((3 * ED, ER), LOW),
        pltpu.VMEM((256, ER), LOW),
        pltpu.SemaphoreType.DMA((15,)), pltpu.SemaphoreType.DMA((5,)),
    ]
    return pl.pallas_call(
        encoder_backward_kernel,
        out_shape=[jax.ShapeDtypeStruct(*s) for s in shapes],
        in_specs=[VMEM] * 3 + [ANY] * 15,
        out_specs=[VMEM] * 2 + [ANY] * 5,
        scratch_shapes=scratch,
        compiler_params=pltpu.CompilerParams(vmem_limit_bytes=63 * 1024 * 1024),
        name="encoder_backward",
    )(g_embedded, arrived, gains, *weights, encoded, x1, m, slope, qT, kT, v, e, linv, oT)

COUNTS = ((3,) * 6, (4,) * 6, (4, 4, 4, 3, 3, 3))


def tag_table(lengths, visible, gsd_index):
    row = jnp.arange(ROWS, dtype=jnp.int32)
    ends = jnp.cumsum(lengths)
    segment = jnp.sum((row[:, None] >= ends[None]).astype(jnp.int32), axis=1)
    onehot = (segment[:, None] == jnp.arange(lengths.shape[0])[None]).astype(jnp.int32)
    offset = row - jnp.sum(onehot * (ends - lengths)[None], axis=1)
    length = jnp.sum(onehot * lengths[None], axis=1)
    factor = jnp.sum(onehot * gsd_index[None], axis=1)
    side = jnp.where(length == 64, 8, jnp.where(length == 196, 14, 28))
    live = segment < lengths.shape[0]
    row_tag = jnp.where(live, factor * 28 + offset // side, -1)
    column_tag = jnp.where(live, factor * 28 + offset % side, -1)
    rank = jnp.cumsum(visible) - 1
    source = jnp.where(visible == 1, rank % 128 * 2 + rank // 128, -1)
    return jnp.stack([source, row_tag, column_tag, segment], axis=1).astype(jnp.int32)


def shared_sums(enc_vectors, d_embed, d_enc, dec_vectors, d_dec):
    vectors = [enc_vectors[i] for i in range(4)] + [dec_vectors[i] for i in (4, 0, 1, 2, 3)]
    rows = jnp.concatenate([vector.reshape(64, -1) for vector in vectors], axis=1).astype(LOW)
    rows = jnp.pad(rows[:, None, :], ((0, 0), (0, 15), (0, 256 - rows.shape[1])))
    dec_qkv, dec_out, dec_up, dec_down = d_dec
    enc_qkv, enc_out, enc_up, enc_down = d_enc
    shares = reduce_call(
        COUNTS, (rows, d_embed, dec_qkv, dec_out, dec_up, dec_down, enc_down, enc_up, enc_out, enc_qkv)
    )
    row = shares[0][0]
    cuts, first = [], 0
    for vector in vectors:
        many = vector.shape[0] // 64
        cuts.append(row[first : first + many])
        first += many
    return (
        cuts[0], cuts[1], shares[9], shares[8], cuts[2], cuts[3], shares[7], shares[6],
        shares[1], cuts[4], cuts[5], cuts[6], shares[2], shares[3], cuts[7], cuts[8], shares[4], shares[5],
    )


def per_device(
    patches, lengths, visible, gsd_index,
    enc_attn_gain, enc_attn_shift, enc_qkv, enc_out, enc_mlp_gain, enc_mlp_shift, enc_up, enc_down,
    dec_embed, mask_token,
    dec_attn_gain, dec_attn_shift, dec_qkv, dec_out, dec_mlp_gain, dec_mlp_shift, dec_up, dec_down,
    out_grad,
):
    both = ("section", "batch")
    arrived = lax.all_to_all(patches, both, split_axis=0, concat_axis=0, tiled=True)
    tags = tag_table(lengths[0], visible, gsd_index[0])
    enc_gains = jnp.stack([enc_attn_gain, enc_attn_shift, enc_mlp_gain, enc_mlp_shift])
    dec_gains = jnp.stack([dec_attn_gain, dec_attn_shift, dec_mlp_gain, dec_mlp_shift])
    weights = (enc_qkv, enc_out, enc_up, enc_down, dec_embed)
    kept = encoder_forward_call(arrived, tags, enc_gains, *weights)
    high, low = wave_tables()
    decoder = decoder_call(
        kept[1], tags, high, low, mask_token[None], dec_gains, dec_qkv, dec_out, dec_up, dec_down, out_grad
    )
    dec_output, g_embedded, *d_dec, dec_vectors = decoder
    received, enc_vectors, d_embed, *d_enc = encoder_backward_call(g_embedded, arrived, enc_gains, weights, kept)
    patch_grad = lax.all_to_all(received, both, split_axis=0, concat_axis=0, tiled=True).astype(FULL)
    return (dec_output, patch_grad) + shared_sums(enc_vectors, d_embed, d_enc, dec_vectors, d_dec)


def solution(mesh):
    return jax.shard_map(
        per_device,
        mesh=mesh,
        in_specs=(
            P(("section", "batch"), None),
            P(("section", "batch"), None),
            P(("section", "batch")),
            P(("section", "batch"), None),
            P(),
            P(),
            P(),
            P(),
            P(),
            P(),
            P(),
            P(),
            P(),
            P(),
            P(),
            P(),
            P(),
            P(),
            P(),
            P(),
            P(),
            P(),
            P(("section", "batch"), None),
        ),
        out_specs=(
            P(("section", "batch"), None),
            P(("section", "batch"), None),
            P("batch"),
            P("batch"),
            P("batch", None),
            P("batch", None),
            P("batch"),
            P("batch"),
            P("batch", None),
            P("batch", None),
            P("batch", None),
            P("batch"),
            P("batch"),
            P("batch"),
            P("batch", None),
            P("batch", None),
            P("batch"),
            P("batch"),
            P("batch", None),
            P("batch", None),
        ),
        check_vma=False,
    )
```

```python
import functools
import math

import jax
import jax.numpy as jnp
import numpy as np
from jax import lax
from jax.experimental import pallas as pl
from jax.experimental.pallas import tpu as pltpu
from jax.sharding import PartitionSpec as P

LOW = jnp.bfloat16
FULL = jnp.float32
LN2 = math.log(2.0)
FAR = -1e30


def dot(a, b):
    return jnp.dot(a, b, preferred_element_type=FULL)


def dot_nt(a, b):
    return lax.dot_general(a, b, (((1,), (1,)), ((), ())), preferred_element_type=FULL)


def norm_parts(v):
    centred = v - jnp.mean(v, axis=-1, keepdims=True)
    r = lax.rsqrt(jnp.mean(centred * centred, axis=-1, keepdims=True) + 1e-6)
    return centred * r, r


def norm_back(gn, v, gain):
    vh, r = norm_parts(v)
    gg = gn * gain
    gv = r * (gg - jnp.mean(gg, axis=-1, keepdims=True) - vh * jnp.mean(gg * vh, axis=-1, keepdims=True))
    return gv, jnp.sum(gn * vh, axis=0, keepdims=True), jnp.sum(gn, axis=0, keepdims=True)


def gelu_parts(u):
    z = jnp.abs(u) * (0.3275911 / math.sqrt(2.0))
    t = 1.0 / (1.0 + z)
    poly = 1.061405429
    for c in (-1.453152027, 1.421413741, -0.284496736, 0.254829592):
        poly = poly * t + c
    bell = jnp.exp2(u * u * (-0.5 / LN2))
    tail = (0.5 * t) * poly * bell
    phi = jnp.where(u >= 0, 1.0 - tail, tail)
    return u * phi, phi + u * (bell * (1.0 / math.sqrt(2.0 * math.pi)))


def paired(a, b):
    w = a.shape[1]
    return jnp.concatenate([a.reshape(64, 8, w), b.reshape(64, 8, w)], axis=1).astype(LOW)


def blocks_of(total, size):
    cuts = list(range(0, total - size + 1, size))
    return [(c, (size if i + 1 < len(cuts) else total - c)) for i, c in enumerate(cuts)]


def attention_forward(rows, heads, hs, k_ref, ones_ref, far_ref, qT, vT, mix, e_ref, oT, linv):
    group = 128 // hs
    mix[...] = jnp.zeros_like(mix)
    mix[128:256, :] = far_ref[...]
    for g in range(heads // group):
        lanes = slice(128 * g, 128 * g + 128)
        left = jnp.concatenate([k_ref[:, lanes], ones_ref[...]], axis=1)
        for i in range(group):
            h = g * group + i
            feat = slice(h * hs, h * hs + hs)
            if i:
                mix[(i - 1) * hs : i * hs, :] = jnp.zeros((hs, rows), LOW)
            else:
                mix[128 - hs : 128, :] = jnp.zeros((hs, rows), LOW)
            mix[i * hs : i * hs + hs, :] = qT[feat, :]
            head_forward(rows, h, feat, left, vT, mix, e_ref, oT, linv)


def head_forward(rows, h, feat, left, vT, mix, e_ref, oT, linv):
    for first, many in blocks_of(rows, 256):
        cols = slice(first, first + many)
        s = dot(left, mix[:, cols])
        peak = jnp.max(s, axis=0, keepdims=True)
        e_ref[h, :, cols] = jnp.exp2(s - peak).astype(LOW)
    lhs = jnp.concatenate([vT[feat, :], jnp.ones((16, rows), LOW)], axis=0)
    o = dot(lhs, e_ref[h])
    hs = feat.stop - feat.start
    inverse = 1.0 / o[hs : hs + 1]
    linv[h : h + 1, :] = inverse
    oT[feat, :] = (o[:hs] * inverse).astype(LOW)


def attention_backward(rows, heads, hs, v_ref, qT, kT, goT, oT, e_ref, linv, mix, gtT, between=None):
    group = 128 // hs
    width = heads * hs
    scale = hs**-0.5
    for g in range(heads // group):
        lanes = slice(128 * g, 128 * g + 128)
        for i in range(group):
            h = g * group + i
            feat = slice(h * hs, h * hs + hs)
            go = goT[feat, :] * linv[h : h + 1, :]
            low = go.astype(LOW)
            centre = jnp.sum(go * oT[feat, :].astype(FULL), axis=0, keepdims=True)
            if i:
                mix[(i - 1) * hs : i * hs, :] = jnp.zeros((hs, rows), LOW)
            else:
                mix[128 - hs : 128, :] = jnp.zeros((hs, rows), LOW)
            mix[i * hs : i * hs + hs, :] = low
            gtT[2 * width + h * hs : 2 * width + h * hs + hs, :] = dot_nt(low, e_ref[h]).astype(LOW)
            for first, many in blocks_of(rows, 256):
                cols = slice(first, first + many)
                gp = dot(v_ref[:, lanes], mix[0:128, cols])
                e_ref[h, :, cols] = (e_ref[h, :, cols].astype(FULL) * (gp - centre[:, cols])).astype(LOW)
            gs = e_ref[h]
            gtT[feat, :] = (dot(kT[feat, :], gs) * scale).astype(LOW)
            gtT[width + h * hs : width + h * hs + hs, :] = (dot_nt(qT[feat, :], gs) * LN2).astype(LOW)
        if between is not None:
            between(g)


ROWS, DD, DFF, HEADS = 784, 512, 2048, 16
STEP = 112


def decoder_kernel(
    embedded, tags, sines_high, sines_low, mask_token, gains, w_qkv, w_out, w_up, w_down, out_grad,
    dec_out, g_embedded, d_qkv, d_out, d_up, d_down, vectors,
    x_ref, low_a, low_aT, k_ref, v_ref, qT, kT, vT, e_ref, oT, linv, x1_ref, gz, ga_ref, y_ref, goT, gtT, mix, ones_ref, far_ref, sums,
):
    sums[...] = jnp.zeros_like(sums)
    tile = 256

    def each(body):
        @pl.loop(0, ROWS // STEP)
        def _(i):
            body(pl.ds(pl.multiple_of(i * STEP, STEP), STEP))

    wide = embedded[...]
    emb_high = wide.astype(LOW)
    emb_low = (wide - emb_high.astype(FULL)).astype(LOW)
    mask = mask_token[...].astype(FULL)

    def inputs(rows):
        tag = tags[rows, :]
        source, row_tag, column_tag, segment = (tag[:, i : i + 1] for i in range(4))
        lane = lax.broadcasted_iota(jnp.int32, (STEP, 256), 1)
        small = lax.broadcasted_iota(jnp.int32, (STEP, 128), 1)
        pick = (lane == source).astype(LOW)
        x = dot(pick, emb_high) + dot(pick, emb_low)
        x = jnp.where(source < 0, mask, x)
        row_pick = (small == row_tag).astype(LOW)
        column_pick = (small == column_tag).astype(LOW)
        row_wave = dot(row_pick, sines_high[...]) + dot(row_pick, sines_low[...])
        column_wave = dot(column_pick, sines_high[...]) + dot(column_pick, sines_low[...])
        x = x + jnp.concatenate([row_wave, column_wave], axis=1)
        x_ref[rows, :] = x
        low_a[rows, :] = (norm_parts(x)[0] * gains[0:1] + gains[1:2]).astype(LOW)
        same = small == segment
        ones_ref[rows, :] = same.astype(LOW)
        y_ref[rows, 0:128] = jnp.where(same | (small > 12), 0.0, FAR)
        live = (segment < 12).astype(FULL)
        gz[rows, :] = (out_grad[rows, :].astype(FULL) * live).astype(LOW)

    each(inputs)
    far_ref[...] = y_ref[:, 0:128].T.astype(LOW)
    low_aT[...] = low_a[...].T

    for j in range(2):
        t = dot(low_a[...], w_qkv[:, j * tile : (j + 1) * tile]) * (32**-0.5 / LN2)
        qT[j * tile : (j + 1) * tile, :] = t.astype(LOW).T
        t = dot(low_a[...], w_qkv[:, DD + j * tile : DD + (j + 1) * tile]).astype(LOW)
        k_ref[:, j * tile : (j + 1) * tile] = t
        kT[j * tile : (j + 1) * tile, :] = t.T
        t = dot(low_a[...], w_qkv[:, 2 * DD + j * tile : 2 * DD + (j + 1) * tile]).astype(LOW)
        v_ref[:, j * tile : (j + 1) * tile] = t
        vT[j * tile : (j + 1) * tile, :] = t.T

    attention_forward(ROWS, HEADS, 32, k_ref, ones_ref, far_ref, qT, vT, mix, e_ref, oT, linv)

    low_a[...] = oT[...].T
    for j in range(2):
        cols = slice(j * tile, (j + 1) * tile)
        x1_ref[:, cols] = x_ref[:, cols] + dot(low_a[...], w_out[:, cols])

    def second(rows):
        x1 = x1_ref[rows, :]
        low_a[rows, :] = (norm_parts(x1)[0] * gains[2:3] + gains[3:4]).astype(LOW)
        y_ref[rows, :] = x1
        ga_ref[rows, :] = jnp.zeros((STEP, DD), FULL)

    each(second)
    a2T = goT
    del a2T
    a2_t = low_a[...].T

    kT_keep = None
    del kT_keep
    gtT[0:DD, :] = a2_t

    @pl.loop(0, DFF // (2 * tile))
    def _(j):
        halves = []
        for half in range(2):
            cols = pl.ds(pl.multiple_of(j * tile + half * (DFF // 2), tile), tile)
            u = dot(low_a[...], w_up[:, cols])
            m, slope = gelu_parts(u)
            m = m.astype(LOW)
            y_ref[...] += dot(m, w_down[cols, :])
            gm = dot_nt(gz[...], w_down[cols, :])
            gu = (gm * slope).astype(LOW)
            ga_ref[...] += dot_nt(gu, w_up[:, cols])
            d_down[cols, :] = dot(m.T, gz[...]).astype(LOW)
            halves.append(dot(gtT[0:DD, :], gu))
        d_up[:, :, pl.ds(pl.multiple_of(j * tile, tile), tile)] = paired(*halves)

    def third(rows):
        live = (tags[rows, 3:4] < 12).astype(FULL)
        dec_out[rows, :] = (y_ref[rows, :] * live).astype(LOW)
        gv, dgain, dshift = norm_back(ga_ref[rows, :], x1_ref[rows, :], gains[2:3])
        gx1 = out_grad[rows, :].astype(FULL) * live + gv
        x1_ref[rows, :] = gx1
        low_a[rows, :] = gx1.astype(LOW)
        sums[2:3, :] += dgain
        sums[3:4, :] += dshift

    each(third)
    for j in range(2):
        goT[j * tile : (j + 1) * tile, :] = dot_nt(w_out[j * tile : (j + 1) * tile, :], low_a[...])
    for j in range(2):
        half = dot(oT[...], low_a[:, j * tile : (j + 1) * tile])
        if j == 0:
            first_half = half
        else:
            d_out[...] = paired(first_half, half)

    attention_backward(ROWS, HEADS, 32, v_ref, qT, kT, goT, oT, e_ref, linv, mix, gtT)

    for j in range(3):
        lo = dot_nt(low_aT[...], gtT[j * tile : (j + 1) * tile, :])
        hi = dot_nt(low_aT[...], gtT[768 + j * tile : 768 + (j + 1) * tile, :])
        d_qkv[:, :, j * tile : (j + 1) * tile] = paired(lo, hi)
    for j in range(2):
        cols = slice(j * tile, (j + 1) * tile)
        y_ref[:, cols] = dot(w_qkv[cols, :], gtT[...]).T

    def fourth(rows):
        gv, dgain, dshift = norm_back(y_ref[rows, :], x_ref[rows, :], gains[0:1])
        gx = x1_ref[rows, :] + gv
        sums[0:1, :] += dgain
        sums[1:2, :] += dshift
        source = tags[rows, 0:1]
        sums[4:5, :] += jnp.sum(jnp.where(source < 0, gx, 0.0), axis=0, keepdims=True)
        low_a[rows, :] = gx.astype(LOW)
        lane = lax.broadcasted_iota(jnp.int32, (STEP, 256), 1)
        y_ref[rows, 0:256] = (lane == source).astype(FULL)

    each(fourth)
    pick = y_ref[:, 0:256].astype(LOW).T
    g_embedded[...] = dot(pick, low_a[...]).astype(LOW)
    vectors[...] = sums[...]


def decoder_call(embedded, tags, sines_high, sines_low, mask_token, gains, w_qkv, w_out, w_up, w_down, out_grad):
    vmem = pl.BlockSpec(memory_space=pltpu.VMEM)
    low = lambda *shape: pltpu.VMEM(shape, LOW)
    full = lambda *shape: pltpu.VMEM(shape, FULL)
    return pl.pallas_call(
        decoder_kernel,
        out_shape=[
            jax.ShapeDtypeStruct((ROWS, DD), LOW),
            jax.ShapeDtypeStruct((256, DD), LOW),
            jax.ShapeDtypeStruct((64, 16, 768), LOW),
            jax.ShapeDtypeStruct((64, 16, 256), LOW),
            jax.ShapeDtypeStruct((64, 16, 1024), LOW),
            jax.ShapeDtypeStruct((DFF, DD), LOW),
            jax.ShapeDtypeStruct((8, DD), FULL),
        ],
        in_specs=[vmem] * 11,
        out_specs=[vmem] * 7,
        scratch_shapes=[
            full(ROWS, DD), low(ROWS, DD), low(DD, ROWS), low(ROWS, DD), low(ROWS, DD),
            low(DD, ROWS), low(DD, ROWS), low(DD, ROWS), low(HEADS, ROWS, ROWS), low(DD, ROWS),
            full(HEADS, ROWS), full(ROWS, DD), low(ROWS, DD), full(ROWS, DD), full(ROWS, DD),
            full(DD, ROWS), low(3 * DD, ROWS), low(256, ROWS), low(ROWS, 128), low(128, ROWS), full(8, DD),
        ],
        compiler_params=pltpu.CompilerParams(vmem_limit_bytes=63 * 1024 * 1024),
        name="decoder",
    )(embedded, tags, sines_high, sines_low, mask_token, gains, w_qkv, w_out, w_up, w_down, out_grad)


def wave_tables():
    quarter = DD // 4
    frequency = np.exp(np.arange(quarter, dtype=np.float32) * np.float32(-math.log(10000.0) / quarter)).astype(np.float32)
    places = np.zeros((128, 1), np.float32)
    for f, factor in enumerate((0.5, 1.0, 2.0, 4.0)):
        places[f * 28 : f * 28 + 28, 0] = np.arange(28, dtype=np.float32) * factor
    angle = (places * frequency[None, :]).astype(np.float32).astype(np.float64)
    waves = np.concatenate([np.sin(angle), np.cos(angle)], axis=1)
    waves[112:] = 0.0
    high = jnp.asarray(waves, FULL).astype(LOW)
    low = (jnp.asarray(waves, FULL) - high.astype(FULL)).astype(LOW)
    return high, low


ER, ED, EF = 256, 1024, 4096
EH = 64


def encoder_forward_kernel(
    arrived, tags, gains, w_qkv_h, w_out_h, w_up_h, w_down_h, w_embed_h,
    encoded_h, embedded_h, x1_h, m_h, slope_h, qT_h, kT_h, v_h, e_h, linv_h, oT_h,
    w_qkv, w_out, w_up, w_down, w_embed,
    encoded, embedded, x1, m_ref, slope_ref, qT, kT, v_ref, e_ref, linv, oT,
    x_ref, low_a, k_ref, vT, mix, ones_ref, far_ref, y_ref, in_sem, out_sem,
):
    loads = []
    for i, (source, target) in enumerate(
        ((w_qkv_h, w_qkv), (w_out_h, w_out), (w_up_h, w_up), (w_down_h, w_down), (w_embed_h, w_embed))
    ):
        copy = pltpu.make_async_copy(source, target, in_sem.at[i])
        copy.start()
        loads.append(copy)
    stores = []

    def keep(source, target):
        copy = pltpu.make_async_copy(source, target, out_sem.at[len(stores)])
        copy.start()
        stores.append(copy)

    tag = tags[...]
    lane = lax.broadcasted_iota(jnp.int32, (ROWS, 256), 1)
    small = lax.broadcasted_iota(jnp.int32, (ROWS, 128), 1)
    pick = (lane == tag[:, 0:1]).astype(FULL).T.astype(LOW)
    items = dot(pick, (small == tag[:, 3:4]).astype(LOW))
    slot = lax.broadcasted_iota(jnp.int32, (ER, 128), 1)
    empty = jnp.sum(items, axis=1, keepdims=True) < 0.5
    items = jnp.where((slot == 13) & empty, 1.0, items)
    ones_ref[...] = items.astype(LOW)
    far_ref[...] = jnp.where((items > 0.5) | (slot > 13), 0.0, FAR).T.astype(LOW)

    x = arrived[...].astype(FULL)
    x_ref[...] = x
    low_a[...] = (norm_parts(x)[0] * gains[0:1] + gains[1:2]).astype(LOW)
    loads[0].wait()

    tile = 256

    @pl.loop(0, ED // tile)
    def _(j):
        cols = pl.ds(pl.multiple_of(j * tile, tile), tile)
        t = dot(low_a[...], w_qkv[:, cols]) * (EH**-0.5 / LN2)
        qT[cols, :] = t.T.astype(LOW)
        t = dot(low_a[...], w_qkv[:, pl.ds(pl.multiple_of(ED + j * tile, tile), tile)])
        k_ref[:, cols] = t.astype(LOW)
        kT[cols, :] = t.T.astype(LOW)
        t = dot(low_a[...], w_qkv[:, pl.ds(pl.multiple_of(2 * ED + j * tile, tile), tile)])
        v_ref[:, cols] = t.astype(LOW)
        vT[cols, :] = t.T.astype(LOW)

    keep(qT, qT_h)
    keep(kT, kT_h)
    keep(v_ref, v_h)
    attention_forward(ER, HEADS, EH, k_ref, ones_ref, far_ref, qT, vT, mix, e_ref, oT, linv)
    keep(e_ref, e_h)
    keep(linv, linv_h)
    keep(oT, oT_h)
    low_a[...] = oT[...].T
    loads[1].wait()

    @pl.loop(0, ED // tile)
    def _(j):
        cols = pl.ds(pl.multiple_of(j * tile, tile), tile)
        x1[:, cols] = x_ref[:, cols] + dot(low_a[...], w_out[:, cols])

    keep(x1, x1_h)
    branch = x1[...]
    low_a[...] = (norm_parts(branch)[0] * gains[2:3] + gains[3:4]).astype(LOW)
    y_ref[...] = branch
    loads[2].wait()
    loads[3].wait()

    @pl.loop(0, EF // 512)
    def _(j):
        cols = pl.ds(pl.multiple_of(j * 512, 512), 512)
        m, slope = gelu_parts(dot(low_a[...], w_up[:, cols]))
        m = m.astype(LOW)
        m_ref[:, cols] = m
        slope_ref[:, cols] = slope.astype(LOW)
        y_ref[...] += dot(m, w_down[cols, :])

    keep(m_ref, m_h)
    keep(slope_ref, slope_h)
    encoded[...] = y_ref[...].astype(LOW)
    keep(encoded, encoded_h)
    loads[4].wait()
    embedded[...] = dot(encoded[...], w_embed[...])
    keep(embedded, embedded_h)
    for copy in stores:
        copy.wait()


ANY = pl.BlockSpec(memory_space=pl.ANY)
VMEM = pl.BlockSpec(memory_space=pltpu.VMEM)
WEIGHTS = [((ED, 3 * ED), LOW), ((ED, ED), LOW), ((ED, EF), LOW), ((EF, ED), LOW), ((ED, DD), LOW)]
KEPT = [
    ((ER, ED), LOW), ((ER, DD), FULL), ((ER, ED), FULL), ((ER, EF), LOW), ((ER, EF), LOW),
    ((ED, ER), LOW), ((ED, ER), LOW), ((ER, ED), LOW), ((HEADS, ER, ER), LOW), ((HEADS, ER), FULL), ((ED, ER), LOW),
]


def encoder_forward_call(arrived, tags, gains, w_qkv, w_out, w_up, w_down, w_embed):
    scratch = [pltpu.VMEM(*s) for s in WEIGHTS + KEPT]
    scratch += [
        pltpu.VMEM((ER, ED), FULL), pltpu.VMEM((ER, ED), LOW), pltpu.VMEM((ER, ED), LOW), pltpu.VMEM((ED, ER), LOW),
        pltpu.VMEM((256, ER), LOW), pltpu.VMEM((ER, 128), LOW), pltpu.VMEM((128, ER), LOW), pltpu.VMEM((ER, ED), FULL),
        pltpu.SemaphoreType.DMA((5,)), pltpu.SemaphoreType.DMA((len(KEPT),)),
    ]
    return pl.pallas_call(
        encoder_forward_kernel,
        out_shape=[jax.ShapeDtypeStruct(*s) for s in KEPT],
        in_specs=[VMEM] * 3 + [ANY] * 5,
        out_specs=[ANY] * len(KEPT),
        scratch_shapes=scratch,
        compiler_params=pltpu.CompilerParams(vmem_limit_bytes=60 * 1024 * 1024),
        name="encoder_forward",
    )(arrived, tags, gains, w_qkv, w_out, w_up, w_down, w_embed)


MESH = pl.DeviceIdType.MESH
LANES = 128
STREAMS = 6
COUNTS = ((2, 2, 2, 2, 2, 2), (3, 3, 3, 3, 3, 3), (3, 3, 3, 3, 2, 2), (3, 3, 3, 3, 3, 2))
DEC_SOURCES = ((16, 768), (16, 256), (16, 1024), (32, 512))
WORK_OF = (0, 1, 2, 0)
STAGE_OF = (None, 0, 1, 0)
WORK_TILES = ((3, 3, 3, 3, 3, 2), (3, 3, 3, 3, 3, 3), (3, 3, 3, 3, 2, 2))
SLOT_TILES = ((3, 3, 3, 3, 2, 2), (3, 3, 3, 3, 3, 3))
LEVEL_SHAPES = ((2, 4, 4), (4, 4), (2, 4), (4,), (2,), ())
FIRST_TILE = (0, 12, 30, 46)
TILES = 63
VECTOR_TILE = 62


def seat(c, tile):
    for s, many in enumerate(COUNTS[c]):
        if tile < many:
            return s, tile
        tile -= many


def dec_pieces():
    found, tile = [], 0
    for source, (rows, columns) in enumerate(DEC_SOURCES):
        for r in range(rows // 16):
            for column in range(columns // (2 * LANES)):
                s, place = seat(0, tile)
                last = found[-1] if found else None
                if last and last[:3] == [s, source, r] and last[3] + last[4] == column:
                    last[4] += 1
                else:
                    found.append([s, source, r, column, 1, place])
                tile += 1
    return found


class Stream:
    def __init__(self, number):
        self.order = tuple((number + step) % 3 for step in range(3))
        self.swap = number >= 3

    def flip(self, p):
        return p + 1 - 2 * lax.rem(p, 2)

    def first(self, p):
        return 3 - p if self.swap else self.flip(p)

    def mate(self, p):
        return self.flip(p) if self.swap else 3 - p


class Reducer:
    def __init__(self, dec_sources, work, stage, landed, steps, final, send_sem, recv_sem, own_sem, credit, credits):
        self.dec_sources, self.work, self.stage = dec_sources, work, stage
        self.landed, self.steps, self.final = landed, steps, final
        self.send_sem, self.recv_sem, self.own_sem = send_sem, recv_sem, own_sem
        self.credit, self.credits = credit, credits
        self.section = lax.axis_index("section")
        self.batch = lax.axis_index("batch")
        batch = self.batch
        self.coords = (batch // 16, lax.rem(batch // 4, 4), lax.rem(batch, 4))
        self.sibling = (1 - self.section, batch)
        self.streams = [Stream(number) for number in range(STREAMS)]
        self.neighbours = []
        for axis in range(3):
            p = self.coords[axis]
            self.neighbours += [self.peer(axis, p + 1 - 2 * lax.rem(p, 2)), self.peer(axis, 3 - p)]
        self.count = 0
        self.arrivals, self.unsent, self.owns = {}, {}, {}

    def peer(self, axis, place):
        return (self.section, self.batch + (place - self.coords[axis]) * (16, 4, 1)[axis])

    def meet(self):
        barrier = pltpu.get_barrier_semaphore()
        partners = [self.sibling] + self.neighbours
        for partner in partners:
            pl.semaphore_signal(barrier, inc=1, device_id=partner, device_id_type=MESH)
        pl.semaphore_wait(barrier, len(partners))

    def send(self, source, target, device, key, chunk):
        number = self.count
        self.count += 1
        copy = pltpu.make_async_remote_copy(
            src_ref=source, dst_ref=target, send_sem=self.send_sem.at[number], recv_sem=self.recv_sem.at[number],
            device_id=device, device_id_type=MESH,
        )
        copy.start()
        self.unsent.setdefault(chunk, []).append(copy)
        self.arrivals.setdefault(key, []).append(copy)

    def arrive(self, key):
        for copy in self.arrivals.pop(key):
            copy.wait_recv()

    def sent(self, chunk):
        for copy in self.unsent.pop(chunk, []):
            copy.wait_send()

    def start_decoder(self):
        for number, (s, source, r, column, width, place) in enumerate(dec_pieces()):
            half = DEC_SOURCES[source][1] // 2
            rows = pl.ds(16 * r, 16)
            there = pl.ds(pl.multiple_of((1 - self.section) * half, LANES) + column * LANES, width * LANES)
            here = pl.ds(pl.multiple_of(self.section * half, LANES) + column * LANES, width * LANES)
            lanes = pl.ds(place * LANES, width * LANES)
            everything = (slice(None),) * 4
            self.send(
                self.dec_sources[source].at[:, :, :, rows, there],
                self.landed[0][s].at[(*everything, lanes)],
                self.sibling, (0, s, 0), 0,
            )
            own = pltpu.make_async_copy(
                self.dec_sources[source].at[:, :, :, rows, here],
                self.work[0][s].at[(*everything, lanes)],
                self.own_sem.at[number],
            )
            own.start()
            self.owns.setdefault(s, []).append(own)

    def swap(self, c):
        if c >= 2:
            pl.semaphore_wait(self.credit, 1)
        for s in range(STREAMS):
            lanes = slice(0, COUNTS[c][s] * LANES)
            index = (slice(None),) * 4 + (lanes,)
            self.send(
                self.stage[STAGE_OF[c]][s].at[index], self.landed[c % 2][s].at[index], self.sibling, (c, s, 0), ("swap", c)
            )

    def terms(self, c, s, level, picks, extra=None, fresh=False):
        order = self.streams[s].order
        lanes = slice(0, COUNTS[c][s] * LANES)
        index = (*[picks.get(a, slice(None)) for a in range(3)], slice(None), lanes)
        found = [(self.work[WORK_OF[c]][s], index)]
        if fresh:
            found.append((self.landed[c % 2][s], index))
        steps = self.steps[c % 2]
        for lower in range(level + (extra is not None)):
            later = [picks.get(a, slice(None)) for a in sorted(order[lower + 1 :])]
            if lower == level:
                found.append((steps[2 * lower][s], (extra, *later, slice(None), lanes)))
            else:
                found.append((steps[2 * lower][s], (0, *later, slice(None), lanes)))
                found.append((steps[2 * lower + 1][s], (*later, slice(None), lanes)))
        return found

    def total(self, found):
        values = [ref[index].astype(FULL) for ref, index in found]
        while len(values) > 1:
            values = [a + b for a, b in zip(values[::2], values[1::2])] + ([values[-1]] if len(values) % 2 else [])
        return values[0]

    def settle(self, c, s, level, picks, **kind):
        free = sorted(self.streams[s].order[level + 1 :])

        def write(inner):
            found = self.terms(c, s, level, inner, **kind)
            ref, index = found[0]
            ref[index] = self.total(found).astype(LOW)

        if len(free) == 2:

            @pl.loop(0, 4)
            def _(i):
                write({**picks, free[0]: i})
        else:
            write(picks)

    def region(self, c, s, picks):
        lanes = slice(0, COUNTS[c][s] * LANES)
        return self.work[WORK_OF[c]][s].at[(*[picks.get(a, slice(None)) for a in range(3)], slice(None), lanes)]

    def place_in(self, c, s, step, *first):
        lanes = slice(0, COUNTS[c][s] * LANES)
        later = len(LEVEL_SHAPES[step]) - len(first)
        return self.steps[c % 2][step][s].at[(*first, *[slice(None)] * later, slice(None), lanes)]

    def halve_a(self, c, level):
        if level == 0 and c >= 2:
            for i in range(6):
                pl.semaphore_wait(self.credits.at[i], 1)
        for s, stream in enumerate(self.streams):
            axis = stream.order[level]
            me = self.coords[axis]
            other = stream.first(me)
            done = {a: self.coords[a] for a in stream.order[:level]}
            if level == 0:
                if c == 0:
                    for own in self.owns.pop(s):
                        own.wait()
                self.arrive((c, s, 0))
            else:
                self.arrive((c, s, ("b", level - 1)))
            for slab, place in ((1, stream.mate(other)), (0, other)):
                picks = {**done, axis: place}
                self.settle(c, s, level, picks, fresh=level == 0)
                self.send(
                    self.region(c, s, picks), self.place_in(c, s, 2 * level, slab), self.peer(axis, other), (c, s, ("a", level, slab)), c
                )
        if level == 0:
            for s, stream in enumerate(self.streams):
                axis = stream.order[0]
                me = self.coords[axis]
                for place in (stream.mate(me), me):
                    self.settle(c, s, 0, {axis: place}, fresh=True)
            if c + 2 < len(COUNTS):
                pl.semaphore_signal(self.credit, inc=1, device_id=self.sibling, device_id_type=MESH)

    def halve_b(self, c, level):
        for s, stream in enumerate(self.streams):
            axis = stream.order[level]
            other = stream.mate(self.coords[axis])
            picks = {**{a: self.coords[a] for a in stream.order[:level]}, axis: other}
            self.arrive((c, s, ("a", level, 1)))
            self.settle(c, s, level, picks, extra=1)
            self.send(self.region(c, s, picks), self.place_in(c, s, 2 * level + 1), self.peer(axis, other), (c, s, ("b", level)), c)
            self.arrive((c, s, ("a", level, 0)))

    def finish(self, c):
        first = FIRST_TILE[c]
        for s in range(STREAMS):
            self.arrive((c, s, ("b", 2)))
            value = self.total(self.terms(c, s, 3, dict(enumerate(self.coords))))
            for place in range(COUNTS[c][s]):
                self.final[self.section, first + place] = value[:, place * LANES : (place + 1) * LANES]
            first += COUNTS[c][s]
        region = self.final.at[self.section, pl.ds(FIRST_TILE[c], sum(COUNTS[c]))]
        self.send(region, region, self.sibling, (c, "final"), c)
        if c + 2 < len(COUNTS):
            for i, neighbour in enumerate(self.neighbours):
                pl.semaphore_signal(self.credits.at[i], inc=1, device_id=neighbour, device_id_type=MESH)

    def put(self, buffers, c, tile, index, value):
        s, place = seat(c, tile)
        buffers[s][(*index, slice(None), slice(place * LANES, (place + 1) * LANES))] = value.astype(LOW)

    def put_columns(self, buffers, c, tile, value):
        for t in range(value.shape[1] // LANES):
            piece = value[:, t * LANES : (t + 1) * LANES].reshape(4, 4, 4, 16, LANES)
            self.put(buffers, c, tile + t, (slice(None),) * 3, piece)


UP_SLOTS, DOWN_SLOTS, KEPT_SLOTS = 4, 3, 3


def backward_kernel(
    g_embedded, arrived, gains, dec_vectors, w_qkv_h, w_out_h, w_up_h, w_down_h, w_embed_h,
    encoded_h, x1_h, m_h, slope_h, qT_h, kT_h, v_h, e_h, linv_h, oT_h, dec0, dec1, dec2, dec3,
    received, shares_h, *refs,
):
    refs = list(refs)
    take = lambda n: [refs.pop(0) for _ in range(n)]
    up_ring, down_ring, m_ring, slope_ring = take(4)
    encoded, x1, qT, kT, v_ref, e_ref, linv, oT = take(8)
    gy, gz, ga_ref, aT, goT, gtT, mix = take(7)
    work = [take(STREAMS) for _ in range(3)]
    stage = [take(STREAMS) for _ in range(2)]
    landed = [take(STREAMS) for _ in range(2)]
    steps = [[take(STREAMS) for _ in range(6)] for _ in range(2)]
    final, send_sem, recv_sem, own_sem, credit, credits, in_sem, ring_sem, out_sem = take(9)

    red = Reducer([dec0, dec1, dec2, dec3], work, stage, landed, steps, final, send_sem, recv_sem, own_sem, credit, credits)
    section = red.section

    loads = {}

    def load(name, source, target, number):
        copy = pltpu.make_async_copy(source, target, in_sem.at[number])
        copy.start()
        loads[name] = copy

    def tile_of(i):
        return (1 - section) * 4 + i if i < 4 else section * 4 + i - 4

    def columns(j):
        return pl.ds(pl.multiple_of(j * 512, 512), 512)

    up_items = [lambda: w_embed_h]
    up_items += [functools.partial(lambda i: w_up_h.at[:, columns(tile_of(i))], i) for i in range(8)]
    up_items += [functools.partial(lambda i: w_out_h.at[:, pl.ds(i * 512, 512)], i) for i in range(2)]
    up_items += [functools.partial(lambda i: w_qkv_h.at[:, pl.ds(i * 512, 512)], i) for i in range(6)]
    rings = {
        "up": (up_ring, UP_SLOTS, up_items, 0),
        "down": (down_ring, DOWN_SLOTS, [functools.partial(lambda i: w_down_h.at[columns(tile_of(i)), :], i) for i in range(8)], 4),
        "m": (m_ring, KEPT_SLOTS, [functools.partial(lambda i: m_h.at[:, columns(tile_of(i))], i) for i in range(8)], 7),
        "slope": (slope_ring, KEPT_SLOTS, [functools.partial(lambda i: slope_h.at[:, columns(tile_of(i))], i) for i in range(8)], 10),
    }
    flying = {name: [] for name in rings}
    issued = {name: 0 for name in rings}

    def fetch(name):
        ring, slots, items, base = rings[name]
        i = issued[name]
        if i < len(items):
            copy = pltpu.make_async_copy(items[i](), ring.at[i % slots], ring_sem.at[base + i % slots])
            copy.start()
            flying[name].append((copy, i % slots))
            issued[name] += 1

    def grab(name):
        copy, slot = flying[name].pop(0)
        copy.wait()
        return rings[name][0].at[slot]

    fetch("up")
    load("encoded", encoded_h, encoded, 0)
    load("x1", x1_h, x1, 1)
    for name in ("down", "slope", "up", "m"):
        fetch(name)
    red.meet()
    red.start_decoder()
    for name in ("down", "slope", "up", "m"):
        fetch(name)
    for number, (name, source, target) in enumerate(
        (("oT", oT_h, oT), ("e", e_h, e_ref), ("linv", linv_h, linv), ("v", v_h, v_ref), ("kT", kT_h, kT), ("qT", qT_h, qT))
    ):
        load(name, source, target, 2 + number)

    w_embed = grab("up")
    gy[...] = dot_nt(g_embedded[...], w_embed[...])
    gz[...] = gy[...].astype(LOW)
    fetch("up")
    loads["encoded"].wait()
    encodedT = encoded[...].T
    for buffers, half in ((stage[0], 1 - section), (work[1], section)):
        red.put_columns(buffers, 1, 0, dot(encodedT, g_embedded[:, pl.ds(pl.multiple_of(half * 256, 256), 256)]))
    loads["x1"].wait()
    aT[...] = (norm_parts(x1[...])[0] * gains[2:3] + gains[3:4]).T.astype(LOW)

    for i in range(8):
        if i:
            for name in ("up", "down", "m", "slope"):
                fetch(name)
        w_down, slope, w_up, m = grab("down"), grab("slope"), grab("up"), grab("m")
        gm = dot_nt(gz[...], w_down[...])
        gu = (gm * slope[...].astype(FULL)).astype(LOW)
        part = dot_nt(gu, w_up[...])
        ga_ref[...] = part if i == 0 else ga_ref[...] + part
        for t in range(2):
            red.put_columns(
                stage[0] if i < 4 else work[1], 1, 2 + 4 * (i % 4) + 2 * t, dot(aT[...], gu[:, 256 * t : 256 * t + 256])
            )
        mT = m[...].T
        z = (1 - section) * 2 + i // 2 if i < 4 else section * 2 + (i - 4) // 2
        x = 2 * (i % 2)
        for buffers, half in ((stage[1], 1 - section), (work[2], section)):
            value = dot(mT, gz[:, pl.ds(pl.multiple_of(half * 512, 512), 512)]).reshape(8, 4, 16, 512)
            for r in range(4):
                for t in range(4):
                    piece = value[:, r, :, t * LANES : (t + 1) * LANES].reshape(2, 4, 16, LANES)
                    red.put(buffers, 2, 4 * r + t, (z, slice(x, x + 2), slice(None)), piece)
        if i == 1:
            red.halve_a(0, 0)
        if i == 3:
            red.swap(1)
        if i == 4:
            red.halve_b(0, 0)
        if i == 6:
            red.halve_a(0, 1)
    red.halve_b(0, 1)
    red.halve_a(1, 0)
    red.swap(2)

    gv, mlp_gain, mlp_shift = norm_back(ga_ref[...], x1[...], gains[2:3])
    gx1 = gy[...] + gv
    gy[...] = gx1
    gz[...] = gx1.astype(LOW)
    fetch("up")
    loads["oT"].wait()
    for k in range(2):
        w_out = grab("up")
        part = dot_nt(w_out[...], gz[:, 512 * k : 512 * k + 512])
        goT[...] = part if k == 0 else goT[...] + part
        fetch("up")
    red.halve_a(0, 2)
    red.halve_b(0, 2)
    red.finish(0)
    red.sent(0)
    red.sent(("swap", 1))
    for buffers, half in ((stage[0], 1 - section), (work[0], section)):
        for t in range(2):
            cols = pl.ds(pl.multiple_of(half * 512, 512) + 256 * t, 256)
            red.put_columns(buffers, 3, 2 * t, dot(oT[...], gz[:, cols]))
    x = arrived[...].astype(FULL)
    aT[...] = (norm_parts(x)[0] * gains[0:1] + gains[1:2]).T.astype(LOW)
    for name in ("e", "linv", "v", "kT", "qT"):
        loads[name].wait()
    mix[...] = jnp.zeros_like(mix)

    def between(g):
        if g == 1:
            red.halve_b(1, 0)
        if g == 3:
            red.halve_a(2, 0)
        if g == 5:
            red.halve_a(1, 1)
        if g == 6:
            red.halve_b(1, 1)

    attention_backward(ER, HEADS, EH, v_ref, qT, kT, goT, oT, e_ref, linv, mix, gtT, between)
    red.halve_b(2, 0)
    red.halve_a(1, 2)

    for k in range(6):
        w_qkv = grab("up")
        part = dot(w_qkv[...], gtT[512 * k : 512 * k + 512, :])
        goT[...] = part if k == 0 else goT[...] + part
        fetch("up")
    ga_ref[...] = goT[...].T
    red.halve_b(1, 2)
    gv, attn_gain, attn_shift = norm_back(ga_ref[...], arrived[...].astype(FULL), gains[0:1])
    received[...] = (gy[...] + gv).astype(LOW)
    for g in range(8):
        lanes = slice(g * LANES, (g + 1) * LANES)
        narrow = slice(g // 2 * LANES, (g // 2 + 1) * LANES)
        rows = [vector[:, lanes] for vector in (attn_gain, attn_shift, mlp_gain, mlp_shift)]
        rows += [dec_vectors[0:5, narrow], jnp.zeros((7, LANES), FULL)]
        value = jnp.broadcast_to(jnp.concatenate(rows, axis=0)[None, None], (2, 4, 16, LANES))
        index = (g // 2, slice(2 * (g % 2), 2 * (g % 2) + 2), slice(None))
        for buffers in (stage[0], work[0]):
            red.put(buffers, 3, 16, index, value)
    for k in range(6):
        rows = pl.ds(pl.multiple_of((1 - section) * 1536, 256) + 256 * k, 256)
        red.put_columns(stage[0], 3, 4 + 2 * k, dot_nt(aT[...], gtT[rows, :]))
    red.swap(3)
    red.finish(1)
    for k in range(6):
        rows = pl.ds(pl.multiple_of(section * 1536, 256) + 256 * k, 256)
        red.put_columns(work[0], 3, 4 + 2 * k, dot_nt(aT[...], gtT[rows, :]))
    red.halve_a(2, 1)
    red.halve_a(3, 0)
    red.halve_b(2, 1)
    red.halve_a(2, 2)
    red.halve_b(3, 0)
    red.halve_b(2, 2)
    red.finish(2)
    red.halve_a(3, 1)
    red.halve_b(3, 1)
    red.halve_a(3, 2)
    red.halve_b(3, 2)
    red.finish(3)
    for c in range(4):
        red.arrive((c, "final"))
    out = pltpu.make_async_copy(final, shares_h, out_sem)
    out.start()
    for chunk in list(red.unsent):
        red.sent(chunk)
    out.wait()


def backward_call(g_embedded, arrived, gains, dec_vectors, weights, kept, dec_grads):
    encoded, _, x1, m, slope, qT, kT, v, e, linv, oT = kept
    dec = [a.reshape(4, 4, 4, rows, columns) for a, (rows, columns) in zip(dec_grads, DEC_SOURCES)]
    vmem = pltpu.VMEM
    scratch = [
        vmem((UP_SLOTS, ED, 512), LOW), vmem((DOWN_SLOTS, 512, ED), LOW), vmem((KEPT_SLOTS, ER, 512), LOW), vmem((KEPT_SLOTS, ER, 512), LOW),
        vmem((ER, ED), LOW), vmem((ER, ED), FULL), vmem((ED, ER), LOW), vmem((ED, ER), LOW), vmem((ER, ED), LOW),
        vmem((HEADS, ER, ER), LOW), vmem((HEADS, ER), FULL), vmem((ED, ER), LOW),
        vmem((ER, ED), FULL), vmem((ER, ED), LOW), vmem((ER, ED), FULL), vmem((ED, ER), LOW), vmem((ED, ER), FULL),
        vmem((3 * ED, ER), LOW), vmem((256, ER), LOW),
    ]
    for tiles in WORK_TILES + (SLOT_TILES[1], SLOT_TILES[0]) + SLOT_TILES:
        scratch += [vmem((4, 4, 4, 16, n * LANES), LOW) for n in tiles]
    for tiles in SLOT_TILES:
        for shape in LEVEL_SHAPES:
            scratch += [vmem((*shape, 16, n * LANES), LOW) for n in tiles]
    copies = len(dec_pieces()) + 3 * STREAMS + 4 * 9 * STREAMS + 4
    dma = pltpu.SemaphoreType.DMA
    scratch += [
        vmem((2, TILES, 16, LANES), FULL), dma((copies,)), dma((copies,)), dma((len(dec_pieces()),)),
        pltpu.SemaphoreType.REGULAR, pltpu.SemaphoreType.REGULAR((6,)), dma((8,)), dma((13,)), dma,
    ]
    return pl.pallas_call(
        backward_kernel,
        out_shape=[jax.ShapeDtypeStruct((ER, ED), LOW), jax.ShapeDtypeStruct((2, TILES, 16, LANES), FULL)],
        in_specs=[VMEM] * 4 + [ANY] * 19,
        out_specs=[VMEM, ANY],
        scratch_shapes=scratch,
        compiler_params=pltpu.CompilerParams(collective_id=0, has_side_effects=True, vmem_limit_bytes=64 * 1024 * 1024 - 65536),
        name="encoder_backward_reduce",
    )(g_embedded, arrived, gains, dec_vectors, *weights, encoded, x1, m, slope, qT, kT, v, e, linv, oT, *dec)


SHARES = (
    ((8, 1536), 0, 0), ((8, 512), 0, 3), ((8, 2048), 0, 4), ((32, 512), 0, 8),
    ((16, 512), 1, 0), ((16, 4096), 1, 2), ((64, 1024), 2, 0), ((16, 1024), 3, 0), ((16, 3072), 3, 4),
)


def unpack_kernel(shares, *outs):
    for out, (shape, c, tile) in zip(outs, SHARES):
        number = FIRST_TILE[c] + tile
        rows, columns = shape
        packed = columns // 2 if rows == 8 else columns
        for r in range(max(rows // 16, 1)):
            for t in range(packed // (2 * LANES)):
                for half in range(2):
                    value = shares[half, number]
                    lane = half * packed // 2 + t * LANES
                    if rows == 8:
                        out[:, lane : lane + LANES] = value[:8]
                        out[:, packed + lane : packed + lane + LANES] = value[8:]
                    else:
                        out[16 * r : 16 * r + 16, lane : lane + LANES] = value
                number += 1
    vectors = outs[len(SHARES) :]
    batch = lax.axis_index("batch")
    value = shares[0, VECTOR_TILE]
    wide = pltpu.roll(value, lax.rem(128 - 16 * lax.rem(batch, 8), 128), axis=1)
    narrow = pltpu.roll(value, lax.rem(128 - 8 * lax.rem(batch, 16), 128), axis=1)
    for i in range(9):
        many = 16 if i < 4 else 8
        vectors[i][...] = (wide if i < 4 else narrow)[i, :many]


def unpack_call(shares):
    shapes = [jax.ShapeDtypeStruct(shape, FULL) for shape, _, _ in SHARES]
    shapes += [jax.ShapeDtypeStruct((16 if i < 4 else 8,), FULL) for i in range(9)]
    return pl.pallas_call(
        unpack_kernel,
        out_shape=shapes,
        in_specs=[VMEM],
        out_specs=[VMEM] * len(shapes),
        name="unpack_shares",
    )(shares)


def tag_table(lengths, visible, gsd_index):
    row = jnp.arange(ROWS, dtype=jnp.int32)
    ends = jnp.cumsum(lengths)
    segment = jnp.sum((row[:, None] >= ends[None]).astype(jnp.int32), axis=1)
    onehot = (segment[:, None] == jnp.arange(lengths.shape[0])[None]).astype(jnp.int32)
    offset = row - jnp.sum(onehot * (ends - lengths)[None], axis=1)
    length = jnp.sum(onehot * lengths[None], axis=1)
    factor = jnp.sum(onehot * gsd_index[None], axis=1)
    side = jnp.where(length == 64, 8, jnp.where(length == 196, 14, 28))
    live = segment < lengths.shape[0]
    row_tag = jnp.where(live, factor * 28 + offset // side, -1)
    column_tag = jnp.where(live, factor * 28 + offset % side, -1)
    rank = jnp.cumsum(visible) - 1
    source = jnp.where(visible == 1, rank % 128 * 2 + rank // 128, -1)
    return jnp.stack([source, row_tag, column_tag, segment], axis=1).astype(jnp.int32)


def per_device(
    patches, lengths, visible, gsd_index,
    enc_attn_gain, enc_attn_shift, enc_qkv, enc_out, enc_mlp_gain, enc_mlp_shift, enc_up, enc_down,
    dec_embed, mask_token,
    dec_attn_gain, dec_attn_shift, dec_qkv, dec_out, dec_mlp_gain, dec_mlp_shift, dec_up, dec_down,
    out_grad,
):
    both = ("section", "batch")
    arrived = lax.all_to_all(patches, both, split_axis=0, concat_axis=0, tiled=True)
    tags = tag_table(lengths[0], visible, gsd_index[0])
    enc_gains = jnp.stack([enc_attn_gain, enc_attn_shift, enc_mlp_gain, enc_mlp_shift])
    dec_gains = jnp.stack([dec_attn_gain, dec_attn_shift, dec_mlp_gain, dec_mlp_shift])
    weights = (enc_qkv, enc_out, enc_up, enc_down, dec_embed)
    kept = encoder_forward_call(arrived, tags, enc_gains, *weights)
    high, low = wave_tables()
    decoder = decoder_call(
        kept[1], tags, high, low, mask_token[None], dec_gains, dec_qkv, dec_out, dec_up, dec_down, out_grad
    )
    dec_output, g_embedded, *d_dec, dec_vectors = decoder
    received, shares = backward_call(g_embedded, arrived, enc_gains, dec_vectors, weights, kept, d_dec)
    patch_grad = lax.all_to_all(received, both, split_axis=0, concat_axis=0, tiled=True).astype(FULL)
    d_qkv, d_out, d_up, d_down, embed, up, down, out, qkv, *vectors = unpack_call(shares)
    gain1, shift1, gain2, shift2, dec_gain1, dec_shift1, dec_gain2, dec_shift2, mask = vectors
    return (
        dec_output, patch_grad, gain1, shift1, qkv, out, gain2, shift2, up, down, embed, mask,
        dec_gain1, dec_shift1, d_qkv, d_out, dec_gain2, dec_shift2, d_up, d_down,
    )


def solution(mesh):
    return jax.shard_map(
        per_device,
        mesh=mesh,
        in_specs=(
            P(("section", "batch"), None),
            P(("section", "batch"), None),
            P(("section", "batch")),
            P(("section", "batch"), None),
            P(),
            P(),
            P(),
            P(),
            P(),
            P(),
            P(),
            P(),
            P(),
            P(),
            P(),
            P(),
            P(),
            P(),
            P(),
            P(),
            P(),
            P(),
            P(("section", "batch"), None),
        ),
        out_specs=(
            P(("section", "batch"), None),
            P(("section", "batch"), None),
            P("batch"),
            P("batch"),
            P("batch", None),
            P("batch", None),
            P("batch"),
            P("batch"),
            P("batch", None),
            P("batch", None),
            P("batch", None),
            P("batch"),
            P("batch"),
            P("batch"),
            P("batch", None),
            P("batch", None),
            P("batch"),
            P("batch"),
            P("batch", None),
            P("batch", None),
        ),
        check_vma=False,
    )
```

```python
import functools
import math

import jax
import jax.numpy as jnp
import numpy as np
from jax import lax
from jax.experimental import pallas as pl
from jax.experimental.pallas import tpu as pltpu
from jax.sharding import PartitionSpec as P

LOW = jnp.bfloat16
FULL = jnp.float32
LN2 = math.log(2.0)
FAR = -1e30


def dot(a, b):
    return jnp.dot(a, b, preferred_element_type=FULL)


def dot_nt(a, b):
    return lax.dot_general(a, b, (((1,), (1,)), ((), ())), preferred_element_type=FULL)


def norm_parts(v):
    centred = v - jnp.mean(v, axis=-1, keepdims=True)
    r = lax.rsqrt(jnp.mean(centred * centred, axis=-1, keepdims=True) + 1e-6)
    return centred * r, r


def norm_back(gn, v, gain):
    vh, r = norm_parts(v)
    gg = gn * gain
    gv = r * (gg - jnp.mean(gg, axis=-1, keepdims=True) - vh * jnp.mean(gg * vh, axis=-1, keepdims=True))
    return gv, jnp.sum(gn * vh, axis=0, keepdims=True), jnp.sum(gn, axis=0, keepdims=True)


def gelu_parts(u):
    z = jnp.abs(u) * (0.3275911 / math.sqrt(2.0))
    t = 1.0 / (1.0 + z)
    poly = 1.061405429
    for c in (-1.453152027, 1.421413741, -0.284496736, 0.254829592):
        poly = poly * t + c
    bell = jnp.exp2(u * u * (-0.5 / LN2))
    tail = (0.5 * t) * poly * bell
    phi = jnp.where(u >= 0, 1.0 - tail, tail)
    return u * phi, phi + u * (bell * (1.0 / math.sqrt(2.0 * math.pi)))


def paired(a, b):
    w = a.shape[1]
    return jnp.concatenate([a.reshape(64, 8, w), b.reshape(64, 8, w)], axis=1).astype(LOW)


def blocks_of(total, size):
    cuts = list(range(0, total - size + 1, size))
    return [(c, (size if i + 1 < len(cuts) else total - c)) for i, c in enumerate(cuts)]


def attention_forward(rows, heads, hs, k_ref, ones_ref, far_ref, qT, vT, mix, e_ref, oT, linv):
    group = 128 // hs
    mix[...] = jnp.zeros_like(mix)
    mix[128:256, :] = far_ref[...]
    for g in range(heads // group):
        lanes = slice(128 * g, 128 * g + 128)
        left = jnp.concatenate([k_ref[:, lanes], ones_ref[...]], axis=1)
        for i in range(group):
            h = g * group + i
            feat = slice(h * hs, h * hs + hs)
            if i:
                mix[(i - 1) * hs : i * hs, :] = jnp.zeros((hs, rows), LOW)
            else:
                mix[128 - hs : 128, :] = jnp.zeros((hs, rows), LOW)
            mix[i * hs : i * hs + hs, :] = qT[feat, :]
            head_forward(rows, h, feat, left, vT, mix, e_ref, oT, linv)


def head_forward(rows, h, feat, left, vT, mix, e_ref, oT, linv):
    for first, many in blocks_of(rows, 256):
        cols = slice(first, first + many)
        s = dot(left, mix[:, cols])
        peak = jnp.max(s, axis=0, keepdims=True)
        e_ref[h, :, cols] = jnp.exp2(s - peak).astype(LOW)
    lhs = jnp.concatenate([vT[feat, :], jnp.ones((16, rows), LOW)], axis=0)
    o = dot(lhs, e_ref[h])
    hs = feat.stop - feat.start
    inverse = 1.0 / o[hs : hs + 1]
    linv[h : h + 1, :] = inverse
    oT[feat, :] = (o[:hs] * inverse).astype(LOW)


def attention_backward(rows, heads, hs, v_ref, qT, kT, goT, oT, e_ref, linv, mix, gtT, between=None):
    group = 128 // hs
    width = heads * hs
    scale = hs**-0.5
    for g in range(heads // group):
        lanes = slice(128 * g, 128 * g + 128)
        for i in range(group):
            h = g * group + i
            feat = slice(h * hs, h * hs + hs)
            go = goT[feat, :].astype(FULL) * linv[h : h + 1, :]
            low = go.astype(LOW)
            centre = jnp.sum(go * oT[feat, :].astype(FULL), axis=0, keepdims=True)
            if i:
                mix[(i - 1) * hs : i * hs, :] = jnp.zeros((hs, rows), LOW)
            else:
                mix[128 - hs : 128, :] = jnp.zeros((hs, rows), LOW)
            mix[i * hs : i * hs + hs, :] = low
            gtT[2 * width + h * hs : 2 * width + h * hs + hs, :] = dot_nt(low, e_ref[h]).astype(LOW)
            for first, many in blocks_of(rows, 256):
                cols = slice(first, first + many)
                gp = dot(v_ref[:, lanes], mix[0:128, cols])
                e_ref[h, :, cols] = (e_ref[h, :, cols].astype(FULL) * (gp - centre[:, cols])).astype(LOW)
            gs = e_ref[h]
            gtT[feat, :] = (dot(kT[feat, :], gs) * scale).astype(LOW)
            gtT[width + h * hs : width + h * hs + hs, :] = (dot_nt(qT[feat, :], gs) * LN2).astype(LOW)
        if between is not None:
            between(g)


ROWS, DD, DFF, HEADS = 784, 512, 2048, 16
STEP = 112


def decoder_kernel(
    embedded, tags, sines_high, sines_low, mask_token, gains, w_qkv, w_out, w_up, w_down, out_grad,
    dec_out, g_embedded, d_qkv, d_out, d_up, d_down, vectors,
    x_ref, low_a, low_aT, k_ref, v_ref, qT, kT, vT, e_ref, oT, linv, x1_ref, gz, ga_ref, y_ref, goT, gtT, mix, ones_ref, far_ref, sums,
):
    sums[...] = jnp.zeros_like(sums)
    tile = 256

    def each(body):
        @pl.loop(0, ROWS // STEP)
        def _(i):
            body(pl.ds(pl.multiple_of(i * STEP, STEP), STEP))

    wide = embedded[...]
    emb_high = wide.astype(LOW)
    emb_low = (wide - emb_high.astype(FULL)).astype(LOW)
    mask = mask_token[...].astype(FULL)

    def inputs(rows):
        tag = tags[rows, :]
        source, row_tag, column_tag, segment = (tag[:, i : i + 1] for i in range(4))
        lane = lax.broadcasted_iota(jnp.int32, (STEP, 256), 1)
        small = lax.broadcasted_iota(jnp.int32, (STEP, 128), 1)
        pick = (lane == source).astype(LOW)
        x = dot(pick, emb_high) + dot(pick, emb_low)
        x = jnp.where(source < 0, mask, x)
        row_pick = (small == row_tag).astype(LOW)
        column_pick = (small == column_tag).astype(LOW)
        row_wave = dot(row_pick, sines_high[...]) + dot(row_pick, sines_low[...])
        column_wave = dot(column_pick, sines_high[...]) + dot(column_pick, sines_low[...])
        x = x + jnp.concatenate([row_wave, column_wave], axis=1)
        x_ref[rows, :] = x
        low_a[rows, :] = (norm_parts(x)[0] * gains[0:1] + gains[1:2]).astype(LOW)
        same = small == segment
        ones_ref[rows, :] = same.astype(LOW)
        y_ref[rows, 0:128] = jnp.where(same | (small > 12), 0.0, FAR)
        live = (segment < 12).astype(FULL)
        gz[rows, :] = (out_grad[rows, :].astype(FULL) * live).astype(LOW)

    each(inputs)
    far_ref[...] = y_ref[:, 0:128].T.astype(LOW)
    low_aT[...] = low_a[...].T

    for j in range(2):
        t = dot(low_a[...], w_qkv[:, j * tile : (j + 1) * tile]) * (32**-0.5 / LN2)
        qT[j * tile : (j + 1) * tile, :] = t.astype(LOW).T
        t = dot(low_a[...], w_qkv[:, DD + j * tile : DD + (j + 1) * tile]).astype(LOW)
        k_ref[:, j * tile : (j + 1) * tile] = t
        kT[j * tile : (j + 1) * tile, :] = t.T
        t = dot(low_a[...], w_qkv[:, 2 * DD + j * tile : 2 * DD + (j + 1) * tile]).astype(LOW)
        v_ref[:, j * tile : (j + 1) * tile] = t
        vT[j * tile : (j + 1) * tile, :] = t.T

    attention_forward(ROWS, HEADS, 32, k_ref, ones_ref, far_ref, qT, vT, mix, e_ref, oT, linv)

    low_a[...] = oT[...].T
    for j in range(2):
        cols = slice(j * tile, (j + 1) * tile)
        x1_ref[:, cols] = x_ref[:, cols] + dot(low_a[...], w_out[:, cols])

    def second(rows):
        x1 = x1_ref[rows, :]
        low_a[rows, :] = (norm_parts(x1)[0] * gains[2:3] + gains[3:4]).astype(LOW)
        y_ref[rows, :] = x1
        ga_ref[rows, :] = jnp.zeros((STEP, DD), FULL)

    each(second)
    a2T = goT
    del a2T
    a2_t = low_a[...].T

    kT_keep = None
    del kT_keep
    gtT[0:DD, :] = a2_t

    @pl.loop(0, DFF // (2 * tile))
    def _(j):
        halves = []
        for half in range(2):
            cols = pl.ds(pl.multiple_of(j * tile + half * (DFF // 2), tile), tile)
            u = dot(low_a[...], w_up[:, cols])
            m, slope = gelu_parts(u)
            m = m.astype(LOW)
            y_ref[...] += dot(m, w_down[cols, :])
            gm = dot_nt(gz[...], w_down[cols, :])
            gu = (gm * slope).astype(LOW)
            ga_ref[...] += dot_nt(gu, w_up[:, cols])
            d_down[cols, :] = dot(m.T, gz[...]).astype(LOW)
            halves.append(dot(gtT[0:DD, :], gu))
        d_up[:, :, pl.ds(pl.multiple_of(j * tile, tile), tile)] = paired(*halves)

    def third(rows):
        live = (tags[rows, 3:4] < 12).astype(FULL)
        dec_out[rows, :] = (y_ref[rows, :] * live).astype(LOW)
        gv, dgain, dshift = norm_back(ga_ref[rows, :], x1_ref[rows, :], gains[2:3])
        gx1 = out_grad[rows, :].astype(FULL) * live + gv
        x1_ref[rows, :] = gx1
        low_a[rows, :] = gx1.astype(LOW)
        sums[2:3, :] += dgain
        sums[3:4, :] += dshift

    each(third)
    for j in range(2):
        goT[j * tile : (j + 1) * tile, :] = dot_nt(w_out[j * tile : (j + 1) * tile, :], low_a[...])
    for j in range(2):
        half = dot(oT[...], low_a[:, j * tile : (j + 1) * tile])
        if j == 0:
            first_half = half
        else:
            d_out[...] = paired(first_half, half)

    attention_backward(ROWS, HEADS, 32, v_ref, qT, kT, goT, oT, e_ref, linv, mix, gtT)

    for j in range(3):
        lo = dot_nt(low_aT[...], gtT[j * tile : (j + 1) * tile, :])
        hi = dot_nt(low_aT[...], gtT[768 + j * tile : 768 + (j + 1) * tile, :])
        d_qkv[:, :, j * tile : (j + 1) * tile] = paired(lo, hi)
    for j in range(2):
        cols = slice(j * tile, (j + 1) * tile)
        y_ref[:, cols] = dot(w_qkv[cols, :], gtT[...]).T

    def fourth(rows):
        gv, dgain, dshift = norm_back(y_ref[rows, :], x_ref[rows, :], gains[0:1])
        gx = x1_ref[rows, :] + gv
        sums[0:1, :] += dgain
        sums[1:2, :] += dshift
        source = tags[rows, 0:1]
        sums[4:5, :] += jnp.sum(jnp.where(source < 0, gx, 0.0), axis=0, keepdims=True)
        low_a[rows, :] = gx.astype(LOW)
        lane = lax.broadcasted_iota(jnp.int32, (STEP, 256), 1)
        y_ref[rows, 0:256] = (lane == source).astype(FULL)

    each(fourth)
    pick = y_ref[:, 0:256].astype(LOW).T
    g_embedded[...] = dot(pick, low_a[...]).astype(LOW)
    vectors[...] = sums[...]


def decoder_call(embedded, tags, sines_high, sines_low, mask_token, gains, w_qkv, w_out, w_up, w_down, out_grad):
    vmem = pl.BlockSpec(memory_space=pltpu.VMEM)
    low = lambda *shape: pltpu.VMEM(shape, LOW)
    full = lambda *shape: pltpu.VMEM(shape, FULL)
    return pl.pallas_call(
        decoder_kernel,
        out_shape=[
            jax.ShapeDtypeStruct((ROWS, DD), LOW),
            jax.ShapeDtypeStruct((256, DD), LOW),
            jax.ShapeDtypeStruct((64, 16, 768), LOW),
            jax.ShapeDtypeStruct((64, 16, 256), LOW),
            jax.ShapeDtypeStruct((64, 16, 1024), LOW),
            jax.ShapeDtypeStruct((DFF, DD), LOW),
            jax.ShapeDtypeStruct((8, DD), FULL),
        ],
        in_specs=[vmem] * 11,
        out_specs=[vmem] * 7,
        scratch_shapes=[
            full(ROWS, DD), low(ROWS, DD), low(DD, ROWS), low(ROWS, DD), low(ROWS, DD),
            low(DD, ROWS), low(DD, ROWS), low(DD, ROWS), low(HEADS, ROWS, ROWS), low(DD, ROWS),
            full(HEADS, ROWS), full(ROWS, DD), low(ROWS, DD), full(ROWS, DD), full(ROWS, DD),
            full(DD, ROWS), low(3 * DD, ROWS), low(256, ROWS), low(ROWS, 128), low(128, ROWS), full(8, DD),
        ],
        compiler_params=pltpu.CompilerParams(vmem_limit_bytes=63 * 1024 * 1024),
        name="decoder",
    )(embedded, tags, sines_high, sines_low, mask_token, gains, w_qkv, w_out, w_up, w_down, out_grad)


def wave_tables():
    quarter = DD // 4
    frequency = np.exp(np.arange(quarter, dtype=np.float32) * np.float32(-math.log(10000.0) / quarter)).astype(np.float32)
    places = np.zeros((128, 1), np.float32)
    for f, factor in enumerate((0.5, 1.0, 2.0, 4.0)):
        places[f * 28 : f * 28 + 28, 0] = np.arange(28, dtype=np.float32) * factor
    angle = (places * frequency[None, :]).astype(np.float32).astype(np.float64)
    waves = np.concatenate([np.sin(angle), np.cos(angle)], axis=1)
    waves[112:] = 0.0
    high = jnp.asarray(waves, FULL).astype(LOW)
    low = (jnp.asarray(waves, FULL) - high.astype(FULL)).astype(LOW)
    return high, low


ER, ED, EF = 256, 1024, 4096
EH = 64


def encoder_forward_kernel(
    arrived, tags, gains, w_qkv_h, w_out_h, w_up_h, w_down_h, w_embed_h,
    encoded_h, embedded_h, x1_h, m_h, slope_h, qT_h, kT_h, v_h, e_h, linv_h, oT_h,
    w_qkv, w_out, w_up, w_down, w_embed,
    encoded, embedded, x1, m_ref, slope_ref, qT, kT, v_ref, e_ref, linv, oT,
    x_ref, low_a, k_ref, vT, mix, ones_ref, far_ref, y_ref, in_sem, out_sem,
):
    loads = []
    for i, (source, target) in enumerate(
        ((w_qkv_h, w_qkv), (w_out_h, w_out), (w_up_h, w_up), (w_down_h, w_down), (w_embed_h, w_embed))
    ):
        copy = pltpu.make_async_copy(source, target, in_sem.at[i])
        copy.start()
        loads.append(copy)
    stores = []

    def keep(source, target):
        copy = pltpu.make_async_copy(source, target, out_sem.at[len(stores)])
        copy.start()
        stores.append(copy)

    tag = tags[...]
    lane = lax.broadcasted_iota(jnp.int32, (ROWS, 256), 1)
    small = lax.broadcasted_iota(jnp.int32, (ROWS, 128), 1)
    pick = (lane == tag[:, 0:1]).astype(FULL).T.astype(LOW)
    items = dot(pick, (small == tag[:, 3:4]).astype(LOW))
    slot = lax.broadcasted_iota(jnp.int32, (ER, 128), 1)
    empty = jnp.sum(items, axis=1, keepdims=True) < 0.5
    items = jnp.where((slot == 13) & empty, 1.0, items)
    ones_ref[...] = items.astype(LOW)
    far_ref[...] = jnp.where((items > 0.5) | (slot > 13), 0.0, FAR).T.astype(LOW)

    x = arrived[...].astype(FULL)
    x_ref[...] = x
    low_a[...] = (norm_parts(x)[0] * gains[0:1] + gains[1:2]).astype(LOW)
    loads[0].wait()

    tile = 256

    @pl.loop(0, ED // tile)
    def _(j):
        cols = pl.ds(pl.multiple_of(j * tile, tile), tile)
        t = dot(low_a[...], w_qkv[:, cols]) * (EH**-0.5 / LN2)
        qT[cols, :] = t.T.astype(LOW)
        t = dot(low_a[...], w_qkv[:, pl.ds(pl.multiple_of(ED + j * tile, tile), tile)])
        k_ref[:, cols] = t.astype(LOW)
        kT[cols, :] = t.T.astype(LOW)
        t = dot(low_a[...], w_qkv[:, pl.ds(pl.multiple_of(2 * ED + j * tile, tile), tile)])
        v_ref[:, cols] = t.astype(LOW)
        vT[cols, :] = t.T.astype(LOW)

    keep(qT, qT_h)
    keep(kT, kT_h)
    keep(v_ref, v_h)
    attention_forward(ER, HEADS, EH, k_ref, ones_ref, far_ref, qT, vT, mix, e_ref, oT, linv)
    keep(e_ref, e_h)
    keep(linv, linv_h)
    keep(oT, oT_h)
    low_a[...] = oT[...].T
    loads[1].wait()

    @pl.loop(0, ED // tile)
    def _(j):
        cols = pl.ds(pl.multiple_of(j * tile, tile), tile)
        x1[:, cols] = x_ref[:, cols] + dot(low_a[...], w_out[:, cols])

    keep(x1, x1_h)
    branch = x1[...]
    low_a[...] = (norm_parts(branch)[0] * gains[2:3] + gains[3:4]).astype(LOW)
    y_ref[...] = branch
    loads[2].wait()
    loads[3].wait()

    @pl.loop(0, EF // 512)
    def _(j):
        cols = pl.ds(pl.multiple_of(j * 512, 512), 512)
        m, slope = gelu_parts(dot(low_a[...], w_up[:, cols]))
        m = m.astype(LOW)
        m_ref[:, cols] = m
        slope_ref[:, cols] = slope.astype(LOW)
        y_ref[...] += dot(m, w_down[cols, :])

    keep(m_ref, m_h)
    keep(slope_ref, slope_h)
    encoded[...] = y_ref[...].astype(LOW)
    keep(encoded, encoded_h)
    loads[4].wait()
    embedded[...] = dot(encoded[...], w_embed[...])
    keep(embedded, embedded_h)
    for copy in stores:
        copy.wait()


ANY = pl.BlockSpec(memory_space=pl.ANY)
VMEM = pl.BlockSpec(memory_space=pltpu.VMEM)
WEIGHTS = [((ED, 3 * ED), LOW), ((ED, ED), LOW), ((ED, EF), LOW), ((EF, ED), LOW), ((ED, DD), LOW)]
KEPT = [
    ((ER, ED), LOW), ((ER, DD), FULL), ((ER, ED), FULL), ((ER, EF), LOW), ((ER, EF), LOW),
    ((ED, ER), LOW), ((ED, ER), LOW), ((ER, ED), LOW), ((HEADS, ER, ER), LOW), ((HEADS, ER), FULL), ((ED, ER), LOW),
]


def encoder_forward_call(arrived, tags, gains, w_qkv, w_out, w_up, w_down, w_embed):
    scratch = [pltpu.VMEM(*s) for s in WEIGHTS + KEPT]
    scratch += [
        pltpu.VMEM((ER, ED), FULL), pltpu.VMEM((ER, ED), LOW), pltpu.VMEM((ER, ED), LOW), pltpu.VMEM((ED, ER), LOW),
        pltpu.VMEM((256, ER), LOW), pltpu.VMEM((ER, 128), LOW), pltpu.VMEM((128, ER), LOW), pltpu.VMEM((ER, ED), FULL),
        pltpu.SemaphoreType.DMA((5,)), pltpu.SemaphoreType.DMA((len(KEPT),)),
    ]
    return pl.pallas_call(
        encoder_forward_kernel,
        out_shape=[jax.ShapeDtypeStruct(*s) for s in KEPT],
        in_specs=[VMEM] * 3 + [ANY] * 5,
        out_specs=[ANY] * len(KEPT),
        scratch_shapes=scratch,
        compiler_params=pltpu.CompilerParams(vmem_limit_bytes=60 * 1024 * 1024),
        name="encoder_forward",
    )(arrived, tags, gains, w_qkv, w_out, w_up, w_down, w_embed)


MESH = pl.DeviceIdType.MESH
LANES = 128
STREAMS = 6
COUNTS = ((2, 2, 2, 2, 2, 2), (3, 3, 3, 3, 3, 3), (3, 3, 3, 3, 2, 2), (3, 3, 3, 3, 3, 2))
DEC_SOURCES = ((16, 768), (16, 256), (16, 1024), (32, 512))
WORK_OF = (0, 1, 2, 0)
STAGE_OF = (None, 0, 1, 0)
WORK_TILES = ((3, 3, 3, 3, 3, 2), (3, 3, 3, 3, 3, 3), (3, 3, 3, 3, 2, 2))
SLOT_TILES = ((3, 3, 3, 3, 2, 2), (3, 3, 3, 3, 3, 3))
STEP_TILES = WORK_TILES
LEVEL_SHAPES = ((2, 4, 4), (4, 4), (2, 4), (4,), (2,), ())
FIRST_TILE = (0, 12, 30, 46)
TILES = 63
VECTOR_TILE = 62


def seat(c, tile):
    for s, many in enumerate(COUNTS[c]):
        if tile < many:
            return s, tile
        tile -= many


def dec_pieces():
    found, tile = [], 0
    for source, (rows, columns) in enumerate(DEC_SOURCES):
        for r in range(rows // 16):
            for column in range(columns // (2 * LANES)):
                s, place = seat(0, tile)
                last = found[-1] if found else None
                if last and last[:3] == [s, source, r] and last[3] + last[4] == column:
                    last[4] += 1
                else:
                    found.append([s, source, r, column, 1, place])
                tile += 1
    return found


class Stream:
    def __init__(self, number):
        self.order = tuple((number + step) % 3 for step in range(3))
        self.swap = number >= 3

    def flip(self, p):
        return p + 1 - 2 * lax.rem(p, 2)

    def first(self, p):
        return 3 - p if self.swap else self.flip(p)

    def mate(self, p):
        return self.flip(p) if self.swap else 3 - p


class Reducer:
    def __init__(self, dec_sources, work, parked, stage, landed, steps, final, send_sem, recv_sem, own_sem, credit, credits):
        self.dec_sources, self.work, self.parked, self.stage = dec_sources, work, parked, stage
        self.landed, self.steps, self.final = landed, steps, final
        self.send_sem, self.recv_sem, self.own_sem = send_sem, recv_sem, own_sem
        self.credit, self.credits = credit, credits
        self.section = lax.axis_index("section")
        self.batch = lax.axis_index("batch")
        batch = self.batch
        self.coords = (batch // 16, lax.rem(batch // 4, 4), lax.rem(batch, 4))
        self.sibling = (1 - self.section, batch)
        self.streams = [Stream(number) for number in range(STREAMS)]
        self.neighbours = []
        for axis in range(3):
            p = self.coords[axis]
            self.neighbours += [self.peer(axis, p + 1 - 2 * lax.rem(p, 2)), self.peer(axis, 3 - p)]
        self.count = 0
        self.arrivals, self.unsent, self.owns = {}, {}, {}

    def peer(self, axis, place):
        return (self.section, self.batch + (place - self.coords[axis]) * (16, 4, 1)[axis])

    def meet(self):
        barrier = pltpu.get_barrier_semaphore()
        partners = [self.sibling] + self.neighbours
        for partner in partners:
            pl.semaphore_signal(barrier, inc=1, device_id=partner, device_id_type=MESH)
        pl.semaphore_wait(barrier, len(partners))

    def send(self, source, target, device, key, chunk):
        number = self.count
        self.count += 1
        copy = pltpu.make_async_remote_copy(
            src_ref=source, dst_ref=target, send_sem=self.send_sem.at[number], recv_sem=self.recv_sem.at[number],
            device_id=device, device_id_type=MESH,
        )
        copy.start()
        self.unsent.setdefault(chunk, []).append(copy)
        self.arrivals.setdefault(key, []).append(copy)

    def arrive(self, key):
        for copy in self.arrivals.pop(key):
            copy.wait_recv()

    def sent(self, chunk):
        for copy in self.unsent.pop(chunk, []):
            copy.wait_send()

    def start_decoder(self):
        for number, (s, source, r, column, width, place) in enumerate(dec_pieces()):
            half = DEC_SOURCES[source][1] // 2
            rows = pl.ds(16 * r, 16)
            there = pl.ds(pl.multiple_of((1 - self.section) * half, LANES) + column * LANES, width * LANES)
            here = pl.ds(pl.multiple_of(self.section * half, LANES) + column * LANES, width * LANES)
            lanes = pl.ds(place * LANES, width * LANES)
            everything = (slice(None),) * 4
            self.send(
                self.dec_sources[source].at[:, :, :, rows, there],
                self.landed[0][s].at[(*everything, lanes)],
                self.sibling, (0, s, 0), ("swap", 0),
            )
            own = pltpu.make_async_copy(
                self.dec_sources[source].at[:, :, :, rows, here],
                self.work[0][s].at[(*everything, lanes)],
                self.own_sem.at[number],
            )
            own.start()
            self.owns.setdefault(s, []).append(own)

    def swap(self, c, streams=range(STREAMS)):
        if c >= 2 and streams[0] == 0:
            pl.semaphore_wait(self.credit, 1)
        for s in streams:
            lanes = slice(0, COUNTS[c][s] * LANES)
            index = (slice(None),) * 4 + (lanes,)
            self.send(
                self.stage[STAGE_OF[c]][s].at[index], self.landed[c % 2][s].at[index], self.sibling, (c, s, 0), ("swap", c)
            )

    def base(self, c, s, level, picks):
        lanes = slice(0, COUNTS[c][s] * LANES)
        if c == 0 and level:
            later = sorted(self.streams[s].order[1:])
            return self.parked[s], (*[picks.get(a, slice(None)) for a in later], slice(None), lanes)
        return self.work[WORK_OF[c]][s], (*[picks.get(a, slice(None)) for a in range(3)], slice(None), lanes)

    def terms(self, c, s, level, picks, extra=None, fresh=False, park=False):
        order = self.streams[s].order
        lanes = slice(0, COUNTS[c][s] * LANES)
        found = [self.base(c, s, 0 if park else level, picks)]
        if fresh:
            found.append((self.landed[c % 2][s], found[0][1]))
        steps = self.steps[c]
        for lower in range(1 if c == 0 and level and not park else 0, level + (extra is not None)):
            later = [picks.get(a, slice(None)) for a in sorted(order[lower + 1 :])]
            if lower == level:
                found.append((steps[2 * lower][s], (extra, *later, slice(None), lanes)))
            else:
                found.append((steps[2 * lower][s], (0, *later, slice(None), lanes)))
                found.append((steps[2 * lower + 1][s], (*later, slice(None), lanes)))
        return found

    def total(self, found):
        if len(found) == 2:
            return found[0][0][found[0][1]] + found[1][0][found[1][1]]
        values = [ref[index].astype(FULL) for ref, index in found]
        while len(values) > 1:
            values = [a + b for a, b in zip(values[::2], values[1::2])] + ([values[-1]] if len(values) % 2 else [])
        return values[0]

    def settle(self, c, s, level, picks, **kind):
        free = sorted(self.streams[s].order[level + 1 :])

        def write(inner):
            found = self.terms(c, s, level, inner, **kind)
            ref, index = self.base(c, s, level, inner)
            ref[index] = self.total(found).astype(LOW)

        if len(free) == 2:

            @pl.loop(0, 4)
            def _(i):
                write({**picks, free[0]: i})
        else:
            write(picks)

    def region(self, c, s, level, picks):
        ref, index = self.base(c, s, level, picks)
        return ref.at[index]

    def place_in(self, c, s, step, *first):
        lanes = slice(0, COUNTS[c][s] * LANES)
        later = len(LEVEL_SHAPES[step]) - len(first)
        return self.steps[c][step][s].at[(*first, *[slice(None)] * later, slice(None), lanes)]

    def halve_a(self, c, level, streams=range(STREAMS)):
        if level == 0 and c == 3 and streams[0] == 0:
            for i in range(6):
                pl.semaphore_wait(self.credits.at[i], 1)
        park = c == 0 and level == 1
        for s in streams:
            stream = self.streams[s]
            axis = stream.order[level]
            me = self.coords[axis]
            other = stream.first(me)
            done = {a: self.coords[a] for a in stream.order[:level]}
            if level == 0:
                if c == 0:
                    for own in self.owns.pop(s):
                        own.wait()
                self.arrive((c, s, 0))
            else:
                self.arrive((c, s, ("b", level - 1)))
            for slab, place in ((1, stream.mate(other)), (0, other)):
                picks = {**done, axis: place}
                self.settle(c, s, level, picks, fresh=level == 0, park=park)
                self.send(
                    self.region(c, s, level, picks), self.place_in(c, s, 2 * level, slab),
                    self.peer(axis, other), (c, s, ("a", level, slab)), (c, level),
                )
        if level == 0 or park:
            for s in streams:
                stream = self.streams[s]
                axis = stream.order[level]
                me = self.coords[axis]
                done = {a: self.coords[a] for a in stream.order[:level]}
                for place in (stream.mate(me), me):
                    self.settle(c, s, level, {**done, axis: place}, fresh=level == 0, park=park)
        if level == 0 and c < 3:
            pl.semaphore_signal(self.credit, inc=1, device_id=self.sibling, device_id_type=MESH)
        if park:
            for i, neighbour in enumerate(self.neighbours):
                pl.semaphore_signal(self.credits.at[i], inc=1, device_id=neighbour, device_id_type=MESH)

    def halve_b(self, c, level):
        for s, stream in enumerate(self.streams):
            axis = stream.order[level]
            other = stream.mate(self.coords[axis])
            picks = {**{a: self.coords[a] for a in stream.order[:level]}, axis: other}
            self.arrive((c, s, ("a", level, 1)))
            self.settle(c, s, level, picks, extra=1)
            self.send(
                self.region(c, s, level, picks), self.place_in(c, s, 2 * level + 1), self.peer(axis, other), (c, s, ("b", level)), (c, level)
            )
            self.arrive((c, s, ("a", level, 0)))

    def finish(self, c):
        first = FIRST_TILE[c]
        for s in range(STREAMS):
            self.arrive((c, s, ("b", 2)))
            value = self.total(self.terms(c, s, 3, dict(enumerate(self.coords))))
            for place in range(COUNTS[c][s]):
                self.final[self.section, first + place] = value[:, place * LANES : (place + 1) * LANES].astype(LOW)
            first += COUNTS[c][s]
        region = self.final.at[self.section, pl.ds(FIRST_TILE[c], sum(COUNTS[c]))]
        self.send(region, region, self.sibling, (c, "final"), "final")

    def put(self, buffers, c, tile, index, value):
        s, place = seat(c, tile)
        buffers[s][(*index, slice(None), slice(place * LANES, (place + 1) * LANES))] = value.astype(LOW)

    def put_columns(self, buffers, c, tile, value):
        for t in range(value.shape[1] // LANES):
            piece = value[:, t * LANES : (t + 1) * LANES].reshape(4, 4, 4, 16, LANES)
            self.put(buffers, c, tile + t, (slice(None),) * 3, piece)


UP_SLOTS, DOWN_SLOTS, KEPT_SLOTS = 3, 2, 2


def backward_kernel(
    g_embedded, arrived, gains, dec_vectors, w_qkv_h, w_out_h, w_up_h, w_down_h, w_embed_h,
    encoded_h, x1_h, m_h, slope_h, qT_h, kT_h, v_h, e_h, linv_h, oT_h, dec0, dec1, dec2, dec3,
    received_h, shares_h, *refs,
):
    refs = list(refs)
    take = lambda n: [refs.pop(0) for _ in range(n)]
    up_ring, down_ring, kept_ring = take(3)
    x1, qT, kT, v_ref, e_ref, linv, oT = take(7)
    gy, gz, ga_ref, aT, goT, gtT, mix = take(7)
    work = [take(STREAMS) for _ in range(3)]
    stage = [take(STREAMS) for _ in range(2)]
    landed = [take(STREAMS) for _ in range(2)]
    parked = take(STREAMS)
    large = [[take(STREAMS) for _ in range(2)] for _ in range(3)]
    steps = [large[WORK_OF[c]] + [take(STREAMS) for _ in range(4)] for c in range(4)]
    final, send_sem, recv_sem, own_sem, credit, credits, in_sem, ring_sem, out_sem = take(9)

    red = Reducer([dec0, dec1, dec2, dec3], work, parked, stage, landed, steps, final, send_sem, recv_sem, own_sem, credit, credits)
    section = red.section

    loads = {}

    def load(name, source, target, number):
        copy = pltpu.make_async_copy(source, target, in_sem.at[number])
        copy.start()
        loads[name] = copy

    def tile_of(i):
        return (1 - section) * 4 + i if i < 4 else section * 4 + i - 4

    def columns(j):
        return pl.ds(pl.multiple_of(j * 512, 512), 512)

    up_items = [lambda: w_embed_h]
    up_items += [functools.partial(lambda i: w_up_h.at[:, columns(tile_of(i))], i) for i in range(8)]
    up_items += [functools.partial(lambda i: w_out_h.at[:, pl.ds(i * 512, 512)], i) for i in range(2)]
    up_items += [functools.partial(lambda i: w_qkv_h.at[:, pl.ds(i * 512, 512)], i) for i in range(6)]
    rings = {
        "up": (up_ring, UP_SLOTS, up_items, 0),
        "down": (down_ring, DOWN_SLOTS, [functools.partial(lambda i: w_down_h.at[columns(tile_of(i)), :], i) for i in range(8)], 4),
        "kept": (
            kept_ring, KEPT_SLOTS,
            [functools.partial(lambda i: m_h.at[:, columns(i)], i) for i in range(8)]
            + [functools.partial(lambda i: slope_h.at[:, columns(tile_of(i))], i) for i in range(8)], 7,
        ),
    }
    flying = {name: [] for name in rings}
    issued = {name: 0 for name in rings}

    def fetch(name):
        ring, slots, items, base = rings[name]
        i = issued[name]
        if i < len(items):
            copy = pltpu.make_async_copy(items[i](), ring.at[i % slots], ring_sem.at[base + i % slots])
            copy.start()
            flying[name].append((copy, i % slots))
            issued[name] += 1

    def grab(name):
        copy, slot = flying[name].pop(0)
        copy.wait()
        return rings[name][0].at[slot]

    fetch("up")
    load("encoded", encoded_h, v_ref, 0)
    load("x1", x1_h, x1, 1)
    fetch("kept")
    red.meet()
    red.start_decoder()
    fetch("kept")
    for name in ("down", "up") * 2:
        fetch(name)
    for number, (name, source, target) in enumerate(
        (("oT", oT_h, oT), ("e", e_h, e_ref), ("linv", linv_h, linv), ("kT", kT_h, kT), ("qT", qT_h, qT))
    ):
        load(name, source, target, 2 + number)

    w_embed = grab("up")
    gy[...] = dot_nt(g_embedded[...], w_embed[...])
    gz[...] = gy[...].astype(LOW)
    fetch("up")
    loads["encoded"].wait()
    encodedT = v_ref[...].T
    for buffers, half in ((stage[0], 1 - section), (work[1], section)):
        red.put_columns(buffers, 1, 0, dot(encodedT, g_embedded[:, pl.ds(pl.multiple_of(half * 256, 256), 256)]))

    load("v", v_h, v_ref, 7)

    for i in range(8):
        mT = grab("kept")[...].T
        fetch("kept")
        for buffers, half in ((stage[0], 1 - section), (work[1], section)):
            value = dot(mT, gz[:, pl.ds(pl.multiple_of(half * 512, 512), 512)]).reshape(8, 4, 16, 512)
            for r in range(4):
                for t in range(4):
                    piece = value[:, r, :, t * LANES : (t + 1) * LANES].reshape(2, 4, 16, LANES)
                    red.put(buffers, 1, 2 + 4 * r + t, (i // 2, slice(2 * (i % 2), 2 * (i % 2) + 2), slice(None)), piece)
        if i == 5:
            red.halve_a(0, 0)
    red.swap(1)
    loads["x1"].wait()
    aT[...] = (norm_parts(x1[...])[0] * gains[2:3] + gains[3:4]).T.astype(LOW)

    for i in range(8):
        if i:
            for name in ("up", "down", "kept"):
                fetch(name)
        w_down, slope, w_up = grab("down"), grab("kept"), grab("up")
        gm = dot_nt(gz[...], w_down[...])
        gu = (gm * slope[...].astype(FULL)).astype(LOW)
        part = dot_nt(gu, w_up[...])
        ga_ref[...] = part if i == 0 else ga_ref[...] + part
        for t in range(2):
            red.put_columns(
                stage[1] if i < 4 else work[2], 2, 4 * (i % 4) + 2 * t, dot(aT[...], gu[:, 256 * t : 256 * t + 256])
            )
        if i == 1:
            red.halve_b(0, 0)
        if i == 3:
            red.swap(2)
            red.halve_a(0, 1)
            red.halve_a(1, 0)

    gv, mlp_gain, mlp_shift = norm_back(ga_ref[...], x1[...], gains[2:3])
    gx1 = gy[...] + gv
    gy[...] = gx1
    gz[...] = gx1.astype(LOW)
    fetch("up")
    loads["oT"].wait()
    w_out = [grab("up"), grab("up")]
    for k in range(2):
        rows = slice(512 * k, 512 * k + 512)
        goT[rows, :] = (dot_nt(w_out[0][rows, :], gz[:, 0:512]) + dot_nt(w_out[1][rows, :], gz[:, 512:1024])).astype(LOW)
    fetch("up")
    fetch("up")
    x = arrived[...].astype(FULL)
    aT[...] = (norm_parts(x)[0] * gains[0:1] + gains[1:2]).T.astype(LOW)
    for name in ("e", "linv", "v", "kT", "qT"):
        loads[name].wait()
    mix[...] = jnp.zeros_like(mix)

    def between(g):
        if g == 0:
            red.halve_b(1, 0)
        if g == 2:
            red.halve_a(2, 0)
        if g == 4:
            red.halve_b(0, 1)
        if g == 6:
            red.halve_a(1, 1)

    attention_backward(ER, HEADS, EH, v_ref, qT, kT, goT, oT, e_ref, linv, mix, gtT, between)

    def out_part(buffers, half):
        for t in range(2):
            cols = pl.ds(pl.multiple_of(half * 512, 512) + 256 * t, 256)
            red.put_columns(buffers, 3, 2 * t, dot(oT[...], gz[:, cols]))

    def qkv_part(buffers, half):
        for k in range(6):
            rows = pl.ds(pl.multiple_of(half * 1536, 256) + 256 * k, 256)
            red.put_columns(buffers, 3, 4 + 2 * k, dot_nt(aT[...], gtT[rows, :]))

    red.sent(("swap", 1))
    out_part(stage[0], 1 - section)
    qkv_part(stage[0], 1 - section)
    red.swap(3, range(5))
    red.sent((0, 0))
    out_part(work[0], section)
    qkv_part(work[0], section)
    red.halve_b(2, 0)
    red.halve_a(3, 0, range(5))

    for k in range(6):
        w_qkv = grab("up")
        part = dot_nt(gtT[512 * k : 512 * k + 512, :].T, w_qkv[...])
        ga_ref[...] = part if k == 0 else ga_ref[...] + part
        fetch("up")
    gv, attn_gain, attn_shift = norm_back(ga_ref[...], arrived[...].astype(FULL), gains[0:1])
    for g in range(8):
        lanes = slice(g * LANES, (g + 1) * LANES)
        narrow = slice(g // 2 * LANES, (g // 2 + 1) * LANES)
        rows = [vector[:, lanes] for vector in (attn_gain, attn_shift, mlp_gain, mlp_shift)]
        rows += [dec_vectors[0:5, narrow], jnp.zeros((7, LANES), FULL)]
        value = jnp.broadcast_to(jnp.concatenate(rows, axis=0)[None, None], (2, 4, 16, LANES))
        index = (g // 2, slice(2 * (g % 2), 2 * (g % 2) + 2), slice(None))
        for buffers in (stage[0], work[0]):
            red.put(buffers, 3, 16, index, value)
    red.swap(3, range(5, 6))
    ga_ref[...] = gy[...] + gv
    bags = landed[0]

    def bag(half):
        rows = ga_ref[pl.ds(pl.multiple_of(half * 128, 128), 128), :]
        return rows.reshape(128, 8, LANES).reshape(4, 4, 4, 16, LANES).astype(LOW)

    everything = (slice(None),) * 4
    mine = pl.ds(pl.multiple_of(section * LANES, LANES), LANES)
    bags[1][:, :, :, :, 0:LANES] = bag(1 - section)
    pl.semaphore_wait(credit, 1)
    red.send(bags[1].at[(*everything, slice(0, LANES))], bags[0].at[(*everything, mine)], red.sibling, "rows", "rows")
    bags[0][:, :, :, :, mine] = bag(section)
    red.halve_b(1, 1)
    red.halve_a(0, 2)
    red.halve_a(2, 1)
    red.halve_a(3, 0, range(5, 6))
    red.halve_a(1, 2)
    red.halve_b(0, 2)
    red.arrive("rows")
    give = pltpu.make_async_copy(bags[0].at[(*everything, slice(0, 2 * LANES))], received_h, in_sem.at[0])
    give.start()
    red.halve_b(3, 0)
    red.halve_b(2, 1)
    red.halve_b(1, 2)
    red.finish(0)
    red.halve_a(3, 1)
    red.halve_a(2, 2)
    red.finish(1)
    red.halve_b(3, 1)
    red.halve_b(2, 2)
    red.halve_a(3, 2)
    red.finish(2)
    red.halve_b(3, 2)
    red.finish(3)
    for c in range(4):
        red.arrive((c, "final"))
    out = pltpu.make_async_copy(final, shares_h, out_sem)
    out.start()
    for chunk in list(red.unsent):
        red.sent(chunk)
    out.wait()
    give.wait()


def backward_call(g_embedded, arrived, gains, dec_vectors, weights, kept, dec_grads):
    encoded, _, x1, m, slope, qT, kT, v, e, linv, oT = kept
    dec = [a.reshape(4, 4, 4, rows, columns) for a, (rows, columns) in zip(dec_grads, DEC_SOURCES)]
    vmem = pltpu.VMEM
    scratch = [
        vmem((UP_SLOTS, ED, 512), LOW), vmem((DOWN_SLOTS, 512, ED), LOW), vmem((KEPT_SLOTS, ER, 512), LOW),
        vmem((ER, ED), FULL), vmem((ED, ER), LOW), vmem((ED, ER), LOW), vmem((ER, ED), LOW),
        vmem((HEADS, ER, ER), LOW), vmem((HEADS, ER), FULL), vmem((ED, ER), LOW),
        vmem((ER, ED), FULL), vmem((ER, ED), LOW), vmem((ER, ED), FULL), vmem((ED, ER), LOW), vmem((ED, ER), LOW),
        vmem((3 * ED, ER), LOW), vmem((256, ER), LOW),
    ]
    for tiles in WORK_TILES + (SLOT_TILES[1], SLOT_TILES[0]) + SLOT_TILES:
        scratch += [vmem((4, 4, 4, 16, n * LANES), LOW) for n in tiles]
    scratch += [vmem((4, 4, 16, n * LANES), LOW) for n in COUNTS[0]]
    for tiles in STEP_TILES:
        for shape in LEVEL_SHAPES[:2]:
            scratch += [vmem((*shape, 16, n * LANES), LOW) for n in tiles]
    for tiles in COUNTS:
        for shape in LEVEL_SHAPES[2:]:
            scratch += [vmem((*shape, 16, n * LANES), LOW) for n in tiles]
    copies = len(dec_pieces()) + 3 * STREAMS + 4 * 9 * STREAMS + 5
    dma = pltpu.SemaphoreType.DMA
    scratch += [
        vmem((2, TILES, 16, LANES), LOW), dma((copies,)), dma((copies,)), dma((len(dec_pieces()),)),
        pltpu.SemaphoreType.REGULAR, pltpu.SemaphoreType.REGULAR((6,)), dma((8,)), dma((9,)), dma,
    ]
    return pl.pallas_call(
        backward_kernel,
        out_shape=[jax.ShapeDtypeStruct((4, 4, 4, 16, 2 * LANES), LOW), jax.ShapeDtypeStruct((2, TILES, 16, LANES), LOW)],
        in_specs=[VMEM] * 4 + [ANY] * 19,
        out_specs=[ANY, ANY],
        scratch_shapes=scratch,
        compiler_params=pltpu.CompilerParams(collective_id=0, has_side_effects=True, vmem_limit_bytes=64 * 1024 * 1024 - 65536),
        name="encoder_backward_reduce",
    )(g_embedded, arrived, gains, dec_vectors, *weights, encoded, x1, m, slope, qT, kT, v, e, linv, oT, *dec)


SHARES = (
    ((8, 1536), 0, 0), ((8, 512), 0, 3), ((8, 2048), 0, 4), ((32, 512), 0, 8),
    ((16, 512), 1, 0), ((16, 4096), 2, 0), ((64, 1024), 1, 2), ((16, 1024), 3, 0), ((16, 3072), 3, 4),
)


def unpack_kernel(shares, *outs):
    for out, (shape, c, tile) in zip(outs, SHARES):
        number = FIRST_TILE[c] + tile
        rows, columns = shape
        packed = columns // 2 if rows == 8 else columns
        for r in range(max(rows // 16, 1)):
            for t in range(packed // (2 * LANES)):
                for half in range(2):
                    value = shares[half, number].astype(FULL)
                    lane = half * packed // 2 + t * LANES
                    if rows == 8:
                        out[:, lane : lane + LANES] = value[:8]
                        out[:, packed + lane : packed + lane + LANES] = value[8:]
                    else:
                        out[16 * r : 16 * r + 16, lane : lane + LANES] = value
                number += 1
    vectors = outs[len(SHARES) :]
    batch = lax.axis_index("batch")
    value = shares[0, VECTOR_TILE].astype(FULL)
    wide = pltpu.roll(value, lax.rem(128 - 16 * lax.rem(batch, 8), 128), axis=1)
    narrow = pltpu.roll(value, lax.rem(128 - 8 * lax.rem(batch, 16), 128), axis=1)
    for i in range(9):
        many = 16 if i < 4 else 8
        vectors[i][...] = (wide if i < 4 else narrow)[i, :many]


def unpack_call(shares):
    shapes = [jax.ShapeDtypeStruct(shape, FULL) for shape, _, _ in SHARES]
    shapes += [jax.ShapeDtypeStruct((16 if i < 4 else 8,), FULL) for i in range(9)]
    return pl.pallas_call(
        unpack_kernel,
        out_shape=shapes,
        in_specs=[VMEM],
        out_specs=[VMEM] * len(shapes),
        name="unpack_shares",
    )(shares)


def rows_kernel(bags, rows):
    for half in range(2):
        value = bags[:, :, half * LANES : (half + 1) * LANES].astype(FULL)
        rows[half * 128 : (half + 1) * 128, :] = value.reshape(128, 8, LANES).reshape(128, ED)


def rows_call(bags):
    return pl.pallas_call(
        rows_kernel,
        out_shape=jax.ShapeDtypeStruct((ER, ED), FULL),
        in_specs=[VMEM],
        out_specs=VMEM,
        name="rows_of_patches",
    )(bags)


def tag_table(lengths, visible, gsd_index):
    row = jnp.arange(ROWS, dtype=jnp.int32)
    ends = jnp.cumsum(lengths)
    segment = jnp.sum((row[:, None] >= ends[None]).astype(jnp.int32), axis=1)
    onehot = (segment[:, None] == jnp.arange(lengths.shape[0])[None]).astype(jnp.int32)
    offset = row - jnp.sum(onehot * (ends - lengths)[None], axis=1)
    length = jnp.sum(onehot * lengths[None], axis=1)
    factor = jnp.sum(onehot * gsd_index[None], axis=1)
    side = jnp.where(length == 64, 8, jnp.where(length == 196, 14, 28))
    live = segment < lengths.shape[0]
    row_tag = jnp.where(live, factor * 28 + offset // side, -1)
    column_tag = jnp.where(live, factor * 28 + offset % side, -1)
    rank = jnp.cumsum(visible) - 1
    source = jnp.where(visible == 1, rank % 128 * 2 + rank // 128, -1)
    return jnp.stack([source, row_tag, column_tag, segment], axis=1).astype(jnp.int32)


def per_device(
    patches, lengths, visible, gsd_index,
    enc_attn_gain, enc_attn_shift, enc_qkv, enc_out, enc_mlp_gain, enc_mlp_shift, enc_up, enc_down,
    dec_embed, mask_token,
    dec_attn_gain, dec_attn_shift, dec_qkv, dec_out, dec_mlp_gain, dec_mlp_shift, dec_up, dec_down,
    out_grad,
):
    both = ("section", "batch")
    arrived = lax.all_to_all(patches, both, split_axis=0, concat_axis=0, tiled=True)
    tags = tag_table(lengths[0], visible, gsd_index[0])
    enc_gains = jnp.stack([enc_attn_gain, enc_attn_shift, enc_mlp_gain, enc_mlp_shift])
    dec_gains = jnp.stack([dec_attn_gain, dec_attn_shift, dec_mlp_gain, dec_mlp_shift])
    weights = (enc_qkv, enc_out, enc_up, enc_down, dec_embed)
    kept = encoder_forward_call(arrived, tags, enc_gains, *weights)
    high, low = wave_tables()
    decoder = decoder_call(
        kept[1], tags, high, low, mask_token[None], dec_gains, dec_qkv, dec_out, dec_up, dec_down, out_grad
    )
    dec_output, g_embedded, *d_dec, dec_vectors = decoder
    received, shares = backward_call(g_embedded, arrived, enc_gains, dec_vectors, weights, kept, d_dec)
    bags = lax.all_to_all(received.reshape(64, 16, 2 * LANES), "batch", split_axis=0, concat_axis=0, tiled=True)
    patch_grad = rows_call(bags)
    d_qkv, d_out, d_up, d_down, embed, up, down, out, qkv, *vectors = unpack_call(shares)
    gain1, shift1, gain2, shift2, dec_gain1, dec_shift1, dec_gain2, dec_shift2, mask = vectors
    return (
        dec_output, patch_grad, gain1, shift1, qkv, out, gain2, shift2, up, down, embed, mask,
        dec_gain1, dec_shift1, d_qkv, d_out, dec_gain2, dec_shift2, d_up, d_down,
    )


def solution(mesh):
    return jax.shard_map(
        per_device,
        mesh=mesh,
        in_specs=(
            P(("section", "batch"), None),
            P(("section", "batch"), None),
            P(("section", "batch")),
            P(("section", "batch"), None),
            P(),
            P(),
            P(),
            P(),
            P(),
            P(),
            P(),
            P(),
            P(),
            P(),
            P(),
            P(),
            P(),
            P(),
            P(),
            P(),
            P(),
            P(),
            P(("section", "batch"), None),
        ),
        out_specs=(
            P(("section", "batch"), None),
            P(("section", "batch"), None),
            P("batch"),
            P("batch"),
            P("batch", None),
            P("batch", None),
            P("batch"),
            P("batch"),
            P("batch", None),
            P("batch", None),
            P("batch", None),
            P("batch"),
            P("batch"),
            P("batch"),
            P("batch", None),
            P("batch", None),
            P("batch"),
            P("batch"),
            P("batch", None),
            P("batch", None),
        ),
        check_vma=False,
    )
```

```python
import functools
import math

import jax
import jax.numpy as jnp
import numpy as np
from jax import lax
from jax.experimental import pallas as pl
from jax.experimental.pallas import tpu as pltpu
from jax.sharding import PartitionSpec as P

LOW = jnp.bfloat16
FULL = jnp.float32
LN2 = math.log(2.0)
FAR = -1e30


def dot(a, b):
    return jnp.dot(a, b, preferred_element_type=FULL)


def dot_nt(a, b):
    return lax.dot_general(a, b, (((1,), (1,)), ((), ())), preferred_element_type=FULL)


def norm_parts(v):
    centred = v - jnp.mean(v, axis=-1, keepdims=True)
    r = lax.rsqrt(jnp.mean(centred * centred, axis=-1, keepdims=True) + 1e-6)
    return centred * r, r


def norm_back(gn, v, gain):
    vh, r = norm_parts(v)
    gg = gn * gain
    gv = r * (gg - jnp.mean(gg, axis=-1, keepdims=True) - vh * jnp.mean(gg * vh, axis=-1, keepdims=True))
    return gv, jnp.sum(gn * vh, axis=0, keepdims=True), jnp.sum(gn, axis=0, keepdims=True)


def gelu_parts(u):
    z = jnp.abs(u) * (0.3275911 / math.sqrt(2.0))
    t = 1.0 / (1.0 + z)
    poly = 1.061405429
    for c in (-1.453152027, 1.421413741, -0.284496736, 0.254829592):
        poly = poly * t + c
    bell = jnp.exp2(u * u * (-0.5 / LN2))
    tail = (0.5 * t) * poly * bell
    phi = jnp.where(u >= 0, 1.0 - tail, tail)
    return u * phi, phi + u * (bell * (1.0 / math.sqrt(2.0 * math.pi)))


def paired(a, b):
    w = a.shape[1]
    return jnp.concatenate([a.reshape(64, 8, w), b.reshape(64, 8, w)], axis=1).astype(LOW)


def blocks_of(total, size):
    cuts = list(range(0, total - size + 1, size))
    return [(c, (size if i + 1 < len(cuts) else total - c)) for i, c in enumerate(cuts)]


def attention_forward(rows, heads, hs, k_ref, ones_ref, far_ref, qT, vT, mix, e_ref, oT, linv):
    group = 128 // hs
    mix[...] = jnp.zeros_like(mix)
    mix[128:256, :] = far_ref[...]
    for g in range(heads // group):
        lanes = slice(128 * g, 128 * g + 128)
        left = jnp.concatenate([k_ref[:, lanes], ones_ref[...]], axis=1)
        for i in range(group):
            h = g * group + i
            feat = slice(h * hs, h * hs + hs)
            if i:
                mix[(i - 1) * hs : i * hs, :] = jnp.zeros((hs, rows), LOW)
            else:
                mix[128 - hs : 128, :] = jnp.zeros((hs, rows), LOW)
            mix[i * hs : i * hs + hs, :] = qT[feat, :]
            head_forward(rows, h, feat, left, vT, mix, e_ref, oT, linv)


def head_forward(rows, h, feat, left, vT, mix, e_ref, oT, linv):
    for first, many in blocks_of(rows, 256):
        cols = slice(first, first + many)
        s = dot(left, mix[:, cols])
        peak = jnp.max(s, axis=0, keepdims=True)
        e_ref[h, :, cols] = jnp.exp2(s - peak).astype(LOW)
    lhs = jnp.concatenate([vT[feat, :], jnp.ones((16, rows), LOW)], axis=0)
    o = dot(lhs, e_ref[h])
    hs = feat.stop - feat.start
    inverse = 1.0 / o[hs : hs + 1]
    linv[h : h + 1, :] = inverse
    oT[feat, :] = (o[:hs] * inverse).astype(LOW)


def attention_backward(rows, heads, hs, v_ref, qT, kT, goT, oT, e_ref, linv, mix, gtT, between=None):
    group = 128 // hs
    width = heads * hs
    scale = hs**-0.5
    for g in range(heads // group):
        lanes = slice(128 * g, 128 * g + 128)
        for i in range(group):
            h = g * group + i
            feat = slice(h * hs, h * hs + hs)
            go = goT[feat, :].astype(FULL) * linv[h : h + 1, :]
            low = go.astype(LOW)
            centre = jnp.sum(go * oT[feat, :].astype(FULL), axis=0, keepdims=True)
            if i:
                mix[(i - 1) * hs : i * hs, :] = jnp.zeros((hs, rows), LOW)
            else:
                mix[128 - hs : 128, :] = jnp.zeros((hs, rows), LOW)
            mix[i * hs : i * hs + hs, :] = low
            gtT[2 * width + h * hs : 2 * width + h * hs + hs, :] = dot_nt(low, e_ref[h]).astype(LOW)
            for first, many in blocks_of(rows, 256):
                cols = slice(first, first + many)
                gp = dot(v_ref[:, lanes], mix[0:128, cols])
                e_ref[h, :, cols] = (e_ref[h, :, cols].astype(FULL) * (gp - centre[:, cols])).astype(LOW)
            gs = e_ref[h]
            gtT[feat, :] = (dot(kT[feat, :], gs) * scale).astype(LOW)
            gtT[width + h * hs : width + h * hs + hs, :] = (dot_nt(qT[feat, :], gs) * LN2).astype(LOW)
        if between is not None:
            between(g)


ROWS, DD, DFF, HEADS = 784, 512, 2048, 16
STEP = 112


def decoder_kernel(
    embedded, tags, sines_high, sines_low, mask_token, gains, w_qkv, w_out_h, w_up_h, w_down_h, out_grad,
    dec_out_h, g_embedded, d_qkv, d_out_h, d_up_h, d_down_h, vectors,
    w_out, w_up, w_down, dec_out, d_out, d_up, d_down, in_sem, out_sem,
    x_ref, low_a, low_aT, k_ref, v_ref, qT, kT, vT, e_ref, oT, linv, x1_ref, gz, ga_ref, y_ref, goT, gtT, mix, ones_ref, far_ref, sums,
):
    loads, stores = [], []
    for i, (source, target) in enumerate(((w_out_h, w_out), (w_up_h, w_up), (w_down_h, w_down))):
        loads.append(pltpu.make_async_copy(source, target, in_sem.at[i]))
        loads[-1].start()

    def keep(source, target):
        stores.append(pltpu.make_async_copy(source, target, out_sem.at[len(stores)]))
        stores[-1].start()

    sums[...] = jnp.zeros_like(sums)
    tile = 256

    def each(body):
        @pl.loop(0, ROWS // STEP)
        def _(i):
            body(pl.ds(pl.multiple_of(i * STEP, STEP), STEP))

    wide = embedded[...]
    emb_high = wide.astype(LOW)
    emb_low = (wide - emb_high.astype(FULL)).astype(LOW)
    mask = mask_token[...].astype(FULL)

    def inputs(rows):
        tag = tags[rows, :]
        source, row_tag, column_tag, segment = (tag[:, i : i + 1] for i in range(4))
        lane = lax.broadcasted_iota(jnp.int32, (STEP, 256), 1)
        small = lax.broadcasted_iota(jnp.int32, (STEP, 128), 1)
        pick = (lane == source).astype(LOW)
        x = dot(pick, emb_high) + dot(pick, emb_low)
        x = jnp.where(source < 0, mask, x)
        row_pick = (small == row_tag).astype(LOW)
        column_pick = (small == column_tag).astype(LOW)
        row_wave = dot(row_pick, sines_high[...]) + dot(row_pick, sines_low[...])
        column_wave = dot(column_pick, sines_high[...]) + dot(column_pick, sines_low[...])
        x = x + jnp.concatenate([row_wave, column_wave], axis=1)
        x_ref[rows, :] = x
        low_a[rows, :] = (norm_parts(x)[0] * gains[0:1] + gains[1:2]).astype(LOW)
        same = small == segment
        ones_ref[rows, :] = same.astype(LOW)
        y_ref[rows, 0:128] = jnp.where(same | (small > 12), 0.0, FAR)
        live = (segment < 12).astype(FULL)
        gz[rows, :] = (out_grad[rows, :].astype(FULL) * live).astype(LOW)

    each(inputs)
    far_ref[...] = y_ref[:, 0:128].T.astype(LOW)
    low_aT[...] = low_a[...].T

    for j in range(2):
        t = dot(low_a[...], w_qkv[:, j * tile : (j + 1) * tile]) * (32**-0.5 / LN2)
        qT[j * tile : (j + 1) * tile, :] = t.astype(LOW).T
        t = dot(low_a[...], w_qkv[:, DD + j * tile : DD + (j + 1) * tile]).astype(LOW)
        k_ref[:, j * tile : (j + 1) * tile] = t
        kT[j * tile : (j + 1) * tile, :] = t.T
        t = dot(low_a[...], w_qkv[:, 2 * DD + j * tile : 2 * DD + (j + 1) * tile]).astype(LOW)
        v_ref[:, j * tile : (j + 1) * tile] = t
        vT[j * tile : (j + 1) * tile, :] = t.T

    attention_forward(ROWS, HEADS, 32, k_ref, ones_ref, far_ref, qT, vT, mix, e_ref, oT, linv)

    for copy in loads:
        copy.wait()
    low_a[...] = oT[...].T
    for j in range(2):
        cols = slice(j * tile, (j + 1) * tile)
        x1_ref[:, cols] = x_ref[:, cols] + dot(low_a[...], w_out[:, cols])

    def second(rows):
        x1 = x1_ref[rows, :]
        low_a[rows, :] = (norm_parts(x1)[0] * gains[2:3] + gains[3:4]).astype(LOW)
        y_ref[rows, :] = x1
        ga_ref[rows, :] = jnp.zeros((STEP, DD), FULL)

    each(second)
    a2T = goT
    del a2T
    a2_t = low_a[...].T

    kT_keep = None
    del kT_keep
    gtT[0:DD, :] = a2_t

    @pl.loop(0, DFF // (2 * tile))
    def _(j):
        halves = []
        for half in range(2):
            cols = pl.ds(pl.multiple_of(j * tile + half * (DFF // 2), tile), tile)
            u = dot(low_a[...], w_up[:, cols])
            m, slope = gelu_parts(u)
            m = m.astype(LOW)
            y_ref[...] += dot(m, w_down[cols, :])
            gm = dot_nt(gz[...], w_down[cols, :])
            gu = (gm * slope).astype(LOW)
            ga_ref[...] += dot_nt(gu, w_up[:, cols])
            d_down[cols, :] = dot(m.T, gz[...]).astype(LOW)
            halves.append(dot(gtT[0:DD, :], gu))
        d_up[:, :, pl.ds(pl.multiple_of(j * tile, tile), tile)] = paired(*halves)

    keep(d_up, d_up_h)
    keep(d_down, d_down_h)

    def third(rows):
        live = (tags[rows, 3:4] < 12).astype(FULL)
        dec_out[rows, :] = (y_ref[rows, :] * live).astype(LOW)
        gv, dgain, dshift = norm_back(ga_ref[rows, :], x1_ref[rows, :], gains[2:3])
        gx1 = out_grad[rows, :].astype(FULL) * live + gv
        x1_ref[rows, :] = gx1
        low_a[rows, :] = gx1.astype(LOW)
        sums[2:3, :] += dgain
        sums[3:4, :] += dshift

    each(third)
    keep(dec_out, dec_out_h)
    for j in range(2):
        goT[j * tile : (j + 1) * tile, :] = dot_nt(w_out[j * tile : (j + 1) * tile, :], low_a[...])
    for j in range(2):
        half = dot(oT[...], low_a[:, j * tile : (j + 1) * tile])
        if j == 0:
            first_half = half
        else:
            d_out[...] = paired(first_half, half)
    keep(d_out, d_out_h)

    attention_backward(ROWS, HEADS, 32, v_ref, qT, kT, goT, oT, e_ref, linv, mix, gtT)

    for j in range(3):
        lo = dot_nt(low_aT[...], gtT[j * tile : (j + 1) * tile, :])
        hi = dot_nt(low_aT[...], gtT[768 + j * tile : 768 + (j + 1) * tile, :])
        d_qkv[:, :, j * tile : (j + 1) * tile] = paired(lo, hi)
    for j in range(2):
        cols = slice(j * tile, (j + 1) * tile)
        y_ref[:, cols] = dot(w_qkv[cols, :], gtT[...]).T

    def fourth(rows):
        gv, dgain, dshift = norm_back(y_ref[rows, :], x_ref[rows, :], gains[0:1])
        gx = x1_ref[rows, :] + gv
        sums[0:1, :] += dgain
        sums[1:2, :] += dshift
        source = tags[rows, 0:1]
        sums[4:5, :] += jnp.sum(jnp.where(source < 0, gx, 0.0), axis=0, keepdims=True)
        low_a[rows, :] = gx.astype(LOW)
        lane = lax.broadcasted_iota(jnp.int32, (STEP, 256), 1)
        y_ref[rows, 0:256] = (lane == source).astype(FULL)

    each(fourth)
    pick = y_ref[:, 0:256].astype(LOW).T
    g_embedded[...] = dot(pick, low_a[...]).astype(LOW)
    vectors[...] = sums[...]
    for copy in stores:
        copy.wait()


def decoder_call(embedded, tags, sines_high, sines_low, mask_token, gains, w_qkv, w_out, w_up, w_down, out_grad):
    vmem = pl.BlockSpec(memory_space=pltpu.VMEM)
    hbm = pl.BlockSpec(memory_space=pl.ANY)
    low = lambda *shape: pltpu.VMEM(shape, LOW)
    full = lambda *shape: pltpu.VMEM(shape, FULL)
    return pl.pallas_call(
        decoder_kernel,
        out_shape=[
            jax.ShapeDtypeStruct((ROWS, DD), LOW),
            jax.ShapeDtypeStruct((256, DD), LOW),
            jax.ShapeDtypeStruct((64, 16, 768), LOW),
            jax.ShapeDtypeStruct((64, 16, 256), LOW),
            jax.ShapeDtypeStruct((64, 16, 1024), LOW),
            jax.ShapeDtypeStruct((DFF, DD), LOW),
            jax.ShapeDtypeStruct((8, DD), FULL),
        ],
        in_specs=[vmem] * 7 + [hbm] * 3 + [vmem],
        out_specs=[hbm, vmem, vmem, hbm, hbm, hbm, vmem],
        scratch_shapes=[
            low(DD, DD), low(DD, DFF), low(DFF, DD),
            low(ROWS, DD), low(64, 16, 256), low(64, 16, 1024), low(DFF, DD),
            pltpu.SemaphoreType.DMA((3,)), pltpu.SemaphoreType.DMA((4,)),
            full(ROWS, DD), low(ROWS, DD), low(DD, ROWS), low(ROWS, DD), low(ROWS, DD),
            low(DD, ROWS), low(DD, ROWS), low(DD, ROWS), low(HEADS, ROWS, ROWS), low(DD, ROWS),
            full(HEADS, ROWS), full(ROWS, DD), low(ROWS, DD), full(ROWS, DD), full(ROWS, DD),
            full(DD, ROWS), low(3 * DD, ROWS), low(256, ROWS), low(ROWS, 128), low(128, ROWS), full(8, DD),
        ],
        compiler_params=pltpu.CompilerParams(vmem_limit_bytes=63 * 1024 * 1024),
        name="decoder",
    )(embedded, tags, sines_high, sines_low, mask_token, gains, w_qkv, w_out, w_up, w_down, out_grad)


def wave_tables():
    quarter = DD // 4
    frequency = np.exp(np.arange(quarter, dtype=np.float32) * np.float32(-math.log(10000.0) / quarter)).astype(np.float32)
    places = np.zeros((128, 1), np.float32)
    for f, factor in enumerate((0.5, 1.0, 2.0, 4.0)):
        places[f * 28 : f * 28 + 28, 0] = np.arange(28, dtype=np.float32) * factor
    angle = (places * frequency[None, :]).astype(np.float32).astype(np.float64)
    waves = np.concatenate([np.sin(angle), np.cos(angle)], axis=1)
    waves[112:] = 0.0
    high = jnp.asarray(waves, FULL).astype(LOW)
    low = (jnp.asarray(waves, FULL) - high.astype(FULL)).astype(LOW)
    return high, low


ER, ED, EF = 256, 1024, 4096
EH = 64


def encoder_forward_kernel(
    arrived, tags, gains, w_qkv_h, w_out_h, w_up_h, w_down_h, w_embed_h,
    encoded_h, embedded_h, x1_h, m_h, slope_h, qT_h, kT_h, v_h, e_h, linv_h, oT_h,
    w_qkv, w_out, w_up, w_down, w_embed,
    encoded, embedded, x1, m_ref, slope_ref, qT, kT, v_ref, e_ref, linv, oT,
    x_ref, low_a, k_ref, vT, mix, ones_ref, far_ref, y_ref, in_sem, out_sem,
):
    loads = []
    for i, (source, target) in enumerate(
        ((w_qkv_h, w_qkv), (w_out_h, w_out), (w_up_h, w_up), (w_down_h, w_down), (w_embed_h, w_embed))
    ):
        copy = pltpu.make_async_copy(source, target, in_sem.at[i])
        copy.start()
        loads.append(copy)
    stores = []

    def keep(source, target):
        copy = pltpu.make_async_copy(source, target, out_sem.at[len(stores)])
        copy.start()
        stores.append(copy)

    tag = tags[...]
    lane = lax.broadcasted_iota(jnp.int32, (ROWS, 256), 1)
    small = lax.broadcasted_iota(jnp.int32, (ROWS, 128), 1)
    pick = (lane == tag[:, 0:1]).astype(FULL).T.astype(LOW)
    items = dot(pick, (small == tag[:, 3:4]).astype(LOW))
    slot = lax.broadcasted_iota(jnp.int32, (ER, 128), 1)
    empty = jnp.sum(items, axis=1, keepdims=True) < 0.5
    items = jnp.where((slot == 13) & empty, 1.0, items)
    ones_ref[...] = items.astype(LOW)
    far_ref[...] = jnp.where((items > 0.5) | (slot > 13), 0.0, FAR).T.astype(LOW)

    x = arrived[...].astype(FULL)
    x_ref[...] = x
    low_a[...] = (norm_parts(x)[0] * gains[0:1] + gains[1:2]).astype(LOW)
    loads[0].wait()

    tile = 256

    @pl.loop(0, ED // tile)
    def _(j):
        cols = pl.ds(pl.multiple_of(j * tile, tile), tile)
        t = dot(low_a[...], w_qkv[:, cols]) * (EH**-0.5 / LN2)
        qT[cols, :] = t.T.astype(LOW)
        t = dot(low_a[...], w_qkv[:, pl.ds(pl.multiple_of(ED + j * tile, tile), tile)])
        k_ref[:, cols] = t.astype(LOW)
        kT[cols, :] = t.T.astype(LOW)
        t = dot(low_a[...], w_qkv[:, pl.ds(pl.multiple_of(2 * ED + j * tile, tile), tile)])
        v_ref[:, cols] = t.astype(LOW)
        vT[cols, :] = t.T.astype(LOW)

    keep(qT, qT_h)
    keep(kT, kT_h)
    keep(v_ref, v_h)
    attention_forward(ER, HEADS, EH, k_ref, ones_ref, far_ref, qT, vT, mix, e_ref, oT, linv)
    keep(e_ref, e_h)
    keep(linv, linv_h)
    keep(oT, oT_h)
    low_a[...] = oT[...].T
    loads[1].wait()

    @pl.loop(0, ED // tile)
    def _(j):
        cols = pl.ds(pl.multiple_of(j * tile, tile), tile)
        x1[:, cols] = x_ref[:, cols] + dot(low_a[...], w_out[:, cols])

    keep(x1, x1_h)
    branch = x1[...]
    low_a[...] = (norm_parts(branch)[0] * gains[2:3] + gains[3:4]).astype(LOW)
    y_ref[...] = branch
    loads[2].wait()
    loads[3].wait()

    @pl.loop(0, EF // 512)
    def _(j):
        cols = pl.ds(pl.multiple_of(j * 512, 512), 512)
        m, slope = gelu_parts(dot(low_a[...], w_up[:, cols]))
        m = m.astype(LOW)
        m_ref[:, cols] = m
        slope_ref[:, cols] = slope.astype(LOW)
        y_ref[...] += dot(m, w_down[cols, :])

    keep(m_ref, m_h)
    keep(slope_ref, slope_h)
    encoded[...] = y_ref[...].astype(LOW)
    keep(encoded, encoded_h)
    loads[4].wait()
    embedded[...] = dot(encoded[...], w_embed[...])
    keep(embedded, embedded_h)
    for copy in stores:
        copy.wait()


ANY = pl.BlockSpec(memory_space=pl.ANY)
VMEM = pl.BlockSpec(memory_space=pltpu.VMEM)
WEIGHTS = [((ED, 3 * ED), LOW), ((ED, ED), LOW), ((ED, EF), LOW), ((EF, ED), LOW), ((ED, DD), LOW)]
KEPT = [
    ((ER, ED), LOW), ((ER, DD), FULL), ((ER, ED), FULL), ((ER, EF), LOW), ((ER, EF), LOW),
    ((ED, ER), LOW), ((ED, ER), LOW), ((ER, ED), LOW), ((HEADS, ER, ER), LOW), ((HEADS, ER), FULL), ((ED, ER), LOW),
]


def encoder_forward_call(arrived, tags, gains, w_qkv, w_out, w_up, w_down, w_embed):
    scratch = [pltpu.VMEM(*s) for s in WEIGHTS + KEPT]
    scratch += [
        pltpu.VMEM((ER, ED), FULL), pltpu.VMEM((ER, ED), LOW), pltpu.VMEM((ER, ED), LOW), pltpu.VMEM((ED, ER), LOW),
        pltpu.VMEM((256, ER), LOW), pltpu.VMEM((ER, 128), LOW), pltpu.VMEM((128, ER), LOW), pltpu.VMEM((ER, ED), FULL),
        pltpu.SemaphoreType.DMA((5,)), pltpu.SemaphoreType.DMA((len(KEPT),)),
    ]
    return pl.pallas_call(
        encoder_forward_kernel,
        out_shape=[jax.ShapeDtypeStruct(*s) for s in KEPT],
        in_specs=[VMEM] * 3 + [ANY] * 5,
        out_specs=[ANY] * len(KEPT),
        scratch_shapes=scratch,
        compiler_params=pltpu.CompilerParams(vmem_limit_bytes=60 * 1024 * 1024),
        name="encoder_forward",
    )(arrived, tags, gains, w_qkv, w_out, w_up, w_down, w_embed)


MESH = pl.DeviceIdType.MESH
LANES = 128
STREAMS = 6
COUNTS = ((2, 2, 2, 2, 2, 2), (3, 3, 3, 3, 3, 3), (3, 3, 3, 3, 2, 2), (3, 3, 3, 3, 3, 2))
DEC_SOURCES = ((16, 768), (16, 256), (16, 1024), (32, 512))
WORK_OF = (0, 1, 2, 0)
STAGE_OF = (None, 0, 1, 0)
WORK_TILES = ((3, 3, 3, 3, 3, 2), (3, 3, 3, 3, 3, 3), (3, 3, 3, 3, 2, 2))
SLOT_TILES = ((3, 3, 3, 3, 2, 2), (3, 3, 3, 3, 3, 3))
STEP_TILES = WORK_TILES
LEVEL_SHAPES = ((2, 4, 4), (4, 4), (2, 4), (4,), (2,), ())
FIRST_TILE = (0, 12, 30, 46)
TILES = 63
VECTOR_TILE = 62


def seat(c, tile):
    for s, many in enumerate(COUNTS[c]):
        if tile < many:
            return s, tile
        tile -= many


def dec_pieces():
    found, tile = [], 0
    for source, (rows, columns) in enumerate(DEC_SOURCES):
        for r in range(rows // 16):
            for column in range(columns // (2 * LANES)):
                s, place = seat(0, tile)
                last = found[-1] if found else None
                if last and last[:3] == [s, source, r] and last[3] + last[4] == column:
                    last[4] += 1
                else:
                    found.append([s, source, r, column, 1, place])
                tile += 1
    return found


class Stream:
    def __init__(self, number):
        self.order = tuple((number + step) % 3 for step in range(3))
        self.swap = number >= 3

    def flip(self, p):
        return p + 1 - 2 * lax.rem(p, 2)

    def first(self, p):
        return 3 - p if self.swap else self.flip(p)

    def mate(self, p):
        return self.flip(p) if self.swap else 3 - p


class Reducer:
    def __init__(self, dec_sources, work, parked, stage, landed, steps, final, send_sem, recv_sem, own_sem, credit, credits):
        self.dec_sources, self.work, self.parked, self.stage = dec_sources, work, parked, stage
        self.landed, self.steps, self.final = landed, steps, final
        self.send_sem, self.recv_sem, self.own_sem = send_sem, recv_sem, own_sem
        self.credit, self.credits = credit, credits
        self.section = lax.axis_index("section")
        self.batch = lax.axis_index("batch")
        batch = self.batch
        self.coords = (batch // 16, lax.rem(batch // 4, 4), lax.rem(batch, 4))
        self.sibling = (1 - self.section, batch)
        self.streams = [Stream(number) for number in range(STREAMS)]
        self.neighbours = []
        for axis in range(3):
            p = self.coords[axis]
            self.neighbours += [self.peer(axis, p + 1 - 2 * lax.rem(p, 2)), self.peer(axis, 3 - p)]
        self.count = 0
        self.arrivals, self.unsent, self.owns = {}, {}, {}

    def peer(self, axis, place):
        return (self.section, self.batch + (place - self.coords[axis]) * (16, 4, 1)[axis])

    def ahead(self, axis, step):
        return self.peer(axis, lax.rem(self.coords[axis] + step, 4))

    def meet(self):
        barrier = pltpu.get_barrier_semaphore()
        partners = [self.sibling] + [self.ahead(axis, step) for axis in range(3) for step in (1, 2, 3)]
        for partner in partners:
            pl.semaphore_signal(barrier, inc=1, device_id=partner, device_id_type=MESH)
        pl.semaphore_wait(barrier, len(partners))

    def send(self, source, target, device, key, chunk):
        number = self.count
        self.count += 1
        copy = pltpu.make_async_remote_copy(
            src_ref=source, dst_ref=target, send_sem=self.send_sem.at[number], recv_sem=self.recv_sem.at[number],
            device_id=device, device_id_type=MESH,
        )
        copy.start()
        self.unsent.setdefault(chunk, []).append(copy)
        self.arrivals.setdefault(key, []).append(copy)

    def arrive(self, key):
        for copy in self.arrivals.pop(key):
            copy.wait_recv()

    def sent(self, chunk):
        for copy in self.unsent.pop(chunk, []):
            copy.wait_send()

    def start_decoder(self):
        for number, (s, source, r, column, width, place) in enumerate(dec_pieces()):
            half = DEC_SOURCES[source][1] // 2
            rows = pl.ds(16 * r, 16)
            there = pl.ds(pl.multiple_of((1 - self.section) * half, LANES) + column * LANES, width * LANES)
            here = pl.ds(pl.multiple_of(self.section * half, LANES) + column * LANES, width * LANES)
            lanes = pl.ds(place * LANES, width * LANES)
            everything = (slice(None),) * 4
            self.send(
                self.dec_sources[source].at[:, :, :, rows, there],
                self.landed[0][s].at[(*everything, lanes)],
                self.sibling, (0, s, 0), ("swap", 0),
            )
            own = pltpu.make_async_copy(
                self.dec_sources[source].at[:, :, :, rows, here],
                self.work[0][s].at[(*everything, lanes)],
                self.own_sem.at[number],
            )
            own.start()
            self.owns.setdefault(s, []).append(own)

    def swap(self, c, streams=range(STREAMS)):
        if c >= 2 and streams[0] == 0:
            pl.semaphore_wait(self.credit, 1)
        for s in streams:
            lanes = slice(0, COUNTS[c][s] * LANES)
            index = (slice(None),) * 4 + (lanes,)
            self.send(
                self.stage[STAGE_OF[c]][s].at[index], self.landed[c % 2][s].at[index], self.sibling, (c, s, 0), ("swap", c)
            )

    def base(self, c, s, level, picks):
        lanes = slice(0, COUNTS[c][s] * LANES)
        if c == 0 and level:
            later = sorted(self.streams[s].order[1:])
            return self.parked[s], (*[picks.get(a, slice(None)) for a in later], slice(None), lanes)
        return self.work[WORK_OF[c]][s], (*[picks.get(a, slice(None)) for a in range(3)], slice(None), lanes)

    def terms(self, c, s, level, picks, extra=None, fresh=False, park=False):
        order = self.streams[s].order
        lanes = slice(0, COUNTS[c][s] * LANES)
        found = [self.base(c, s, 0 if park else level, picks)]
        if fresh:
            found.append((self.landed[c % 2][s], found[0][1]))
        steps = self.steps[c]
        for lower in range(1 if c == 0 and level and not park else 0, level + (extra is not None)):
            later = [picks.get(a, slice(None)) for a in sorted(order[lower + 1 :])]
            if lower == level:
                found.append((steps[2 * lower][s], (extra, *later, slice(None), lanes)))
            else:
                found.append((steps[2 * lower][s], (0, *later, slice(None), lanes)))
                found.append((steps[2 * lower + 1][s], (*later, slice(None), lanes)))
        return found

    def total(self, found):
        if len(found) == 2:
            return found[0][0][found[0][1]] + found[1][0][found[1][1]]
        values = [ref[index].astype(FULL) for ref, index in found]
        while len(values) > 1:
            values = [a + b for a, b in zip(values[::2], values[1::2])] + ([values[-1]] if len(values) % 2 else [])
        return values[0]

    def settle(self, c, s, level, picks, **kind):
        free = sorted(self.streams[s].order[level + 1 :])

        def write(inner):
            found = self.terms(c, s, level, inner, **kind)
            ref, index = self.base(c, s, level, inner)
            ref[index] = self.total(found).astype(LOW)

        if len(free) == 2:

            @pl.loop(0, 4)
            def _(i):
                write({**picks, free[0]: i})
        else:
            write(picks)

    def region(self, c, s, level, picks):
        ref, index = self.base(c, s, level, picks)
        return ref.at[index]

    def place_in(self, c, s, step, *first):
        lanes = slice(0, COUNTS[c][s] * LANES)
        later = len(LEVEL_SHAPES[step]) - len(first)
        return self.steps[c][step][s].at[(*first, *[slice(None)] * later, slice(None), lanes)]

    def halve_a(self, c, level, streams=range(STREAMS)):
        if level == 0 and c == 3 and streams[0] == 0:
            for i in range(6):
                pl.semaphore_wait(self.credits.at[i], 1)
        park = c == 0 and level == 1
        for s in streams:
            stream = self.streams[s]
            axis = stream.order[level]
            me = self.coords[axis]
            other = stream.first(me)
            done = {a: self.coords[a] for a in stream.order[:level]}
            if level == 0:
                if c == 0:
                    for own in self.owns.pop(s):
                        own.wait()
                self.arrive((c, s, 0))
            else:
                self.arrive((c, s, ("b", level - 1)))
            for slab, place in ((1, stream.mate(other)), (0, other)):
                picks = {**done, axis: place}
                self.settle(c, s, level, picks, fresh=level == 0, park=park)
                self.send(
                    self.region(c, s, level, picks), self.place_in(c, s, 2 * level, slab),
                    self.peer(axis, other), (c, s, ("a", level, slab)), (c, level),
                )
        if level == 0 or park:
            for s in streams:
                stream = self.streams[s]
                axis = stream.order[level]
                me = self.coords[axis]
                done = {a: self.coords[a] for a in stream.order[:level]}
                for place in (stream.mate(me), me):
                    self.settle(c, s, level, {**done, axis: place}, fresh=level == 0, park=park)
        if level == 0 and c < 3:
            pl.semaphore_signal(self.credit, inc=1, device_id=self.sibling, device_id_type=MESH)
        if park:
            for i, neighbour in enumerate(self.neighbours):
                pl.semaphore_signal(self.credits.at[i], inc=1, device_id=neighbour, device_id_type=MESH)

    def halve_b(self, c, level):
        for s, stream in enumerate(self.streams):
            axis = stream.order[level]
            other = stream.mate(self.coords[axis])
            picks = {**{a: self.coords[a] for a in stream.order[:level]}, axis: other}
            self.arrive((c, s, ("a", level, 1)))
            self.settle(c, s, level, picks, extra=1)
            self.send(
                self.region(c, s, level, picks), self.place_in(c, s, 2 * level + 1), self.peer(axis, other), (c, s, ("b", level)), (c, level)
            )
            self.arrive((c, s, ("a", level, 0)))

    def finish(self, c):
        first = FIRST_TILE[c]
        for s in range(STREAMS):
            self.arrive((c, s, ("b", 2)))
            value = self.total(self.terms(c, s, 3, dict(enumerate(self.coords))))
            for place in range(COUNTS[c][s]):
                self.final[self.section, first + place] = value[:, place * LANES : (place + 1) * LANES].astype(LOW)
            first += COUNTS[c][s]
        region = self.final.at[self.section, pl.ds(FIRST_TILE[c], sum(COUNTS[c]))]
        self.send(region, region, self.sibling, (c, "final"), "final")

    def put(self, buffers, c, tile, index, value):
        s, place = seat(c, tile)
        buffers[s][(*index, slice(None), slice(place * LANES, (place + 1) * LANES))] = value.astype(LOW)

    def put_columns(self, buffers, c, tile, value):
        for t in range(value.shape[1] // LANES):
            piece = value[:, t * LANES : (t + 1) * LANES].reshape(4, 4, 4, 16, LANES)
            self.put(buffers, c, tile + t, (slice(None),) * 3, piece)


UP_SLOTS, DOWN_SLOTS, KEPT_SLOTS = 3, 2, 2


def backward_kernel(
    g_embedded, arrived, gains, dec_vectors, w_qkv_h, w_out_h, w_up_h, w_down_h, w_embed_h,
    encoded_h, x1_h, m_h, slope_h, qT_h, kT_h, v_h, e_h, linv_h, oT_h, dec0, dec1, dec2, dec3,
    received_h, shares_h, *refs,
):
    refs = list(refs)
    take = lambda n: [refs.pop(0) for _ in range(n)]
    up_ring, down_ring, kept_ring = take(3)
    x1, qT, kT, v_ref, e_ref, linv, oT = take(7)
    gy, gz, ga_ref, aT, goT, gtT, mix = take(7)
    work = [take(STREAMS) for _ in range(3)]
    stage = [take(STREAMS) for _ in range(2)]
    landed = [take(STREAMS) for _ in range(2)]
    parked = take(STREAMS)
    large = [[take(STREAMS) for _ in range(2)] for _ in range(3)]
    steps = [large[WORK_OF[c]] + [take(STREAMS) for _ in range(4)] for c in range(4)]
    final, send_sem, recv_sem, own_sem, credit, credits, rows_credit, in_sem, ring_sem, out_sem = take(10)

    red = Reducer([dec0, dec1, dec2, dec3], work, parked, stage, landed, steps, final, send_sem, recv_sem, own_sem, credit, credits)
    section = red.section

    loads = {}

    def load(name, source, target, number):
        copy = pltpu.make_async_copy(source, target, in_sem.at[number])
        copy.start()
        loads[name] = copy

    def tile_of(i):
        return (1 - section) * 4 + i if i < 4 else section * 4 + i - 4

    def columns(j):
        return pl.ds(pl.multiple_of(j * 512, 512), 512)

    up_items = [lambda: w_embed_h]
    up_items += [functools.partial(lambda i: w_up_h.at[:, columns(tile_of(i))], i) for i in range(8)]
    up_items += [functools.partial(lambda i: w_out_h.at[:, pl.ds(i * 512, 512)], i) for i in range(2)]
    up_items += [functools.partial(lambda i: w_qkv_h.at[:, pl.ds(i * 512, 512)], i) for i in range(6)]
    rings = {
        "up": (up_ring, UP_SLOTS, up_items, 0),
        "down": (down_ring, DOWN_SLOTS, [functools.partial(lambda i: w_down_h.at[columns(tile_of(i)), :], i) for i in range(8)], 4),
        "kept": (
            kept_ring, KEPT_SLOTS,
            [functools.partial(lambda i: m_h.at[:, columns(i)], i) for i in range(8)]
            + [functools.partial(lambda i: slope_h.at[:, columns(tile_of(i))], i) for i in range(8)], 7,
        ),
    }
    flying = {name: [] for name in rings}
    issued = {name: 0 for name in rings}

    def fetch(name):
        ring, slots, items, base = rings[name]
        i = issued[name]
        if i < len(items):
            copy = pltpu.make_async_copy(items[i](), ring.at[i % slots], ring_sem.at[base + i % slots])
            copy.start()
            flying[name].append((copy, i % slots))
            issued[name] += 1

    def grab(name):
        copy, slot = flying[name].pop(0)
        copy.wait()
        return rings[name][0].at[slot]

    fetch("up")
    load("encoded", encoded_h, v_ref, 0)
    load("x1", x1_h, x1, 1)
    fetch("kept")
    red.meet()
    red.start_decoder()
    fetch("kept")
    for name in ("down", "up") * 2:
        fetch(name)
    for number, (name, source, target) in enumerate(
        (("oT", oT_h, oT), ("e", e_h, e_ref), ("linv", linv_h, linv), ("kT", kT_h, kT), ("qT", qT_h, qT))
    ):
        load(name, source, target, 2 + number)

    w_embed = grab("up")
    gy[...] = dot_nt(g_embedded[...], w_embed[...])
    gz[...] = gy[...].astype(LOW)
    fetch("up")
    loads["encoded"].wait()
    encodedT = v_ref[...].T
    for buffers, half in ((stage[0], 1 - section), (work[1], section)):
        red.put_columns(buffers, 1, 0, dot(encodedT, g_embedded[:, pl.ds(pl.multiple_of(half * 256, 256), 256)]))

    load("v", v_h, v_ref, 7)

    for i in range(8):
        mT = grab("kept")[...].T
        fetch("kept")
        for buffers, half in ((stage[0], 1 - section), (work[1], section)):
            value = dot(mT, gz[:, pl.ds(pl.multiple_of(half * 512, 512), 512)]).reshape(8, 4, 16, 512)
            for r in range(4):
                for t in range(4):
                    piece = value[:, r, :, t * LANES : (t + 1) * LANES].reshape(2, 4, 16, LANES)
                    red.put(buffers, 1, 2 + 4 * r + t, (i // 2, slice(2 * (i % 2), 2 * (i % 2) + 2), slice(None)), piece)
        if i == 5:
            red.halve_a(0, 0)
    red.swap(1)
    loads["x1"].wait()
    aT[...] = (norm_parts(x1[...])[0] * gains[2:3] + gains[3:4]).T.astype(LOW)

    for i in range(8):
        if i:
            for name in ("up", "down", "kept"):
                fetch(name)
        w_down, slope, w_up = grab("down"), grab("kept"), grab("up")
        gm = dot_nt(gz[...], w_down[...])
        gu = (gm * slope[...].astype(FULL)).astype(LOW)
        part = dot_nt(gu, w_up[...])
        ga_ref[...] = part if i == 0 else ga_ref[...] + part
        for t in range(2):
            red.put_columns(
                stage[1] if i < 4 else work[2], 2, 4 * (i % 4) + 2 * t, dot(aT[...], gu[:, 256 * t : 256 * t + 256])
            )
        if i == 1:
            red.halve_b(0, 0)
        if i == 3:
            red.swap(2)
            red.halve_a(0, 1)
            red.halve_a(1, 0)

    gv, mlp_gain, mlp_shift = norm_back(ga_ref[...], x1[...], gains[2:3])
    gx1 = gy[...] + gv
    gy[...] = gx1
    gz[...] = gx1.astype(LOW)
    fetch("up")
    loads["oT"].wait()
    w_out = [grab("up"), grab("up")]
    for k in range(2):
        rows = slice(512 * k, 512 * k + 512)
        goT[rows, :] = (dot_nt(w_out[0][rows, :], gz[:, 0:512]) + dot_nt(w_out[1][rows, :], gz[:, 512:1024])).astype(LOW)
    fetch("up")
    fetch("up")
    x = arrived[...].astype(FULL)
    aT[...] = (norm_parts(x)[0] * gains[0:1] + gains[1:2]).T.astype(LOW)
    for name in ("e", "linv", "v", "kT", "qT"):
        loads[name].wait()
    mix[...] = jnp.zeros_like(mix)

    def between(g):
        if g == 0:
            red.halve_b(1, 0)
        if g == 2:
            red.halve_a(2, 0)
            for axis in range(3):
                for step in (1, 2, 3):
                    pl.semaphore_signal(
                        rows_credit.at[3 * axis + 3 - step], inc=1, device_id=red.ahead(axis, step), device_id_type=MESH
                    )
        if g == 4:
            red.halve_b(0, 1)
        if g == 6:
            red.halve_a(1, 1)

    attention_backward(ER, HEADS, EH, v_ref, qT, kT, goT, oT, e_ref, linv, mix, gtT, between)

    def out_part(buffers, half):
        for t in range(2):
            cols = pl.ds(pl.multiple_of(half * 512, 512) + 256 * t, 256)
            red.put_columns(buffers, 3, 2 * t, dot(oT[...], gz[:, cols]))

    def qkv_part(buffers, half):
        for k in range(6):
            rows = pl.ds(pl.multiple_of(half * 1536, 256) + 256 * k, 256)
            red.put_columns(buffers, 3, 4 + 2 * k, dot_nt(aT[...], gtT[rows, :]))

    red.sent(("swap", 1))
    out_part(stage[0], 1 - section)
    qkv_part(stage[0], 1 - section)
    red.swap(3, range(5))
    red.sent((0, 0))
    out_part(work[0], section)
    qkv_part(work[0], section)
    red.halve_b(2, 0)
    red.halve_a(3, 0, range(5))

    for k in range(6):
        w_qkv = grab("up")
        part = dot_nt(gtT[512 * k : 512 * k + 512, :].T, w_qkv[...])
        ga_ref[...] = part if k == 0 else ga_ref[...] + part
        fetch("up")
    gv, attn_gain, attn_shift = norm_back(ga_ref[...], arrived[...].astype(FULL), gains[0:1])
    for g in range(8):
        lanes = slice(g * LANES, (g + 1) * LANES)
        narrow = slice(g // 2 * LANES, (g // 2 + 1) * LANES)
        rows = [vector[:, lanes] for vector in (attn_gain, attn_shift, mlp_gain, mlp_shift)]
        rows += [dec_vectors[0:5, narrow], jnp.zeros((7, LANES), FULL)]
        value = jnp.broadcast_to(jnp.concatenate(rows, axis=0)[None, None], (2, 4, 16, LANES))
        index = (g // 2, slice(2 * (g % 2), 2 * (g % 2) + 2), slice(None))
        for buffers in (stage[0], work[0]):
            red.put(buffers, 3, 16, index, value)
    red.swap(3, range(5, 6))
    ga_ref[...] = gy[...] + gv
    bags = landed[0]

    def bag(half):
        rows = ga_ref[pl.ds(pl.multiple_of(half * 128, 128), 128), :]
        return rows.reshape(128, 8, LANES).reshape(4, 4, 4, 16, LANES).astype(LOW)

    everything = (slice(None),) * 4
    mine = pl.ds(pl.multiple_of(section * LANES, LANES), LANES)
    bags[4][:, :, :, :, 0:LANES] = bag(1 - section)
    pl.semaphore_wait(credit, 1)
    red.send(bags[4].at[(*everything, slice(0, LANES))], bags[0].at[(*everything, mine)], red.sibling, ("rows", -1), "rows")
    bags[0][:, :, :, :, mine] = bag(section)

    def pass_rows(n):
        red.arrive(("rows", n - 1))
        for half in range(2):
            axis = (n + half) % 3
            me = red.coords[axis]

            def at(place):
                index = [slice(None)] * 3
                index[axis] = place
                return (*index, slice(None), slice(half * LANES, (half + 1) * LANES))

            for step in (1, 2, 3):
                place = lax.rem(me + step, 4)
                red.send(bags[n].at[at(place)], bags[n + 1].at[at(me)], red.peer(axis, place), ("rows", n), "rows")
            bags[n + 1][at(me)] = bags[n][at(me)]
    red.halve_b(1, 1)
    red.halve_a(0, 2)
    red.halve_a(2, 1)
    red.halve_a(3, 0, range(5, 6))
    for i in range(9):
        pl.semaphore_wait(rows_credit.at[i], 1)
    pass_rows(0)
    red.halve_a(1, 2)
    red.halve_b(0, 2)
    red.halve_b(3, 0)
    pass_rows(1)
    red.halve_b(2, 1)
    red.halve_b(1, 2)
    red.finish(0)
    red.halve_a(3, 1)
    red.halve_a(2, 2)
    pass_rows(2)
    red.finish(1)
    red.halve_b(3, 1)
    red.halve_b(2, 2)
    red.halve_a(3, 2)
    red.finish(2)
    red.arrive(("rows", 2))
    give = pltpu.make_async_copy(bags[3].at[(*everything, slice(0, 2 * LANES))], received_h, in_sem.at[0])
    give.start()
    red.halve_b(3, 2)
    red.finish(3)
    for c in range(4):
        red.arrive((c, "final"))
    out = pltpu.make_async_copy(final, shares_h, out_sem)
    out.start()
    for chunk in list(red.unsent):
        red.sent(chunk)
    out.wait()
    give.wait()


def backward_call(g_embedded, arrived, gains, dec_vectors, weights, kept, dec_grads):
    encoded, _, x1, m, slope, qT, kT, v, e, linv, oT = kept
    dec = [a.reshape(4, 4, 4, rows, columns) for a, (rows, columns) in zip(dec_grads, DEC_SOURCES)]
    vmem = pltpu.VMEM
    scratch = [
        vmem((UP_SLOTS, ED, 512), LOW), vmem((DOWN_SLOTS, 512, ED), LOW), vmem((KEPT_SLOTS, ER, 512), LOW),
        vmem((ER, ED), FULL), vmem((ED, ER), LOW), vmem((ED, ER), LOW), vmem((ER, ED), LOW),
        vmem((HEADS, ER, ER), LOW), vmem((HEADS, ER), FULL), vmem((ED, ER), LOW),
        vmem((ER, ED), FULL), vmem((ER, ED), LOW), vmem((ER, ED), FULL), vmem((ED, ER), LOW), vmem((ED, ER), LOW),
        vmem((3 * ED, ER), LOW), vmem((256, ER), LOW),
    ]
    for tiles in WORK_TILES + (SLOT_TILES[1], SLOT_TILES[0]) + SLOT_TILES:
        scratch += [vmem((4, 4, 4, 16, n * LANES), LOW) for n in tiles]
    scratch += [vmem((4, 4, 16, n * LANES), LOW) for n in COUNTS[0]]
    for tiles in STEP_TILES:
        for shape in LEVEL_SHAPES[:2]:
            scratch += [vmem((*shape, 16, n * LANES), LOW) for n in tiles]
    for tiles in COUNTS:
        for shape in LEVEL_SHAPES[2:]:
            scratch += [vmem((*shape, 16, n * LANES), LOW) for n in tiles]
    copies = len(dec_pieces()) + 3 * STREAMS + 4 * 9 * STREAMS + 5 + 18
    dma = pltpu.SemaphoreType.DMA
    scratch += [
        vmem((2, TILES, 16, LANES), LOW), dma((copies,)), dma((copies,)), dma((len(dec_pieces()),)),
        pltpu.SemaphoreType.REGULAR, pltpu.SemaphoreType.REGULAR((6,)), pltpu.SemaphoreType.REGULAR((9,)), dma((8,)), dma((9,)), dma,
    ]
    return pl.pallas_call(
        backward_kernel,
        out_shape=[jax.ShapeDtypeStruct((4, 4, 4, 16, 2 * LANES), LOW), jax.ShapeDtypeStruct((2, TILES, 16, LANES), LOW)],
        in_specs=[VMEM] * 4 + [ANY] * 19,
        out_specs=[ANY, ANY],
        scratch_shapes=scratch,
        compiler_params=pltpu.CompilerParams(collective_id=0, has_side_effects=True, vmem_limit_bytes=64 * 1024 * 1024 - 65536),
        name="encoder_backward_reduce",
    )(g_embedded, arrived, gains, dec_vectors, *weights, encoded, x1, m, slope, qT, kT, v, e, linv, oT, *dec)


SHARES = (
    ((8, 1536), 0, 0), ((8, 512), 0, 3), ((8, 2048), 0, 4), ((32, 512), 0, 8),
    ((16, 512), 1, 0), ((16, 4096), 2, 0), ((64, 1024), 1, 2), ((16, 1024), 3, 0), ((16, 3072), 3, 4),
)


def unpack_kernel(shares, bags, rows, *outs):
    for half in range(2):
        value = bags[:, :, half * LANES : (half + 1) * LANES].astype(FULL)
        rows[half * 128 : (half + 1) * 128, :] = value.reshape(128, 8, LANES).reshape(128, ED)
    for out, (shape, c, tile) in zip(outs, SHARES):
        number = FIRST_TILE[c] + tile
        rows, columns = shape
        packed = columns // 2 if rows == 8 else columns
        for r in range(max(rows // 16, 1)):
            for t in range(packed // (2 * LANES)):
                for half in range(2):
                    value = shares[half, number].astype(FULL)
                    lane = half * packed // 2 + t * LANES
                    if rows == 8:
                        out[:, lane : lane + LANES] = value[:8]
                        out[:, packed + lane : packed + lane + LANES] = value[8:]
                    else:
                        out[16 * r : 16 * r + 16, lane : lane + LANES] = value
                number += 1
    vectors = outs[len(SHARES) :]
    batch = lax.axis_index("batch")
    value = shares[0, VECTOR_TILE].astype(FULL)
    wide = pltpu.roll(value, lax.rem(128 - 16 * lax.rem(batch, 8), 128), axis=1)
    narrow = pltpu.roll(value, lax.rem(128 - 8 * lax.rem(batch, 16), 128), axis=1)
    for i in range(9):
        many = 16 if i < 4 else 8
        vectors[i][...] = (wide if i < 4 else narrow)[i, :many]


def unpack_call(shares, bags):
    shapes = [jax.ShapeDtypeStruct((ER, ED), FULL)]
    shapes += [jax.ShapeDtypeStruct(shape, FULL) for shape, _, _ in SHARES]
    shapes += [jax.ShapeDtypeStruct((16 if i < 4 else 8,), FULL) for i in range(9)]
    return pl.pallas_call(
        unpack_kernel,
        out_shape=shapes,
        in_specs=[VMEM] * 2,
        out_specs=[VMEM] * len(shapes),
        name="unpack_shares",
    )(shares, bags)


def tag_table(lengths, visible, gsd_index):
    row = jnp.arange(ROWS, dtype=jnp.int32)
    ends = jnp.cumsum(lengths)
    segment = jnp.sum((row[:, None] >= ends[None]).astype(jnp.int32), axis=1)
    onehot = (segment[:, None] == jnp.arange(lengths.shape[0])[None]).astype(jnp.int32)
    offset = row - jnp.sum(onehot * (ends - lengths)[None], axis=1)
    length = jnp.sum(onehot * lengths[None], axis=1)
    factor = jnp.sum(onehot * gsd_index[None], axis=1)
    side = jnp.where(length == 64, 8, jnp.where(length == 196, 14, 28))
    live = segment < lengths.shape[0]
    row_tag = jnp.where(live, factor * 28 + offset // side, -1)
    column_tag = jnp.where(live, factor * 28 + offset % side, -1)
    rank = jnp.cumsum(visible) - 1
    source = jnp.where(visible == 1, rank % 128 * 2 + rank // 128, -1)
    return jnp.stack([source, row_tag, column_tag, segment], axis=1).astype(jnp.int32)


def per_device(
    patches, lengths, visible, gsd_index,
    enc_attn_gain, enc_attn_shift, enc_qkv, enc_out, enc_mlp_gain, enc_mlp_shift, enc_up, enc_down,
    dec_embed, mask_token,
    dec_attn_gain, dec_attn_shift, dec_qkv, dec_out, dec_mlp_gain, dec_mlp_shift, dec_up, dec_down,
    out_grad,
):
    both = ("section", "batch")
    arrived = lax.all_to_all(patches, both, split_axis=0, concat_axis=0, tiled=True)
    tags = tag_table(lengths[0], visible, gsd_index[0])
    enc_gains = jnp.stack([enc_attn_gain, enc_attn_shift, enc_mlp_gain, enc_mlp_shift])
    dec_gains = jnp.stack([dec_attn_gain, dec_attn_shift, dec_mlp_gain, dec_mlp_shift])
    weights = (enc_qkv, enc_out, enc_up, enc_down, dec_embed)
    kept = encoder_forward_call(arrived, tags, enc_gains, *weights)
    high, low = wave_tables()
    decoder = decoder_call(
        kept[1], tags, high, low, mask_token[None], dec_gains, dec_qkv, dec_out, dec_up, dec_down, out_grad
    )
    dec_output, g_embedded, *d_dec, dec_vectors = decoder
    received, shares = backward_call(g_embedded, arrived, enc_gains, dec_vectors, weights, kept, d_dec)
    unpacked = unpack_call(shares, received.reshape(64, 16, 2 * LANES))
    patch_grad, d_qkv, d_out, d_up, d_down, embed, up, down, out, qkv, *vectors = unpacked
    gain1, shift1, gain2, shift2, dec_gain1, dec_shift1, dec_gain2, dec_shift2, mask = vectors
    return (
        dec_output, patch_grad, gain1, shift1, qkv, out, gain2, shift2, up, down, embed, mask,
        dec_gain1, dec_shift1, d_qkv, d_out, dec_gain2, dec_shift2, d_up, d_down,
    )


def solution(mesh):
    return jax.shard_map(
        per_device,
        mesh=mesh,
        in_specs=(
            P(("section", "batch"), None),
            P(("section", "batch"), None),
            P(("section", "batch")),
            P(("section", "batch"), None),
            P(),
            P(),
            P(),
            P(),
            P(),
            P(),
            P(),
            P(),
            P(),
            P(),
            P(),
            P(),
            P(),
            P(),
            P(),
            P(),
            P(),
            P(),
            P(("section", "batch"), None),
        ),
        out_specs=(
            P(("section", "batch"), None),
            P(("section", "batch"), None),
            P("batch"),
            P("batch"),
            P("batch", None),
            P("batch", None),
            P("batch"),
            P("batch"),
            P("batch", None),
            P("batch", None),
            P("batch", None),
            P("batch"),
            P("batch"),
            P("batch"),
            P("batch", None),
            P("batch", None),
            P("batch"),
            P("batch"),
            P("batch", None),
            P("batch", None),
        ),
        check_vma=False,
    )
```

```python
import functools
import math

import jax
import jax.numpy as jnp
import numpy as np
from jax import lax
from jax.experimental import pallas as pl
from jax.experimental.pallas import tpu as pltpu
from jax.sharding import PartitionSpec as P

LOW = jnp.bfloat16
FULL = jnp.float32
LN2 = math.log(2.0)
FAR = -1e30


def dot(a, b):
    return jnp.dot(a, b, preferred_element_type=FULL)


def dot_nt(a, b):
    return lax.dot_general(a, b, (((1,), (1,)), ((), ())), preferred_element_type=FULL)


def norm_parts(v):
    centred = v - jnp.mean(v, axis=-1, keepdims=True)
    r = lax.rsqrt(jnp.mean(centred * centred, axis=-1, keepdims=True) + 1e-6)
    return centred * r, r


def norm_back(gn, v, gain):
    vh, r = norm_parts(v)
    gg = gn * gain
    gv = r * (gg - jnp.mean(gg, axis=-1, keepdims=True) - vh * jnp.mean(gg * vh, axis=-1, keepdims=True))
    return gv, jnp.sum(gn * vh, axis=0, keepdims=True), jnp.sum(gn, axis=0, keepdims=True)


def gelu_parts(u):
    z = jnp.abs(u) * (0.3275911 / math.sqrt(2.0))
    t = 1.0 / (1.0 + z)
    poly = 1.061405429
    for c in (-1.453152027, 1.421413741, -0.284496736, 0.254829592):
        poly = poly * t + c
    bell = jnp.exp2(u * u * (-0.5 / LN2))
    tail = (0.5 * t) * poly * bell
    phi = jnp.where(u >= 0, 1.0 - tail, tail)
    return u * phi, phi + u * (bell * (1.0 / math.sqrt(2.0 * math.pi)))


def paired(a, b):
    w = a.shape[1]
    return jnp.concatenate([a.reshape(64, 8, w), b.reshape(64, 8, w)], axis=1).astype(LOW)


def blocks_of(total, size):
    cuts = list(range(0, total - size + 1, size))
    return [(c, (size if i + 1 < len(cuts) else total - c)) for i, c in enumerate(cuts)]


def attention_forward(rows, heads, hs, k_ref, ones_ref, far_ref, qT, vT, mix, e_ref, oT, linv):
    group = 128 // hs
    mix[...] = jnp.zeros_like(mix)
    mix[128:256, :] = far_ref[...]
    for g in range(heads // group):
        lanes = slice(128 * g, 128 * g + 128)
        left = jnp.concatenate([k_ref[:, lanes], ones_ref[...]], axis=1)
        for i in range(group):
            h = g * group + i
            feat = slice(h * hs, h * hs + hs)
            if i:
                mix[(i - 1) * hs : i * hs, :] = jnp.zeros((hs, rows), LOW)
            else:
                mix[128 - hs : 128, :] = jnp.zeros((hs, rows), LOW)
            mix[i * hs : i * hs + hs, :] = qT[feat, :]
            head_forward(rows, h, feat, left, vT, mix, e_ref, oT, linv)


def head_forward(rows, h, feat, left, vT, mix, e_ref, oT, linv):
    for first, many in blocks_of(rows, 256):
        cols = slice(first, first + many)
        s = dot(left, mix[:, cols])
        peak = jnp.max(s, axis=0, keepdims=True)
        e_ref[h, :, cols] = jnp.exp2(s - peak).astype(LOW)
    lhs = jnp.concatenate([vT[feat, :], jnp.ones((16, rows), LOW)], axis=0)
    o = dot(lhs, e_ref[h])
    hs = feat.stop - feat.start
    inverse = 1.0 / o[hs : hs + 1]
    linv[h : h + 1, :] = inverse
    oT[feat, :] = (o[:hs] * inverse).astype(LOW)


def attention_backward(rows, heads, hs, v_ref, qT, kT, goT, oT, e_ref, linv, mix, gtT, between=None):
    group = 128 // hs
    width = heads * hs
    scale = hs**-0.5
    for g in range(heads // group):
        lanes = slice(128 * g, 128 * g + 128)
        for i in range(group):
            h = g * group + i
            feat = slice(h * hs, h * hs + hs)
            go = goT[feat, :].astype(FULL) * linv[h : h + 1, :]
            low = go.astype(LOW)
            centre = jnp.sum(go * oT[feat, :].astype(FULL), axis=0, keepdims=True)
            if i:
                mix[(i - 1) * hs : i * hs, :] = jnp.zeros((hs, rows), LOW)
            else:
                mix[128 - hs : 128, :] = jnp.zeros((hs, rows), LOW)
            mix[i * hs : i * hs + hs, :] = low
            gtT[2 * width + h * hs : 2 * width + h * hs + hs, :] = dot_nt(low, e_ref[h]).astype(LOW)
            for first, many in blocks_of(rows, 256):
                cols = slice(first, first + many)
                gp = dot(v_ref[:, lanes], mix[0:128, cols])
                e_ref[h, :, cols] = (e_ref[h, :, cols].astype(FULL) * (gp - centre[:, cols])).astype(LOW)
            gs = e_ref[h]
            gtT[feat, :] = (dot(kT[feat, :], gs) * scale).astype(LOW)
            gtT[width + h * hs : width + h * hs + hs, :] = (dot_nt(qT[feat, :], gs) * LN2).astype(LOW)
        if between is not None:
            between(g)


ROWS, DD, DFF, HEADS = 784, 512, 2048, 16
STEP = 112


def decoder_kernel(
    embedded, tags, sines_high, sines_low, mask_token, gains, w_qkv, w_out_h, w_up_h, w_down_h, out_grad,
    dec_out_h, g_embedded, d_qkv, d_out_h, d_up_h, d_down_h, vectors,
    w_out, w_up, w_down, dec_out, d_out, d_up, d_down, in_sem, out_sem,
    x_ref, low_a, low_aT, k_ref, v_ref, qT, kT, vT, e_ref, oT, linv, x1_ref, gz, ga_ref, y_ref, goT, gtT, mix, ones_ref, far_ref, sums,
):
    loads, stores = [], []
    for i, (source, target) in enumerate(((w_out_h, w_out), (w_up_h, w_up), (w_down_h, w_down))):
        loads.append(pltpu.make_async_copy(source, target, in_sem.at[i]))
        loads[-1].start()

    def keep(source, target):
        stores.append(pltpu.make_async_copy(source, target, out_sem.at[len(stores)]))
        stores[-1].start()

    sums[...] = jnp.zeros_like(sums)
    tile = 256

    def each(body):
        @pl.loop(0, ROWS // STEP)
        def _(i):
            body(pl.ds(pl.multiple_of(i * STEP, STEP), STEP))

    wide = embedded[...]
    emb_high = wide.astype(LOW)
    emb_low = (wide - emb_high.astype(FULL)).astype(LOW)
    mask = mask_token[...].astype(FULL)

    def inputs(rows):
        tag = tags[rows, :]
        source, row_tag, column_tag, segment = (tag[:, i : i + 1] for i in range(4))
        lane = lax.broadcasted_iota(jnp.int32, (STEP, 256), 1)
        small = lax.broadcasted_iota(jnp.int32, (STEP, 128), 1)
        pick = (lane == source).astype(LOW)
        x = dot(pick, emb_high) + dot(pick, emb_low)
        x = jnp.where(source < 0, mask, x)
        row_pick = (small == row_tag).astype(LOW)
        column_pick = (small == column_tag).astype(LOW)
        row_wave = dot(row_pick, sines_high[...]) + dot(row_pick, sines_low[...])
        column_wave = dot(column_pick, sines_high[...]) + dot(column_pick, sines_low[...])
        x = x + jnp.concatenate([row_wave, column_wave], axis=1)
        x_ref[rows, :] = x
        low_a[rows, :] = (norm_parts(x)[0] * gains[0:1] + gains[1:2]).astype(LOW)
        same = small == segment
        ones_ref[rows, :] = same.astype(LOW)
        y_ref[rows, 0:128] = jnp.where(same | (small > 12), 0.0, FAR)
        live = (segment < 12).astype(FULL)
        gz[rows, :] = (out_grad[rows, :].astype(FULL) * live).astype(LOW)

    each(inputs)
    far_ref[...] = y_ref[:, 0:128].T.astype(LOW)
    low_aT[...] = low_a[...].T

    for j in range(2):
        t = dot(low_a[...], w_qkv[:, j * tile : (j + 1) * tile]) * (32**-0.5 / LN2)
        qT[j * tile : (j + 1) * tile, :] = t.astype(LOW).T
        t = dot(low_a[...], w_qkv[:, DD + j * tile : DD + (j + 1) * tile]).astype(LOW)
        k_ref[:, j * tile : (j + 1) * tile] = t
        kT[j * tile : (j + 1) * tile, :] = t.T
        t = dot(low_a[...], w_qkv[:, 2 * DD + j * tile : 2 * DD + (j + 1) * tile]).astype(LOW)
        v_ref[:, j * tile : (j + 1) * tile] = t
        vT[j * tile : (j + 1) * tile, :] = t.T

    attention_forward(ROWS, HEADS, 32, k_ref, ones_ref, far_ref, qT, vT, mix, e_ref, oT, linv)

    for copy in loads:
        copy.wait()
    low_a[...] = oT[...].T
    for j in range(2):
        cols = slice(j * tile, (j + 1) * tile)
        x1_ref[:, cols] = x_ref[:, cols] + dot(low_a[...], w_out[:, cols])

    def second(rows):
        x1 = x1_ref[rows, :]
        low_a[rows, :] = (norm_parts(x1)[0] * gains[2:3] + gains[3:4]).astype(LOW)
        y_ref[rows, :] = x1
        ga_ref[rows, :] = jnp.zeros((STEP, DD), FULL)

    each(second)
    a2T = goT
    del a2T
    a2_t = low_a[...].T

    kT_keep = None
    del kT_keep
    gtT[0:DD, :] = a2_t

    @pl.loop(0, DFF // (2 * tile))
    def _(j):
        halves = []
        for half in range(2):
            cols = pl.ds(pl.multiple_of(j * tile + half * (DFF // 2), tile), tile)
            u = dot(low_a[...], w_up[:, cols])
            m, slope = gelu_parts(u)
            m = m.astype(LOW)
            y_ref[...] += dot(m, w_down[cols, :])
            gm = dot_nt(gz[...], w_down[cols, :])
            gu = (gm * slope).astype(LOW)
            ga_ref[...] += dot_nt(gu, w_up[:, cols])
            d_down[cols, :] = dot(m.T, gz[...]).astype(LOW)
            halves.append(dot(gtT[0:DD, :], gu))
        d_up[:, :, pl.ds(pl.multiple_of(j * tile, tile), tile)] = paired(*halves)

    keep(d_up, d_up_h)
    keep(d_down, d_down_h)

    def third(rows):
        live = (tags[rows, 3:4] < 12).astype(FULL)
        dec_out[rows, :] = (y_ref[rows, :] * live).astype(LOW)
        gv, dgain, dshift = norm_back(ga_ref[rows, :], x1_ref[rows, :], gains[2:3])
        gx1 = out_grad[rows, :].astype(FULL) * live + gv
        x1_ref[rows, :] = gx1
        low_a[rows, :] = gx1.astype(LOW)
        sums[2:3, :] += dgain
        sums[3:4, :] += dshift

    each(third)
    keep(dec_out, dec_out_h)
    for j in range(2):
        goT[j * tile : (j + 1) * tile, :] = dot_nt(w_out[j * tile : (j + 1) * tile, :], low_a[...])
    for j in range(2):
        half = dot(oT[...], low_a[:, j * tile : (j + 1) * tile])
        if j == 0:
            first_half = half
        else:
            d_out[...] = paired(first_half, half)
    keep(d_out, d_out_h)

    attention_backward(ROWS, HEADS, 32, v_ref, qT, kT, goT, oT, e_ref, linv, mix, gtT)

    for j in range(3):
        lo = dot_nt(low_aT[...], gtT[j * tile : (j + 1) * tile, :])
        hi = dot_nt(low_aT[...], gtT[768 + j * tile : 768 + (j + 1) * tile, :])
        d_qkv[:, :, j * tile : (j + 1) * tile] = paired(lo, hi)
    for j in range(2):
        cols = slice(j * tile, (j + 1) * tile)
        y_ref[:, cols] = dot(w_qkv[cols, :], gtT[...]).T

    def fourth(rows):
        gv, dgain, dshift = norm_back(y_ref[rows, :], x_ref[rows, :], gains[0:1])
        gx = x1_ref[rows, :] + gv
        sums[0:1, :] += dgain
        sums[1:2, :] += dshift
        source = tags[rows, 0:1]
        sums[4:5, :] += jnp.sum(jnp.where(source < 0, gx, 0.0), axis=0, keepdims=True)
        low_a[rows, :] = gx.astype(LOW)
        lane = lax.broadcasted_iota(jnp.int32, (STEP, 256), 1)
        y_ref[rows, 0:256] = (lane == source).astype(FULL)

    each(fourth)
    pick = y_ref[:, 0:256].astype(LOW).T
    g_embedded[...] = dot(pick, low_a[...]).astype(LOW)
    vectors[...] = sums[...]
    for copy in stores:
        copy.wait()


def decoder_call(embedded, tags, sines_high, sines_low, mask_token, gains, w_qkv, w_out, w_up, w_down, out_grad):
    vmem = pl.BlockSpec(memory_space=pltpu.VMEM)
    hbm = pl.BlockSpec(memory_space=pl.ANY)
    low = lambda *shape: pltpu.VMEM(shape, LOW)
    full = lambda *shape: pltpu.VMEM(shape, FULL)
    return pl.pallas_call(
        decoder_kernel,
        out_shape=[
            jax.ShapeDtypeStruct((ROWS, DD), LOW),
            jax.ShapeDtypeStruct((256, DD), LOW),
            jax.ShapeDtypeStruct((64, 16, 768), LOW),
            jax.ShapeDtypeStruct((64, 16, 256), LOW),
            jax.ShapeDtypeStruct((64, 16, 1024), LOW),
            jax.ShapeDtypeStruct((DFF, DD), LOW),
            jax.ShapeDtypeStruct((8, DD), FULL),
        ],
        in_specs=[vmem] * 7 + [hbm] * 3 + [vmem],
        out_specs=[hbm, vmem, vmem, hbm, hbm, hbm, vmem],
        scratch_shapes=[
            low(DD, DD), low(DD, DFF), low(DFF, DD),
            low(ROWS, DD), low(64, 16, 256), low(64, 16, 1024), low(DFF, DD),
            pltpu.SemaphoreType.DMA((3,)), pltpu.SemaphoreType.DMA((4,)),
            full(ROWS, DD), low(ROWS, DD), low(DD, ROWS), low(ROWS, DD), low(ROWS, DD),
            low(DD, ROWS), low(DD, ROWS), low(DD, ROWS), low(HEADS, ROWS, ROWS), low(DD, ROWS),
            full(HEADS, ROWS), full(ROWS, DD), low(ROWS, DD), full(ROWS, DD), full(ROWS, DD),
            full(DD, ROWS), low(3 * DD, ROWS), low(256, ROWS), low(ROWS, 128), low(128, ROWS), full(8, DD),
        ],
        compiler_params=pltpu.CompilerParams(vmem_limit_bytes=63 * 1024 * 1024),
        name="decoder",
    )(embedded, tags, sines_high, sines_low, mask_token, gains, w_qkv, w_out, w_up, w_down, out_grad)


def wave_tables():
    quarter = DD // 4
    frequency = np.exp(np.arange(quarter, dtype=np.float32) * np.float32(-math.log(10000.0) / quarter)).astype(np.float32)
    places = np.zeros((128, 1), np.float32)
    for f, factor in enumerate((0.5, 1.0, 2.0, 4.0)):
        places[f * 28 : f * 28 + 28, 0] = np.arange(28, dtype=np.float32) * factor
    angle = (places * frequency[None, :]).astype(np.float32).astype(np.float64)
    waves = np.concatenate([np.sin(angle), np.cos(angle)], axis=1)
    waves[112:] = 0.0
    high = jnp.asarray(waves, FULL).astype(LOW)
    low = (jnp.asarray(waves, FULL) - high.astype(FULL)).astype(LOW)
    return high, low


ER, ED, EF = 256, 1024, 4096
EH = 64


def encoder_forward_kernel(
    arrived, tags, gains, w_qkv_h, w_out_h, w_up_h, w_down_h, w_embed_h,
    encoded_h, embedded_h, x1_h, m_h, slope_h, qT_h, kT_h, v_h, e_h, linv_h, oT_h,
    w_qkv, w_out, w_up, w_down, w_embed,
    encoded, embedded, x1, m_ref, slope_ref, qT, kT, v_ref, e_ref, linv, oT,
    x_ref, low_a, k_ref, vT, mix, ones_ref, far_ref, y_ref, in_sem, out_sem, tile_sem,
):
    loads = []
    for i, (source, target) in enumerate(
        ((w_qkv_h, w_qkv), (w_out_h, w_out), (w_up_h, w_up), (w_down_h, w_down), (w_embed_h, w_embed))
    ):
        copy = pltpu.make_async_copy(source, target, in_sem.at[i])
        copy.start()
        loads.append(copy)
    stores = []
    seats = iter(range(len(KEPT)))

    def keep(source, target):
        copy = pltpu.make_async_copy(source, target, out_sem.at[next(seats)])
        copy.start()
        stores.append(copy)

    tag = tags[...]
    lane = lax.broadcasted_iota(jnp.int32, (ROWS, 256), 1)
    small = lax.broadcasted_iota(jnp.int32, (ROWS, 128), 1)
    pick = (lane == tag[:, 0:1]).astype(FULL).T.astype(LOW)
    items = dot(pick, (small == tag[:, 3:4]).astype(LOW))
    slot = lax.broadcasted_iota(jnp.int32, (ER, 128), 1)
    empty = jnp.sum(items, axis=1, keepdims=True) < 0.5
    items = jnp.where((slot == 13) & empty, 1.0, items)
    ones_ref[...] = items.astype(LOW)
    far_ref[...] = jnp.where((items > 0.5) | (slot > 13), 0.0, FAR).T.astype(LOW)

    x = arrived[...].astype(FULL)
    x_ref[...] = x
    low_a[...] = (norm_parts(x)[0] * gains[0:1] + gains[1:2]).astype(LOW)
    loads[0].wait()

    tile = 256

    @pl.loop(0, ED // tile)
    def _(j):
        cols = pl.ds(pl.multiple_of(j * tile, tile), tile)
        t = dot(low_a[...], w_qkv[:, cols]) * (EH**-0.5 / LN2)
        qT[cols, :] = t.T.astype(LOW)
        t = dot(low_a[...], w_qkv[:, pl.ds(pl.multiple_of(ED + j * tile, tile), tile)])
        k_ref[:, cols] = t.astype(LOW)
        kT[cols, :] = t.T.astype(LOW)
        t = dot(low_a[...], w_qkv[:, pl.ds(pl.multiple_of(2 * ED + j * tile, tile), tile)])
        v_ref[:, cols] = t.astype(LOW)
        vT[cols, :] = t.T.astype(LOW)

    keep(qT, qT_h)
    keep(kT, kT_h)
    keep(v_ref, v_h)
    attention_forward(ER, HEADS, EH, k_ref, ones_ref, far_ref, qT, vT, mix, e_ref, oT, linv)
    keep(e_ref, e_h)
    keep(linv, linv_h)
    keep(oT, oT_h)
    low_a[...] = oT[...].T
    loads[1].wait()

    @pl.loop(0, ED // tile)
    def _(j):
        cols = pl.ds(pl.multiple_of(j * tile, tile), tile)
        x1[:, cols] = x_ref[:, cols] + dot(low_a[...], w_out[:, cols])

    keep(x1, x1_h)
    branch = x1[...]
    low_a[...] = (norm_parts(branch)[0] * gains[2:3] + gains[3:4]).astype(LOW)
    y_ref[...] = branch
    loads[2].wait()
    loads[3].wait()

    @pl.loop(0, EF // 512)
    def _(j):
        cols = pl.ds(pl.multiple_of(j * 512, 512), 512)
        m, slope = gelu_parts(dot(low_a[...], w_up[:, cols]))
        m = m.astype(LOW)
        m_ref[:, cols] = m
        slope_ref[:, cols] = slope.astype(LOW)
        pltpu.make_async_copy(m_ref.at[:, cols], m_h.at[:, cols], tile_sem.at[0, j]).start()
        pltpu.make_async_copy(slope_ref.at[:, cols], slope_h.at[:, cols], tile_sem.at[1, j]).start()
        y_ref[...] += dot(m, w_down[cols, :])

    for j in range(EF // 512):
        cols = pl.ds(j * 512, 512)
        stores.append(pltpu.make_async_copy(m_ref.at[:, cols], m_h.at[:, cols], tile_sem.at[0, j]))
        stores.append(pltpu.make_async_copy(slope_ref.at[:, cols], slope_h.at[:, cols], tile_sem.at[1, j]))
    encoded[...] = y_ref[...].astype(LOW)
    keep(encoded, encoded_h)
    loads[4].wait()
    embedded[...] = dot(encoded[...], w_embed[...])
    keep(embedded, embedded_h)
    for copy in stores:
        copy.wait()


ANY = pl.BlockSpec(memory_space=pl.ANY)
VMEM = pl.BlockSpec(memory_space=pltpu.VMEM)
WEIGHTS = [((ED, 3 * ED), LOW), ((ED, ED), LOW), ((ED, EF), LOW), ((EF, ED), LOW), ((ED, DD), LOW)]
KEPT = [
    ((ER, ED), LOW), ((ER, DD), FULL), ((ER, ED), FULL), ((ER, EF), LOW), ((ER, EF), LOW),
    ((ED, ER), LOW), ((ED, ER), LOW), ((ER, ED), LOW), ((HEADS, ER, ER), LOW), ((HEADS, ER), FULL), ((ED, ER), LOW),
]


def encoder_forward_call(arrived, tags, gains, w_qkv, w_out, w_up, w_down, w_embed):
    scratch = [pltpu.VMEM(*s) for s in WEIGHTS + KEPT]
    scratch += [
        pltpu.VMEM((ER, ED), FULL), pltpu.VMEM((ER, ED), LOW), pltpu.VMEM((ER, ED), LOW), pltpu.VMEM((ED, ER), LOW),
        pltpu.VMEM((256, ER), LOW), pltpu.VMEM((ER, 128), LOW), pltpu.VMEM((128, ER), LOW), pltpu.VMEM((ER, ED), FULL),
        pltpu.SemaphoreType.DMA((5,)), pltpu.SemaphoreType.DMA((len(KEPT),)), pltpu.SemaphoreType.DMA((2, EF // 512)),
    ]
    return pl.pallas_call(
        encoder_forward_kernel,
        out_shape=[jax.ShapeDtypeStruct(*s) for s in KEPT],
        in_specs=[VMEM] * 3 + [ANY] * 5,
        out_specs=[ANY] * len(KEPT),
        scratch_shapes=scratch,
        compiler_params=pltpu.CompilerParams(vmem_limit_bytes=60 * 1024 * 1024),
        name="encoder_forward",
    )(arrived, tags, gains, w_qkv, w_out, w_up, w_down, w_embed)


MESH = pl.DeviceIdType.MESH
LANES = 128
STREAMS = 6
COUNTS = ((2, 2, 2, 2, 2, 2), (3, 3, 3, 3, 3, 3), (3, 3, 3, 3, 2, 2), (3, 3, 3, 3, 3, 2))
DEC_SOURCES = ((16, 768), (16, 256), (16, 1024), (32, 512))
WORK_OF = (0, 1, 2, 0)
STAGE_OF = (None, 0, 1, 0)
WORK_TILES = ((3, 3, 3, 3, 3, 2), (3, 3, 3, 3, 3, 3), (3, 3, 3, 3, 2, 2))
SLOT_TILES = ((3, 3, 3, 3, 2, 2), (3, 3, 3, 3, 3, 3))
STEP_TILES = WORK_TILES
LEVEL_SHAPES = ((2, 4, 4), (4, 4), (2, 4), (4,), (2,), ())
FIRST_TILE = (0, 12, 30, 46)
TILES = 63
VECTOR_TILE = 62


def seat(c, tile):
    for s, many in enumerate(COUNTS[c]):
        if tile < many:
            return s, tile
        tile -= many


def dec_pieces():
    found, tile = [], 0
    for source, (rows, columns) in enumerate(DEC_SOURCES):
        for r in range(rows // 16):
            for column in range(columns // (2 * LANES)):
                s, place = seat(0, tile)
                last = found[-1] if found else None
                if last and last[:3] == [s, source, r] and last[3] + last[4] == column:
                    last[4] += 1
                else:
                    found.append([s, source, r, column, 1, place])
                tile += 1
    return found


class Stream:
    def __init__(self, number):
        self.order = tuple((number + step) % 3 for step in range(3))
        self.swap = number >= 3

    def flip(self, p):
        return p + 1 - 2 * lax.rem(p, 2)

    def first(self, p):
        return 3 - p if self.swap else self.flip(p)

    def mate(self, p):
        return self.flip(p) if self.swap else 3 - p


class Reducer:
    def __init__(self, dec_sources, work, parked, stage, landed, steps, final, send_sem, recv_sem, own_sem, credit, credits):
        self.dec_sources, self.work, self.parked, self.stage = dec_sources, work, parked, stage
        self.landed, self.steps, self.final = landed, steps, final
        self.send_sem, self.recv_sem, self.own_sem = send_sem, recv_sem, own_sem
        self.credit, self.credits = credit, credits
        self.section = lax.axis_index("section")
        self.batch = lax.axis_index("batch")
        batch = self.batch
        self.coords = (batch // 16, lax.rem(batch // 4, 4), lax.rem(batch, 4))
        self.sibling = (1 - self.section, batch)
        self.streams = [Stream(number) for number in range(STREAMS)]
        self.neighbours = []
        for axis in range(3):
            p = self.coords[axis]
            self.neighbours += [self.peer(axis, p + 1 - 2 * lax.rem(p, 2)), self.peer(axis, 3 - p)]
        self.count = 0
        self.arrivals, self.unsent, self.owns = {}, {}, {}

    def peer(self, axis, place):
        return (self.section, self.batch + (place - self.coords[axis]) * (16, 4, 1)[axis])

    def ahead(self, axis, step):
        return self.peer(axis, lax.rem(self.coords[axis] + step, 4))

    def meet(self):
        barrier = pltpu.get_barrier_semaphore()
        partners = [self.sibling] + [self.ahead(axis, step) for axis in range(3) for step in (1, 2, 3)]
        for partner in partners:
            pl.semaphore_signal(barrier, inc=1, device_id=partner, device_id_type=MESH)
        pl.semaphore_wait(barrier, len(partners))

    def send(self, source, target, device, key, chunk):
        number = self.count
        self.count += 1
        copy = pltpu.make_async_remote_copy(
            src_ref=source, dst_ref=target, send_sem=self.send_sem.at[number], recv_sem=self.recv_sem.at[number],
            device_id=device, device_id_type=MESH,
        )
        copy.start()
        self.unsent.setdefault(chunk, []).append(copy)
        self.arrivals.setdefault(key, []).append(copy)

    def arrive(self, key):
        for copy in self.arrivals.pop(key):
            copy.wait_recv()

    def sent(self, chunk):
        for copy in self.unsent.pop(chunk, []):
            copy.wait_send()

    def start_decoder(self):
        for number, (s, source, r, column, width, place) in enumerate(dec_pieces()):
            half = DEC_SOURCES[source][1] // 2
            rows = pl.ds(16 * r, 16)
            there = pl.ds(pl.multiple_of((1 - self.section) * half, LANES) + column * LANES, width * LANES)
            here = pl.ds(pl.multiple_of(self.section * half, LANES) + column * LANES, width * LANES)
            lanes = pl.ds(place * LANES, width * LANES)
            everything = (slice(None),) * 4
            self.send(
                self.dec_sources[source].at[:, :, :, rows, there],
                self.landed[0][s].at[(*everything, lanes)],
                self.sibling, (0, s, 0), ("swap", 0),
            )
            own = pltpu.make_async_copy(
                self.dec_sources[source].at[:, :, :, rows, here],
                self.work[0][s].at[(*everything, lanes)],
                self.own_sem.at[number],
            )
            own.start()
            self.owns.setdefault(s, []).append(own)

    def swap(self, c, streams=range(STREAMS)):
        if c >= 2 and streams[0] == 0:
            pl.semaphore_wait(self.credit, 1)
        for s in streams:
            lanes = slice(0, COUNTS[c][s] * LANES)
            index = (slice(None),) * 4 + (lanes,)
            self.send(
                self.stage[STAGE_OF[c]][s].at[index], self.landed[c % 2][s].at[index], self.sibling, (c, s, 0), ("swap", c)
            )

    def base(self, c, s, level, picks):
        lanes = slice(0, COUNTS[c][s] * LANES)
        if c == 0 and level:
            later = sorted(self.streams[s].order[1:])
            return self.parked[s], (*[picks.get(a, slice(None)) for a in later], slice(None), lanes)
        return self.work[WORK_OF[c]][s], (*[picks.get(a, slice(None)) for a in range(3)], slice(None), lanes)

    def terms(self, c, s, level, picks, extra=None, fresh=False, park=False):
        order = self.streams[s].order
        lanes = slice(0, COUNTS[c][s] * LANES)
        found = [self.base(c, s, 0 if park else level, picks)]
        if fresh:
            found.append((self.landed[c % 2][s], found[0][1]))
        steps = self.steps[c]
        for lower in range(1 if c == 0 and level and not park else 0, level + (extra is not None)):
            later = [picks.get(a, slice(None)) for a in sorted(order[lower + 1 :])]
            if lower == level:
                found.append((steps[2 * lower][s], (extra, *later, slice(None), lanes)))
            else:
                found.append((steps[2 * lower][s], (0, *later, slice(None), lanes)))
                found.append((steps[2 * lower + 1][s], (*later, slice(None), lanes)))
        return found

    def total(self, found):
        if len(found) == 2:
            return found[0][0][found[0][1]] + found[1][0][found[1][1]]
        values = [ref[index].astype(FULL) for ref, index in found]
        while len(values) > 1:
            values = [a + b for a, b in zip(values[::2], values[1::2])] + ([values[-1]] if len(values) % 2 else [])
        return values[0]

    def settle(self, c, s, level, picks, **kind):
        free = sorted(self.streams[s].order[level + 1 :])

        def write(inner):
            found = self.terms(c, s, level, inner, **kind)
            ref, index = self.base(c, s, level, inner)
            ref[index] = self.total(found).astype(LOW)

        if len(free) == 2:

            @pl.loop(0, 4)
            def _(i):
                write({**picks, free[0]: i})
        else:
            write(picks)

    def region(self, c, s, level, picks):
        ref, index = self.base(c, s, level, picks)
        return ref.at[index]

    def place_in(self, c, s, step, *first):
        lanes = slice(0, COUNTS[c][s] * LANES)
        later = len(LEVEL_SHAPES[step]) - len(first)
        return self.steps[c][step][s].at[(*first, *[slice(None)] * later, slice(None), lanes)]

    def halve_a(self, c, level, streams=range(STREAMS)):
        if level == 0 and c == 3 and streams[0] == 0:
            for i in range(6):
                pl.semaphore_wait(self.credits.at[i], 1)
        park = c == 0 and level == 1
        for s in streams:
            stream = self.streams[s]
            axis = stream.order[level]
            me = self.coords[axis]
            other = stream.first(me)
            done = {a: self.coords[a] for a in stream.order[:level]}
            if level == 0:
                if c == 0:
                    for own in self.owns.pop(s):
                        own.wait()
                self.arrive((c, s, 0))
            else:
                self.arrive((c, s, ("b", level - 1)))
            for slab, place in ((1, stream.mate(other)), (0, other)):
                picks = {**done, axis: place}
                self.settle(c, s, level, picks, fresh=level == 0, park=park)
                self.send(
                    self.region(c, s, level, picks), self.place_in(c, s, 2 * level, slab),
                    self.peer(axis, other), (c, s, ("a", level, slab)), (c, level),
                )
        if level == 0 or park:
            for s in streams:
                stream = self.streams[s]
                axis = stream.order[level]
                me = self.coords[axis]
                done = {a: self.coords[a] for a in stream.order[:level]}
                for place in (stream.mate(me), me):
                    self.settle(c, s, level, {**done, axis: place}, fresh=level == 0, park=park)
        if level == 0 and c < 3:
            pl.semaphore_signal(self.credit, inc=1, device_id=self.sibling, device_id_type=MESH)
        if park:
            for i, neighbour in enumerate(self.neighbours):
                pl.semaphore_signal(self.credits.at[i], inc=1, device_id=neighbour, device_id_type=MESH)

    def halve_b(self, c, level):
        for s, stream in enumerate(self.streams):
            axis = stream.order[level]
            other = stream.mate(self.coords[axis])
            picks = {**{a: self.coords[a] for a in stream.order[:level]}, axis: other}
            self.arrive((c, s, ("a", level, 1)))
            self.settle(c, s, level, picks, extra=1)
            self.send(
                self.region(c, s, level, picks), self.place_in(c, s, 2 * level + 1), self.peer(axis, other), (c, s, ("b", level)), (c, level)
            )
            self.arrive((c, s, ("a", level, 0)))

    def finish(self, c):
        first = FIRST_TILE[c]
        for s in range(STREAMS):
            self.arrive((c, s, ("b", 2)))
            value = self.total(self.terms(c, s, 3, dict(enumerate(self.coords))))
            for place in range(COUNTS[c][s]):
                self.final[self.section, first + place] = value[:, place * LANES : (place + 1) * LANES].astype(LOW)
            first += COUNTS[c][s]
        region = self.final.at[self.section, pl.ds(FIRST_TILE[c], sum(COUNTS[c]))]
        self.send(region, region, self.sibling, (c, "final"), "final")

    def put(self, buffers, c, tile, index, value):
        s, place = seat(c, tile)
        buffers[s][(*index, slice(None), slice(place * LANES, (place + 1) * LANES))] = value.astype(LOW)

    def put_columns(self, buffers, c, tile, value):
        for t in range(value.shape[1] // LANES):
            piece = value[:, t * LANES : (t + 1) * LANES].reshape(4, 4, 4, 16, LANES)
            self.put(buffers, c, tile + t, (slice(None),) * 3, piece)


UP_SLOTS, DOWN_SLOTS, KEPT_SLOTS = 3, 2, 2


def backward_kernel(
    g_embedded, arrived, gains, dec_vectors, w_qkv_h, w_out_h, w_up_h, w_down_h, w_embed_h,
    encoded_h, x1_h, m_h, slope_h, qT_h, kT_h, v_h, e_h, linv_h, oT_h, dec0, dec1, dec2, dec3,
    received_h, shares_h, *refs,
):
    refs = list(refs)
    take = lambda n: [refs.pop(0) for _ in range(n)]
    up_ring, down_ring, kept_ring = take(3)
    x1, qT, kT, v_ref, e_ref, linv, oT = take(7)
    gy, gz, ga_ref, aT, goT, gtT, mix = take(7)
    work = [take(STREAMS) for _ in range(3)]
    stage = [take(STREAMS) for _ in range(2)]
    landed = [take(STREAMS) for _ in range(2)]
    parked = take(STREAMS)
    large = [[take(STREAMS) for _ in range(2)] for _ in range(3)]
    steps = [large[WORK_OF[c]] + [take(STREAMS) for _ in range(4)] for c in range(4)]
    final, send_sem, recv_sem, own_sem, credit, credits, rows_credit, in_sem, ring_sem, out_sem = take(10)

    red = Reducer([dec0, dec1, dec2, dec3], work, parked, stage, landed, steps, final, send_sem, recv_sem, own_sem, credit, credits)
    section = red.section

    loads = {}

    def load(name, source, target, number):
        copy = pltpu.make_async_copy(source, target, in_sem.at[number])
        copy.start()
        loads[name] = copy

    def tile_of(i):
        return (1 - section) * 4 + i if i < 4 else section * 4 + i - 4

    def columns(j):
        return pl.ds(pl.multiple_of(j * 512, 512), 512)

    up_items = [lambda: w_embed_h]
    up_items += [functools.partial(lambda i: w_up_h.at[:, columns(tile_of(i))], i) for i in range(8)]
    up_items += [functools.partial(lambda i: w_out_h.at[:, pl.ds(i * 512, 512)], i) for i in range(2)]
    up_items += [functools.partial(lambda i: w_qkv_h.at[:, pl.ds(i * 512, 512)], i) for i in range(6)]
    rings = {
        "up": (up_ring, UP_SLOTS, up_items, 0),
        "down": (down_ring, DOWN_SLOTS, [functools.partial(lambda i: w_down_h.at[columns(tile_of(i)), :], i) for i in range(8)], 4),
        "kept": (
            kept_ring, KEPT_SLOTS,
            [functools.partial(lambda i: m_h.at[:, columns(i)], i) for i in range(8)]
            + [functools.partial(lambda i: slope_h.at[:, columns(tile_of(i))], i) for i in range(8)], 7,
        ),
    }
    flying = {name: [] for name in rings}
    issued = {name: 0 for name in rings}

    def fetch(name):
        ring, slots, items, base = rings[name]
        i = issued[name]
        if i < len(items):
            copy = pltpu.make_async_copy(items[i](), ring.at[i % slots], ring_sem.at[base + i % slots])
            copy.start()
            flying[name].append((copy, i % slots))
            issued[name] += 1

    def grab(name):
        copy, slot = flying[name].pop(0)
        copy.wait()
        return rings[name][0].at[slot]

    fetch("up")
    load("encoded", encoded_h, v_ref, 0)
    load("x1", x1_h, x1, 1)
    fetch("kept")
    red.meet()
    red.start_decoder()
    fetch("kept")
    for name in ("down", "up") * 2:
        fetch(name)
    for number, (name, source, target) in enumerate(
        (("oT", oT_h, oT), ("e", e_h, e_ref), ("linv", linv_h, linv), ("kT", kT_h, kT), ("qT", qT_h, qT))
    ):
        load(name, source, target, 2 + number)

    w_embed = grab("up")
    gy[...] = dot_nt(g_embedded[...], w_embed[...])
    gz[...] = gy[...].astype(LOW)
    fetch("up")
    loads["encoded"].wait()
    encodedT = v_ref[...].T
    for buffers, half in ((stage[0], 1 - section), (work[1], section)):
        red.put_columns(buffers, 1, 0, dot(encodedT, g_embedded[:, pl.ds(pl.multiple_of(half * 256, 256), 256)]))

    load("v", v_h, v_ref, 7)

    for i in range(8):
        mT = grab("kept")[...].T
        fetch("kept")
        for buffers, half in ((stage[0], 1 - section), (work[1], section)):
            value = dot(mT, gz[:, pl.ds(pl.multiple_of(half * 512, 512), 512)]).reshape(8, 4, 16, 512)
            for r in range(4):
                for t in range(4):
                    piece = value[:, r, :, t * LANES : (t + 1) * LANES].reshape(2, 4, 16, LANES)
                    red.put(buffers, 1, 2 + 4 * r + t, (i // 2, slice(2 * (i % 2), 2 * (i % 2) + 2), slice(None)), piece)
        if i == 5:
            red.halve_a(0, 0)
    red.swap(1)
    loads["x1"].wait()
    aT[...] = (norm_parts(x1[...])[0] * gains[2:3] + gains[3:4]).T.astype(LOW)

    for i in range(8):
        if i:
            for name in ("up", "down", "kept"):
                fetch(name)
        w_down, slope, w_up = grab("down"), grab("kept"), grab("up")
        gm = dot_nt(gz[...], w_down[...])
        gu = (gm * slope[...].astype(FULL)).astype(LOW)
        part = dot_nt(gu, w_up[...])
        ga_ref[...] = part if i == 0 else ga_ref[...] + part
        for t in range(2):
            red.put_columns(
                stage[1] if i < 4 else work[2], 2, 4 * (i % 4) + 2 * t, dot(aT[...], gu[:, 256 * t : 256 * t + 256])
            )
        if i == 1:
            red.halve_b(0, 0)
        if i == 3:
            red.swap(2)
            red.halve_a(0, 1)
            red.halve_a(1, 0)

    gv, mlp_gain, mlp_shift = norm_back(ga_ref[...], x1[...], gains[2:3])
    gx1 = gy[...] + gv
    gy[...] = gx1
    gz[...] = gx1.astype(LOW)
    fetch("up")
    loads["oT"].wait()
    w_out = [grab("up"), grab("up")]
    for k in range(2):
        rows = slice(512 * k, 512 * k + 512)
        goT[rows, :] = (dot_nt(w_out[0][rows, :], gz[:, 0:512]) + dot_nt(w_out[1][rows, :], gz[:, 512:1024])).astype(LOW)
    fetch("up")
    fetch("up")
    x = arrived[...].astype(FULL)
    aT[...] = (norm_parts(x)[0] * gains[0:1] + gains[1:2]).T.astype(LOW)
    for name in ("e", "linv", "v", "kT", "qT"):
        loads[name].wait()
    mix[...] = jnp.zeros_like(mix)

    def between(g):
        if g == 0:
            red.halve_b(1, 0)
        if g == 2:
            red.halve_a(2, 0)
            for axis in range(3):
                for step in (1, 2, 3):
                    pl.semaphore_signal(
                        rows_credit.at[3 * axis + 3 - step], inc=1, device_id=red.ahead(axis, step), device_id_type=MESH
                    )
        if g == 4:
            red.halve_b(0, 1)
        if g == 6:
            red.halve_a(1, 1)

    attention_backward(ER, HEADS, EH, v_ref, qT, kT, goT, oT, e_ref, linv, mix, gtT, between)

    def out_part(buffers, half):
        for t in range(2):
            cols = pl.ds(pl.multiple_of(half * 512, 512) + 256 * t, 256)
            red.put_columns(buffers, 3, 2 * t, dot(oT[...], gz[:, cols]))

    def qkv_part(buffers, half):
        for k in range(6):
            rows = pl.ds(pl.multiple_of(half * 1536, 256) + 256 * k, 256)
            red.put_columns(buffers, 3, 4 + 2 * k, dot_nt(aT[...], gtT[rows, :]))

    red.sent(("swap", 1))
    out_part(stage[0], 1 - section)
    qkv_part(stage[0], 1 - section)
    red.swap(3, range(5))
    red.sent((0, 0))
    out_part(work[0], section)
    qkv_part(work[0], section)
    red.halve_b(2, 0)
    red.halve_a(3, 0, range(5))

    for k in range(6):
        w_qkv = grab("up")
        part = dot_nt(gtT[512 * k : 512 * k + 512, :].T, w_qkv[...])
        ga_ref[...] = part if k == 0 else ga_ref[...] + part
        fetch("up")
    gv, attn_gain, attn_shift = norm_back(ga_ref[...], arrived[...].astype(FULL), gains[0:1])
    for g in range(8):
        lanes = slice(g * LANES, (g + 1) * LANES)
        narrow = slice(g // 2 * LANES, (g // 2 + 1) * LANES)
        rows = [vector[:, lanes] for vector in (attn_gain, attn_shift, mlp_gain, mlp_shift)]
        rows += [dec_vectors[0:5, narrow], jnp.zeros((7, LANES), FULL)]
        value = jnp.broadcast_to(jnp.concatenate(rows, axis=0)[None, None], (2, 4, 16, LANES))
        index = (g // 2, slice(2 * (g % 2), 2 * (g % 2) + 2), slice(None))
        for buffers in (stage[0], work[0]):
            red.put(buffers, 3, 16, index, value)
    red.swap(3, range(5, 6))
    ga_ref[...] = gy[...] + gv
    bags = landed[0]

    def bag(half):
        rows = ga_ref[pl.ds(pl.multiple_of(half * 128, 128), 128), :]
        return rows.reshape(128, 8, LANES).reshape(4, 4, 4, 16, LANES).astype(LOW)

    everything = (slice(None),) * 4
    mine = pl.ds(pl.multiple_of(section * LANES, LANES), LANES)
    bags[4][:, :, :, :, 0:LANES] = bag(1 - section)
    pl.semaphore_wait(credit, 1)
    red.send(bags[4].at[(*everything, slice(0, LANES))], bags[0].at[(*everything, mine)], red.sibling, ("rows", -1), "rows")
    bags[0][:, :, :, :, mine] = bag(section)

    def pass_rows(n):
        red.arrive(("rows", n - 1))
        for half in range(2):
            axis = (n + half) % 3
            me = red.coords[axis]

            def at(place):
                index = [slice(None)] * 3
                index[axis] = place
                return (*index, slice(None), slice(half * LANES, (half + 1) * LANES))

            for step in (1, 2, 3):
                place = lax.rem(me + step, 4)
                red.send(bags[n].at[at(place)], bags[n + 1].at[at(me)], red.peer(axis, place), ("rows", n), "rows")
            bags[n + 1][at(me)] = bags[n][at(me)]
    red.halve_b(1, 1)
    red.halve_a(0, 2)
    red.halve_a(2, 1)
    red.halve_a(3, 0, range(5, 6))
    for i in range(9):
        pl.semaphore_wait(rows_credit.at[i], 1)
    pass_rows(0)
    red.halve_b(3, 0)
    red.halve_a(1, 2)
    red.halve_b(0, 2)
    pass_rows(1)
    red.halve_a(3, 1)
    red.halve_b(2, 1)
    red.halve_b(1, 2)
    red.halve_b(3, 1)
    red.halve_a(2, 2)
    red.finish(0)
    pass_rows(2)
    red.halve_a(3, 2)
    red.halve_b(2, 2)
    red.finish(1)
    red.halve_b(3, 2)
    red.finish(2)
    red.arrive(("rows", 2))
    give = pltpu.make_async_copy(bags[3].at[(*everything, slice(0, 2 * LANES))], received_h, in_sem.at[0])
    give.start()
    red.finish(3)
    for c in range(4):
        red.arrive((c, "final"))
    out = pltpu.make_async_copy(final, shares_h, out_sem)
    out.start()
    for chunk in list(red.unsent):
        red.sent(chunk)
    out.wait()
    give.wait()


def backward_call(g_embedded, arrived, gains, dec_vectors, weights, kept, dec_grads):
    encoded, _, x1, m, slope, qT, kT, v, e, linv, oT = kept
    dec = [a.reshape(4, 4, 4, rows, columns) for a, (rows, columns) in zip(dec_grads, DEC_SOURCES)]
    vmem = pltpu.VMEM
    scratch = [
        vmem((UP_SLOTS, ED, 512), LOW), vmem((DOWN_SLOTS, 512, ED), LOW), vmem((KEPT_SLOTS, ER, 512), LOW),
        vmem((ER, ED), FULL), vmem((ED, ER), LOW), vmem((ED, ER), LOW), vmem((ER, ED), LOW),
        vmem((HEADS, ER, ER), LOW), vmem((HEADS, ER), FULL), vmem((ED, ER), LOW),
        vmem((ER, ED), FULL), vmem((ER, ED), LOW), vmem((ER, ED), FULL), vmem((ED, ER), LOW), vmem((ED, ER), LOW),
        vmem((3 * ED, ER), LOW), vmem((256, ER), LOW),
    ]
    for tiles in WORK_TILES + (SLOT_TILES[1], SLOT_TILES[0]) + SLOT_TILES:
        scratch += [vmem((4, 4, 4, 16, n * LANES), LOW) for n in tiles]
    scratch += [vmem((4, 4, 16, n * LANES), LOW) for n in COUNTS[0]]
    for tiles in STEP_TILES:
        for shape in LEVEL_SHAPES[:2]:
            scratch += [vmem((*shape, 16, n * LANES), LOW) for n in tiles]
    for tiles in COUNTS:
        for shape in LEVEL_SHAPES[2:]:
            scratch += [vmem((*shape, 16, n * LANES), LOW) for n in tiles]
    copies = len(dec_pieces()) + 3 * STREAMS + 4 * 9 * STREAMS + 5 + 18
    dma = pltpu.SemaphoreType.DMA
    scratch += [
        vmem((2, TILES, 16, LANES), LOW), dma((copies,)), dma((copies,)), dma((len(dec_pieces()),)),
        pltpu.SemaphoreType.REGULAR, pltpu.SemaphoreType.REGULAR((6,)), pltpu.SemaphoreType.REGULAR((9,)), dma((8,)), dma((9,)), dma,
    ]
    return pl.pallas_call(
        backward_kernel,
        out_shape=[jax.ShapeDtypeStruct((4, 4, 4, 16, 2 * LANES), LOW), jax.ShapeDtypeStruct((2, TILES, 16, LANES), LOW)],
        in_specs=[VMEM] * 4 + [ANY] * 19,
        out_specs=[ANY, ANY],
        scratch_shapes=scratch,
        compiler_params=pltpu.CompilerParams(collective_id=0, has_side_effects=True, vmem_limit_bytes=64 * 1024 * 1024 - 65536),
        name="encoder_backward_reduce",
    )(g_embedded, arrived, gains, dec_vectors, *weights, encoded, x1, m, slope, qT, kT, v, e, linv, oT, *dec)


SHARES = (
    ((8, 1536), 0, 0), ((8, 512), 0, 3), ((8, 2048), 0, 4), ((32, 512), 0, 8),
    ((16, 512), 1, 0), ((16, 4096), 2, 0), ((64, 1024), 1, 2), ((16, 1024), 3, 0), ((16, 3072), 3, 4),
)


def unpack_kernel(shares, bags, rows, *outs):
    for half in range(2):
        value = bags[:, :, half * LANES : (half + 1) * LANES].astype(FULL)
        rows[half * 128 : (half + 1) * 128, :] = value.reshape(128, 8, LANES).reshape(128, ED)
    for out, (shape, c, tile) in zip(outs, SHARES):
        number = FIRST_TILE[c] + tile
        rows, columns = shape
        packed = columns // 2 if rows == 8 else columns
        for r in range(max(rows // 16, 1)):
            for t in range(packed // (2 * LANES)):
                for half in range(2):
                    value = shares[half, number].astype(FULL)
                    lane = half * packed // 2 + t * LANES
                    if rows == 8:
                        out[:, lane : lane + LANES] = value[:8]
                        out[:, packed + lane : packed + lane + LANES] = value[8:]
                    else:
                        out[16 * r : 16 * r + 16, lane : lane + LANES] = value
                number += 1
    vectors = outs[len(SHARES) :]
    batch = lax.axis_index("batch")
    value = shares[0, VECTOR_TILE].astype(FULL)
    wide = pltpu.roll(value, lax.rem(128 - 16 * lax.rem(batch, 8), 128), axis=1)
    narrow = pltpu.roll(value, lax.rem(128 - 8 * lax.rem(batch, 16), 128), axis=1)
    for i in range(9):
        many = 16 if i < 4 else 8
        vectors[i][...] = (wide if i < 4 else narrow)[i, :many]


def unpack_call(shares, bags):
    shapes = [jax.ShapeDtypeStruct((ER, ED), FULL)]
    shapes += [jax.ShapeDtypeStruct(shape, FULL) for shape, _, _ in SHARES]
    shapes += [jax.ShapeDtypeStruct((16 if i < 4 else 8,), FULL) for i in range(9)]
    return pl.pallas_call(
        unpack_kernel,
        out_shape=shapes,
        in_specs=[VMEM] * 2,
        out_specs=[VMEM] * len(shapes),
        name="unpack_shares",
    )(shares, bags)


def tag_table(lengths, visible, gsd_index):
    row = jnp.arange(ROWS, dtype=jnp.int32)
    ends = jnp.cumsum(lengths)
    segment = jnp.sum((row[:, None] >= ends[None]).astype(jnp.int32), axis=1)
    onehot = (segment[:, None] == jnp.arange(lengths.shape[0])[None]).astype(jnp.int32)
    offset = row - jnp.sum(onehot * (ends - lengths)[None], axis=1)
    length = jnp.sum(onehot * lengths[None], axis=1)
    factor = jnp.sum(onehot * gsd_index[None], axis=1)
    side = jnp.where(length == 64, 8, jnp.where(length == 196, 14, 28))
    live = segment < lengths.shape[0]
    row_tag = jnp.where(live, factor * 28 + offset // side, -1)
    column_tag = jnp.where(live, factor * 28 + offset % side, -1)
    rank = jnp.cumsum(visible) - 1
    source = jnp.where(visible == 1, rank % 128 * 2 + rank // 128, -1)
    return jnp.stack([source, row_tag, column_tag, segment], axis=1).astype(jnp.int32)


def per_device(
    patches, lengths, visible, gsd_index,
    enc_attn_gain, enc_attn_shift, enc_qkv, enc_out, enc_mlp_gain, enc_mlp_shift, enc_up, enc_down,
    dec_embed, mask_token,
    dec_attn_gain, dec_attn_shift, dec_qkv, dec_out, dec_mlp_gain, dec_mlp_shift, dec_up, dec_down,
    out_grad,
):
    both = ("section", "batch")
    arrived = lax.all_to_all(patches, both, split_axis=0, concat_axis=0, tiled=True)
    tags = tag_table(lengths[0], visible, gsd_index[0])
    enc_gains = jnp.stack([enc_attn_gain, enc_attn_shift, enc_mlp_gain, enc_mlp_shift])
    dec_gains = jnp.stack([dec_attn_gain, dec_attn_shift, dec_mlp_gain, dec_mlp_shift])
    weights = (enc_qkv, enc_out, enc_up, enc_down, dec_embed)
    kept = encoder_forward_call(arrived, tags, enc_gains, *weights)
    high, low = wave_tables()
    decoder = decoder_call(
        kept[1], tags, high, low, mask_token[None], dec_gains, dec_qkv, dec_out, dec_up, dec_down, out_grad
    )
    dec_output, g_embedded, *d_dec, dec_vectors = decoder
    received, shares = backward_call(g_embedded, arrived, enc_gains, dec_vectors, weights, kept, d_dec)
    unpacked = unpack_call(shares, received.reshape(64, 16, 2 * LANES))
    patch_grad, d_qkv, d_out, d_up, d_down, embed, up, down, out, qkv, *vectors = unpacked
    gain1, shift1, gain2, shift2, dec_gain1, dec_shift1, dec_gain2, dec_shift2, mask = vectors
    return (
        dec_output, patch_grad, gain1, shift1, qkv, out, gain2, shift2, up, down, embed, mask,
        dec_gain1, dec_shift1, d_qkv, d_out, dec_gain2, dec_shift2, d_up, d_down,
    )


def solution(mesh):
    return jax.shard_map(
        per_device,
        mesh=mesh,
        in_specs=(
            P(("section", "batch"), None),
            P(("section", "batch"), None),
            P(("section", "batch")),
            P(("section", "batch"), None),
            P(),
            P(),
            P(),
            P(),
            P(),
            P(),
            P(),
            P(),
            P(),
            P(),
            P(),
            P(),
            P(),
            P(),
            P(),
            P(),
            P(),
            P(),
            P(("section", "batch"), None),
        ),
        out_specs=(
            P(("section", "batch"), None),
            P(("section", "batch"), None),
            P("batch"),
            P("batch"),
            P("batch", None),
            P("batch", None),
            P("batch"),
            P("batch"),
            P("batch", None),
            P("batch", None),
            P("batch", None),
            P("batch"),
            P("batch"),
            P("batch"),
            P("batch", None),
            P("batch", None),
            P("batch"),
            P("batch"),
            P("batch", None),
            P("batch", None),
        ),
        check_vma=False,
    )
```
